128 devices in a mesh: dp: 4 (over x), dict: 32 (over y, z, core).
Axes of the slice: x: 4, y: 4, z: 4, core: 2. Of those that a mesh axis runs over, the one named last changes fastest.
Arguments:
- resid: bfloat16 [32768, 4096], P(('dp', 'dict')), may hold values from -6 to 6
- block_ids: int32 [32768, 2], P(('dp', 'dict')), may hold values from 0 to 127, all different within a row; in each aligned block of 256 rows (0 to 255, 256 to 511, ...) at most 8 rows name the same one
- enc_w: bfloat16 [8192, 4096], P('dict'), may hold values from -0.09375 to 0.09375
- enc_b: float32 [8192], P('dict'), may hold values from -3 to 3
- dec_w: bfloat16 [8192, 4096], P('dict'), may hold values from -0.5 to 0.5
- dec_b: float32 [4096], replicated, may hold values from -3 to 3
Outputs:
- recon: bfloat16 [32768, 4096], P(('dp', 'dict'))
- enc_grad: float32 [8192, 4096], P('dict', 'dp')
- dec_grad: float32 [8192, 4096], P('dict', 'dp')
The draws below stay inside these ranges and needn't reach their ends.
Inputs may be any that keep to these rules, and one draw needn't show every extreme that they name: `block_ids`: each row names 2 different blocks. Within the rows of one device no block is named by more than 8 rows, and some block is named by exactly 8 of them.
All inputs are finite; a program needn't handle non-finite values.
Results may differ from the reference program's by a relative error of at most 0.012.
Values may be sent and summed in bfloat16 or wider, within the bound.
No kernel may reach another device: no remote copies, remote signals or barrier semaphores. Data moves between devices by JAX's collectives and lax.ppermute only.
A program may use at most 128 MiB of HBM per device.

```python
import math
import jax
import jax.numpy as jnp
import numpy as np
from jax import lax

D = 4096
LAT = 64
ACT = 2
TOK_DEV = 256
NBLK = 128
LATENTS = 8192
TOKENS = 32768
CAP = 8


def block_levels(rng, extent, shards, least, largest):
    level, own = 1.0, jax.random.fold_in(rng, 6)
    for axis_at, blocks in shards:
        draws = jnp.exp(jax.random.uniform(jax.random.fold_in(own, axis_at), (blocks,), jnp.float32, least / len(shards), largest / len(shards)))
        level = level * jnp.repeat(draws, extent[axis_at] // blocks).reshape([-1 if axis == axis_at else 1 for axis in range(len(extent))])
    return level


def routed_block(own_key, own, number, rows, count, top, limit, skew):
    order = jax.random.permutation(own_key, count)
    packed, usual = load_shares(count, rows * top, limit, skew, True), load_shares(count, rows * top, limit, skew, False)
    places = jnp.arange(count)

    def named(sizes, turn):
        used = int((sizes > 0).sum())
        fixed = max(1, used // 4)
        shifted = fixed + (places - fixed + turn * (used - fixed)) % max(1, count - fixed)
        return jnp.zeros((count,), jnp.int32).at[order[jnp.where(places < fixed, places, shifted)]].set(jnp.asarray(sizes, jnp.int32))

    sizes = jnp.where(number % 4 == 0, named(packed, number // 4), named(usual, number - number // 4 - 1))
    mixed = jax.random.permutation(jax.random.fold_in(own, 3), count)
    source_of, receiver = mixed[0:count // 2 * 2:2], mixed[1:count // 2 * 2:2]
    room = jnp.minimum(sizes[source_of] - 1, limit - sizes[receiver]) // 2
    room = jnp.where((source_of == order[0]) | (receiver == order[0]) | (sizes[receiver] == 0), 0, jnp.maximum(room, 0))
    shifted = jax.random.randint(jax.random.fold_in(own, 4), (count // 2,), 0, 1 << 20) % (room + 1)
    sizes = sizes.at[source_of].add(-shifted).at[receiver].add(shifted)
    members = jnp.searchsorted(jnp.cumsum(sizes), jnp.arange(rows * top), side="right").astype(jnp.int32)
    table = members.reshape(top, rows).T
    table = table[jax.random.permutation(jax.random.fold_in(own, 1), rows)]
    turn = jax.random.randint(jax.random.fold_in(own, 2), (rows, 1), 0, top)
    return jnp.take_along_axis(table, (jnp.arange(top)[None, :] + turn) % top, axis=1)


def load_shares(amount, total, reach, slope, full):
    portions = [(1 << 20) // math.isqrt(standing ** slope) + 1 for standing in range(1, amount + 1)]
    largest = reach if full else min(reach, max(-(-total // amount), total * portions[0] // sum(portions)))
    least = 1 if total - largest >= amount - 1 else 0
    given, spare = [largest] + [least] * (amount - 1), total - largest - least * (amount - 1)
    while spare > 0:
        movable = [i for i in range(1, amount) if given[i] < largest] or [i for i in range(1, amount) if given[i] < reach]
        mass, remaining = sum([portions[i] for i in movable]), spare
        for i in movable:
            more = min(reach - given[i], max(1, remaining * portions[i] // mass), spare)
            given[i] = given[i] + more
            spare = spare - more
    return np.array(given)


def gaussian(rng, extent, width, bound, split=(), kind=jnp.bfloat16):
    gain = block_levels(rng, extent, split, -0.22, 0.18) if split else 1.0
    entries = jax.random.normal(rng, extent, jnp.float32) * width * gain
    return jnp.minimum(jnp.maximum(entries, -bound), bound).astype(kind)


def setup_inputs(seed: int = 0) -> dict:
    streams_of = jax.random.split(jax.random.key(seed), 7)
    resid = gaussian(streams_of[0], (TOKENS, D), 1.0, 6.0, ((0, 128),))
    block_ids_keys = jax.random.split(jax.random.fold_in(streams_of[1], 1), TOKENS // TOK_DEV)
    block_ids_turns = jax.random.permutation(jax.random.fold_in(streams_of[1], 3), TOKENS // TOK_DEV)
    block_ids = jax.vmap(lambda own, number: routed_block(jax.random.fold_in(streams_of[1], 2), own, number, TOK_DEV, NBLK, ACT, CAP, 2))(block_ids_keys, block_ids_turns).reshape((TOKENS, ACT))
    enc_w = gaussian(streams_of[2], (LATENTS, D), D ** -0.5, 0.09375, ((0, 32),))
    enc_b = gaussian(streams_of[3], (LATENTS,), 0.5, 3.0, ((0, 32),), jnp.float32)
    dec_w = gaussian(streams_of[4], (LATENTS, D), (LAT * ACT) ** -0.5, 0.5, ((0, 32),))
    dec_b = gaussian(streams_of[5], (D,), 0.5, 3.0, (), jnp.float32)
    return dict(resid=resid, block_ids=block_ids, enc_w=enc_w, enc_b=enc_b, dec_w=dec_w, dec_b=dec_b)


def reference(resid, block_ids, enc_w, enc_b, dec_w, dec_b):
    groups = TOKENS // TOK_DEV
    pairs = TOK_DEV * ACT
    centered = (resid.astype(jnp.float32) - dec_b).astype(jnp.bfloat16)
    flat = block_ids.reshape(groups, pairs)
    onehot = (flat[:, :, None] == jnp.arange(NBLK, dtype=jnp.int32)[None, None, :]).astype(jnp.int32)
    rank = jnp.sum(jnp.cumsum(onehot, axis=1) * onehot, axis=2) - 1
    slot = (jnp.arange(groups, dtype=jnp.int32)[:, None] * NBLK + flat) * CAP + rank
    source_row = (jnp.arange(TOKENS * ACT, dtype=jnp.int32) // ACT).astype(jnp.int32)
    table = jnp.full((groups * NBLK * CAP,), TOKENS, jnp.int32).at[slot.reshape(-1)].set(source_row)
    table = table.reshape(groups, NBLK, CAP).transpose(1, 0, 2).reshape(NBLK, groups * CAP)
    padded = jnp.concatenate([centered, jnp.zeros((1, D), jnp.bfloat16)], axis=0)
    enc_blocks = enc_w.reshape(NBLK, LAT, D)
    dec_blocks = dec_w.reshape(NBLK, LAT, D)
    bias_blocks = enc_b.reshape(NBLK, LAT)

    def forward(total, inputs):
        index, encoder, bias, decoder = inputs
        rows = padded[index]
        pre = jnp.dot(rows, encoder.T, preferred_element_type=jnp.float32) + bias
        acts = jnp.maximum(pre, 0.0).astype(jnp.bfloat16)
        part = jnp.dot(acts, decoder, preferred_element_type=jnp.float32).astype(jnp.bfloat16)
        return total.at[index].add(part.astype(jnp.float32)), None

    total, unused = lax.scan(forward, jnp.zeros((TOKENS + 1, D), jnp.float32),
                             (table, enc_blocks, bias_blocks, dec_blocks))
    recon = (dec_b + total[:TOKENS]).astype(jnp.bfloat16)
    error = recon.astype(jnp.float32) - dec_b - centered.astype(jnp.float32)
    scale = (NBLK / (TOKENS * ACT)) ** 0.5
    gpad = jnp.concatenate([error * scale, jnp.zeros((1, D), jnp.float32)], axis=0)
    high = lax.Precision.HIGHEST

    def backward(carry, inputs):
        index, encoder, bias, decoder = inputs
        rows = padded[index]
        pre = jnp.dot(rows, encoder.T, preferred_element_type=jnp.float32) + bias
        acts = jnp.maximum(pre, 0.0).astype(jnp.bfloat16)
        grads = gpad[index]
        dec_part = jnp.dot(acts.astype(jnp.float32).T, grads, precision=high)
        gate = (pre > 0).astype(jnp.float32)
        gpre = jnp.dot(grads, decoder.astype(jnp.float32).T, precision=high) * gate
        enc_part = jnp.dot(gpre.T, rows.astype(jnp.float32), precision=high)
        return carry, (enc_part, dec_part)

    unused, (enc_grad, dec_grad) = lax.scan(backward, jnp.zeros((), jnp.float32),
                                            (table, enc_blocks, bias_blocks, dec_blocks))
    return recon, enc_grad.reshape(LATENTS, D), dec_grad.reshape(LATENTS, D)
```

```python
import jax
import jax.numpy as jnp
from jax import lax
from jax.experimental import pallas as pl
from jax.experimental.pallas import tpu as pltpu
from jax.sharding import PartitionSpec as P

LAT = 64
CAP = 8
BF = jnp.bfloat16
F32 = jnp.float32
VMEM_LIMIT = 56 * 1024 * 1024


def params(**more):
    return pltpu.CompilerParams(vmem_limit_bytes=VMEM_LIMIT, **more)


def dot(a, b):
    return jnp.dot(a, b, preferred_element_type=F32)


def dot_tn(a, b):
    return lax.dot_general(a, b, (((0,), (0,)), ((), ())), preferred_element_type=F32)


def dot_nt(a, b):
    return lax.dot_general(a, b, (((1,), (1,)), ((), ())), preferred_element_type=F32)


def iota(shape, axis):
    return lax.broadcasted_iota(jnp.int32, shape, axis)


def ranks(ids, blocks):
    rows = ids.shape[1]
    block = iota((blocks, rows), 0)
    one0 = (block == ids[0:1, :]).astype(F32)
    one1 = (block == ids[1:2, :]).astype(F32)
    before = (iota((rows, rows), 0) < iota((rows, rows), 1)).astype(BF)
    pre0 = dot(one0.astype(BF), before)
    pre1 = dot(one1.astype(BF), before) + jnp.sum(one0, axis=1, keepdims=True)
    rank0 = jnp.sum(one0 * pre0, axis=0, keepdims=True).astype(jnp.int32)
    rank1 = jnp.sum(one1 * pre1, axis=0, keepdims=True).astype(jnp.int32)
    return rank0, rank1


def route_kernel(ids_ref, resid_ref, bias_ref, out_ref, table_ref, pick_ref):
    slots, rows = pick_ref.shape

    @pl.when(pl.program_id(0) == 0)
    def _():
        ids = ids_ref[...]
        rank0, rank1 = ranks(ids, slots // CAP)
        slot = iota((slots, rows), 0)
        is0 = slot == ids[0:1, :] * CAP + rank0
        is1 = slot == ids[1:2, :] * CAP + rank1
        pick_ref[...] = jnp.where(is0 | is1, 1.0, 0.0).astype(BF)
        other = jnp.where(is0, ids[1:2, :] + 1, 0) + jnp.where(is1, ids[0:1, :] + 1, 0)
        table_ref[...] = jnp.sum(other.astype(F32), axis=1, keepdims=True).astype(jnp.int32) - 1

    centered = (resid_ref[...].astype(F32) - bias_ref[...]).astype(BF)
    step = 256
    for at in range(0, slots, step):
        out_ref[0, at : at + step, :] = dot(pick_ref[at : at + step, :], centered).astype(BF)


def route(ids, resid, dec_b, parts, slots):
    rows, width = resid.shape
    cols = width // parts
    return pl.pallas_call(
        route_kernel,
        grid=(parts,),
        in_specs=[
            pl.BlockSpec(ids.shape, lambda i: (0, 0)),
            pl.BlockSpec((rows, cols), lambda i: (0, i)),
            pl.BlockSpec((1, cols), lambda i: (0, i)),
        ],
        out_specs=[
            pl.BlockSpec((1, slots, cols), lambda i: (i, 0, 0)),
            pl.BlockSpec((slots, 1), lambda i: (0, 0)),
        ],
        out_shape=[
            jax.ShapeDtypeStruct((parts, slots, cols), BF),
            jax.ShapeDtypeStruct((slots, 1), jnp.int32),
        ],
        scratch_shapes=[pltpu.VMEM((slots, rows), BF)],
        compiler_params=params(),
        name="route_rows",
    )(ids, resid, dec_b.reshape(1, width))


def encode_kernel(rows_ref, weight_ref, bias_ref, pre_ref, proj_ref):
    count, _, cols = rows_ref.shape
    low = iota((1, 1, 128), 2) < LAT
    for p in range(2):
        rows = rows_ref[:, p * 16 : (p + 1) * 16, :].reshape(count * 16, cols)
        both = dot_nt(rows, weight_ref[p]).reshape(count, 2, CAP, 256)
        pre = jnp.where(low, both[:, 0, :, :128], both[:, 1, :, :128])
        pre_ref[:, p * CAP : (p + 1) * CAP, :] = pre + bias_ref[p : p + 1, :][None]
        proj = jnp.where(low, both[:, 0, :, 128:], both[:, 1, :, 128:])
        proj_ref[:, p * CAP : (p + 1) * CAP, :] = proj


def encode(arrived, weights, bias):
    sources, here, cols = arrived.shape
    step = 32
    shape = jax.ShapeDtypeStruct((sources, 2 * CAP, 128), F32)
    return pl.pallas_call(
        encode_kernel,
        grid=(sources // step,),
        in_specs=[
            pl.BlockSpec((step, here, cols), lambda i: (i, 0, 0)),
            pl.BlockSpec(weights.shape, lambda i: (0, 0, 0)),
            pl.BlockSpec(bias.shape, lambda i: (0, 0)),
        ],
        out_specs=[pl.BlockSpec((step, 2 * CAP, 128), lambda i: (i, 0, 0))] * 2,
        out_shape=[shape, shape],
        compiler_params=params(),
        name="encode_rows",
    )(arrived, weights, bias)


def activate_kernel(ids_ref, pre_ref, rows_ref, msg_ref):
    packed = pre_ref.shape[1]
    rows = ids_ref.shape[1]
    slots = 2 * packed
    ids = ids_ref[...]
    rank0, rank1 = ranks(ids, slots // CAP)
    total = pre_ref[0] + pre_ref[1] + pre_ref[2] + pre_ref[3]
    acts = jnp.maximum(total, 0.0).astype(BF)
    slot = iota((slots, rows), 0)
    found = []
    for k, rank in ((0, rank0), (1, rank1)):
        block = ids[k : k + 1, :]
        half = block % 2
        at = (block // 2) * CAP + rank
        here = jnp.where(slot == half * packed + at, 1.0, 0.0).astype(BF)
        found.append(dot_tn(here[:packed], acts)[:, :LAT] + dot_tn(here[packed:], acts)[:, LAT:])
    first, second = found
    straight = jnp.concatenate([first, second], axis=1).astype(BF)
    crossed = jnp.concatenate([second, first], axis=1).astype(BF)
    rows_ref[...] = straight
    pick0 = jnp.where(slot == ids[0:1, :] * CAP + rank0, 1.0, 0.0).astype(BF)
    pick1 = jnp.where(slot == ids[1:2, :] * CAP + rank1, 1.0, 0.0).astype(BF)
    msg = (dot(pick0, straight) + dot(pick1, crossed)).astype(BF)
    for copy in range(msg_ref.shape[0]):
        msg_ref[copy] = msg


def activate(ids, partial):
    parts, packed, lanes = partial.shape
    rows = ids.shape[1]
    return pl.pallas_call(
        activate_kernel,
        out_shape=[
            jax.ShapeDtypeStruct((rows, lanes), BF),
            jax.ShapeDtypeStruct((parts, 2 * packed, lanes), BF),
        ],
        compiler_params=params(),
        name="activate_rows",
    )(ids, partial)


def doubled(pair):
    source, target = iota((128, 256), 0), iota((128, 256), 1)
    copy = source == (target // 128) * LAT + target % LAT
    return dot(pair, jnp.where(copy, 1.0, 0.0).astype(BF)).astype(BF)


def lane_block(group):
    return (iota((1, 128), 1) // LAT + group * 2).astype(F32).astype(BF)


def own_expanded(own):
    count = own.shape[0]
    twice = jnp.concatenate([own, own], axis=1)
    mine = (iota((count, 256), 0) // CAP) % 4 == iota((count, 256), 1) // LAT
    return jnp.where(mine, twice.astype(F32), 0.0).astype(BF)


def recon_kernel(acts_ref, ids_ref, dec_ref, bias_ref, out_ref, twice_ref, name0_ref, name1_ref, acc_ref):
    at = pl.program_id(0)
    rows = acts_ref.shape[0]
    chunk = dec_ref.shape[0]

    @pl.when(at == 0)
    def _():
        twice_ref[...] = doubled(acts_ref[...])
        ids = ids_ref[...].astype(F32)
        name0_ref[...] = jnp.broadcast_to(ids[:, 0:1], (rows, 128)).astype(BF)
        name1_ref[...] = jnp.broadcast_to(ids[:, 1:2], (rows, 128)).astype(BF)
        acc_ref[...] = jnp.broadcast_to(bias_ref[...], acc_ref.shape)

    spread = []
    zero = jnp.zeros((rows, 128), BF)
    for q in range(chunk // 128):
        block = lane_block(at * (chunk // 128) + q)
        one = jnp.where(name0_ref[...] == block, twice_ref[:, :128], zero)
        spread.append(jnp.where(name1_ref[...] == block, twice_ref[:, 128:], one))
    acc_ref[...] += dot(jnp.concatenate(spread, axis=1), dec_ref[...])

    @pl.when(at == pl.num_programs(0) - 1)
    def _():
        out_ref[...] = acc_ref[...].astype(BF)


def reconstruct(acts, ids, dec_all, bias):
    rows = acts.shape[0]
    latents, cols = dec_all.shape
    chunk = 1024
    return pl.pallas_call(
        recon_kernel,
        grid=(latents // chunk,),
        in_specs=[
            pl.BlockSpec(acts.shape, lambda i: (0, 0)),
            pl.BlockSpec(ids.shape, lambda i: (0, 0)),
            pl.BlockSpec((chunk, cols), lambda i: (i, 0)),
            pl.BlockSpec((1, cols), lambda i: (0, 0)),
        ],
        out_specs=pl.BlockSpec((rows, cols), lambda i: (0, 0)),
        out_shape=jax.ShapeDtypeStruct((rows, cols), BF),
        scratch_shapes=[
            pltpu.VMEM((rows, 256), BF),
            pltpu.VMEM((rows, 128), BF),
            pltpu.VMEM((rows, 128), BF),
            pltpu.VMEM((rows, cols), F32),
        ],
        compiler_params=params(),
        name="reconstruct_rows",
    )(acts, ids, dec_all, bias)


def gate_kernel(scale, msg_ref, other_ref, gram_ref, own_gram_ref, proj_ref, out_ref):
    count = msg_ref.shape[0]
    twice = doubled(msg_ref[...])
    names = jnp.broadcast_to(other_ref[...].astype(F32), (count, 128)).astype(BF)
    zero = jnp.zeros((count, 128), BF)
    total = dot(own_expanded(twice[:, :128]), own_gram_ref[...])
    chunk = 1024
    for at in range(0, gram_ref.shape[0], chunk):
        spread = [
            jnp.where(names == lane_block(group), twice[:, 128:], zero)
            for group in range(at // 128, (at + chunk) // 128)
        ]
        total = total + dot(jnp.concatenate(spread, axis=1), gram_ref[at : at + chunk, :])
    total = total.reshape(count // 32, 4, CAP, 256)
    low = iota((1, 1, 128), 2) < LAT
    packed = []
    for p in range(2):
        lanes = slice(p * 128, (p + 1) * 128)
        packed.append(jnp.where(low, total[:, 2 * p, :, lanes], total[:, 2 * p + 1, :, lanes]))
    out_ref[...] = ((jnp.concatenate(packed, axis=1) - proj_ref[...]) * scale).astype(BF)


def gate_partial(scale, msg, other, gram, own_gram, proj):
    count, lanes = msg.shape
    step = 512
    return pl.pallas_call(
        lambda *refs: gate_kernel(scale, *refs),
        grid=(count // step,),
        in_specs=[
            pl.BlockSpec((step, lanes), lambda i: (i, 0)),
            pl.BlockSpec((step, 1), lambda i: (i, 0)),
            pl.BlockSpec(gram.shape, lambda i: (0, 0)),
            pl.BlockSpec(own_gram.shape, lambda i: (0, 0)),
            pl.BlockSpec((step // 32, 2 * CAP, 128), lambda i: (i, 0, 0)),
        ],
        out_specs=pl.BlockSpec((step // 32, 2 * CAP, 128), lambda i: (i, 0, 0)),
        out_shape=jax.ShapeDtypeStruct(proj.shape, BF),
        compiler_params=params(),
        name="gate_partial",
    )(msg, other, gram, own_gram, proj)


def mix_kernel(msg_ref, other_ref, dec_ref, own_dec_ref, out_ref, own_ref, twice_ref, name_ref):
    at = pl.program_id(0)
    count = msg_ref.shape[0]
    chunk = dec_ref.shape[0]

    @pl.when(at == 0)
    def _():
        twice = doubled(msg_ref[...])
        twice_ref[...] = twice[:, 128:]
        name_ref[...] = jnp.broadcast_to(other_ref[...].astype(F32), (count, 128)).astype(BF)
        own = own_expanded(twice[:, :128])
        own_ref[...] = own.T
        out_ref[...] = dot(dot(own_ref[...], own).astype(BF), own_dec_ref[...])

    zero = jnp.zeros((count, 128), BF)
    spread = []
    for q in range(chunk // 128):
        block = lane_block(at * (chunk // 128) + q)
        spread.append(jnp.where(name_ref[...] == block, twice_ref[...], zero))
    mixed = dot(own_ref[...], jnp.concatenate(spread, axis=1)).astype(BF)
    out_ref[...] += dot(mixed, dec_ref[...])


def mix(msg, other, dec_all, own_dec):
    count, lanes = msg.shape
    latents, cols = dec_all.shape
    chunk = 512
    return pl.pallas_call(
        mix_kernel,
        grid=(latents // chunk,),
        in_specs=[
            pl.BlockSpec(msg.shape, lambda i: (0, 0)),
            pl.BlockSpec(other.shape, lambda i: (0, 0)),
            pl.BlockSpec((chunk, cols), lambda i: (i, 0)),
            pl.BlockSpec(own_dec.shape, lambda i: (0, 0)),
        ],
        out_specs=pl.BlockSpec(own_dec.shape, lambda i: (0, 0)),
        out_shape=jax.ShapeDtypeStruct(own_dec.shape, F32),
        scratch_shapes=[
            pltpu.VMEM((256, count), BF),
            pltpu.VMEM((count, 128), BF),
            pltpu.VMEM((count, 128), BF),
        ],
        compiler_params=params(),
        name="mix_decoder",
    )(msg, other, dec_all, own_dec)


def grads_kernel(scale, gate_ref, msg_ref, rows_ref, mixed_ref, enc_ref, dec_ref, acc_ref):
    at = pl.program_id(0)
    count = msg_ref.shape[0]
    sources = count // 32
    own = own_expanded(doubled(msg_ref[...])[:, :128])
    total = gate_ref[0].astype(F32)
    for part in range(1, gate_ref.shape[0]):
        total = total + gate_ref[part].astype(F32)
    low = iota((1, 1, 128), 2) < LAT
    zero = jnp.zeros((sources, CAP, 128), F32)
    spread = []
    for p in range(2):
        piece = total[:, p * CAP : (p + 1) * CAP, :]
        for even in (True, False):
            kept = jnp.where(low if even else ~low, piece, 0.0)
            pair = [kept, zero] if p == 0 else [zero, kept]
            spread.append(jnp.concatenate(pair, axis=2))
    wide = jnp.concatenate(spread, axis=1).reshape(count, 256)
    wide = jnp.where(own.astype(F32) > 0, wide, 0.0).astype(BF)

    @pl.when(at == 0)
    def _():
        acc_ref[...] = jnp.zeros_like(acc_ref)

    acc_ref[...] += dot_tn(jnp.concatenate([wide, own], axis=1), rows_ref[...])

    @pl.when(at == pl.num_programs(0) - 1)
    def _():
        enc_ref[...] = acc_ref[:256, :]
        dec_ref[...] = (mixed_ref[...] - acc_ref[256:, :]) * scale


def grads(scale, gates, msg, rows, mixed):
    count, lanes = msg.shape
    cols = rows.shape[1]
    step = 512
    shape = jax.ShapeDtypeStruct(mixed.shape, F32)
    return pl.pallas_call(
        lambda *refs: grads_kernel(scale, *refs),
        grid=(count // step,),
        in_specs=[
            pl.BlockSpec((gates.shape[0], step // 32, 2 * CAP, 128), lambda i: (0, i, 0, 0)),
            pl.BlockSpec((step, lanes), lambda i: (i, 0)),
            pl.BlockSpec((step, cols), lambda i: (i, 0)),
            pl.BlockSpec(mixed.shape, lambda i: (0, 0)),
        ],
        out_specs=[pl.BlockSpec(mixed.shape, lambda i: (0, 0))] * 2,
        out_shape=[shape, shape],
        scratch_shapes=[pltpu.VMEM((512, cols), F32)],
        compiler_params=params(),
        name="dictionary_grads",
    )(gates, msg, rows, mixed)


def body(resid, block_ids, enc_w, enc_b, dec_w, dec_b):
    tok_rows, width = resid.shape
    parts = lax.axis_size("dp")
    shards = lax.axis_size("dict")
    local = enc_w.shape[0]
    here = local // LAT
    slots = here * shards * CAP
    cols = width // parts
    everyone = ("dp", "dict")
    devices = parts * shards
    blocks = here * shards
    scale = (blocks / (tok_rows * devices * block_ids.shape[1])) ** 0.5
    at_x = lax.axis_index("dp")
    at_dict = lax.axis_index("dict")

    ids = block_ids.T
    outgoing, table = route(ids, resid, dec_b, parts, slots)
    arrived = lax.all_to_all(
        outgoing.reshape(devices, here * CAP, cols), everyone, 0, 0, tiled=True
    )

    enc_x = lax.dynamic_slice(enc_w, (0, at_x * cols), (local, cols))
    dec_x = lax.dynamic_slice(dec_w, (0, at_x * cols), (local, cols))
    bias_x = lax.dynamic_slice(dec_b, (at_x * cols,), (cols,)).reshape(1, cols)
    dec_all = lax.all_gather(dec_x, "dict", axis=0, tiled=True)
    gram = dot_nt(dec_all, dec_x).astype(BF)
    own_gram = lax.dynamic_slice(gram, (at_dict * local, 0), (local, local))
    group_ids = lax.all_gather(block_ids, "dp", axis=0, tiled=True)
    tables = lax.all_gather(table.reshape(shards, here * CAP), everyone, axis=0, tiled=False)
    other = lax.dynamic_slice(tables, (0, at_dict, 0), (devices, 1, here * CAP))
    other = other.reshape(devices * here * CAP, 1)

    weights = jnp.concatenate(
        [enc_x.reshape(2, 2 * LAT, cols), dec_x.reshape(2, 2 * LAT, cols)], axis=1
    )
    bias = jnp.where(at_x == 0, enc_b, 0.0).reshape(2, 2 * LAT)
    pre, proj = encode(arrived, weights, bias)
    partial = lax.all_to_all(pre, everyone, 0, 0, tiled=True)
    acts, msg = activate(ids, partial.reshape(parts, shards * 2 * CAP, 128))
    message = lax.all_to_all(
        msg.reshape(devices, here * CAP, 128), everyone, 0, 0, tiled=True
    ).reshape(devices * here * CAP, 128)
    group_acts = lax.all_gather(acts, "dp", axis=0, tiled=True)

    recon_x = reconstruct(group_acts, group_ids, dec_all, bias_x)
    recon = lax.all_to_all(recon_x, "dp", 0, 1, tiled=True)

    gate = gate_partial(scale, message, other, gram, own_gram, proj)
    gates = lax.all_gather(gate, "dp", axis=0, tiled=False)
    mixed = mix(message, other, dec_all, dec_x)
    enc_grad, dec_grad = grads(
        scale, gates, message, arrived.reshape(devices * here * CAP, cols), mixed
    )
    return (recon, enc_grad, dec_grad)


def solution(mesh):
    placed = (
        P(("dp", "dict"), None),
        P(("dp", "dict"), None),
        P("dict", None),
        P("dict"),
        P("dict", None),
        P(),
    )
    return jax.shard_map(
        body,
        mesh=mesh,
        in_specs=placed,
        out_specs=(P(("dp", "dict"), None), P("dict", "dp"), P("dict", "dp")),
        check_vma=False,
    )
```

```python
import jax
import jax.numpy as jnp
from jax import lax
from jax.experimental import pallas as pl
from jax.experimental.pallas import tpu as pltpu
from jax.sharding import PartitionSpec as P

LAT = 64
CAP = 8
BF = jnp.bfloat16
F32 = jnp.float32
VMEM_LIMIT = 56 * 1024 * 1024


def params(**more):
    return pltpu.CompilerParams(vmem_limit_bytes=VMEM_LIMIT, **more)


def cost(flops, moved):
    return pl.CostEstimate(flops=int(flops), bytes_accessed=int(moved), transcendentals=0)


def dot(a, b):
    return jnp.dot(a, b, preferred_element_type=F32)


def dot_tn(a, b):
    return lax.dot_general(a, b, (((0,), (0,)), ((), ())), preferred_element_type=F32)


def dot_nt(a, b):
    return lax.dot_general(a, b, (((1,), (1,)), ((), ())), preferred_element_type=F32)


def iota(shape, axis):
    return lax.broadcasted_iota(jnp.int32, shape, axis)


def ranks(ids, blocks):
    rows = ids.shape[1]
    block = iota((blocks, rows), 0)
    one0 = (block == ids[0:1, :]).astype(F32)
    one1 = (block == ids[1:2, :]).astype(F32)
    before = (iota((rows, rows), 0) < iota((rows, rows), 1)).astype(BF)
    pre0 = dot(one0.astype(BF), before)
    pre1 = dot(one1.astype(BF), before) + jnp.sum(one0, axis=1, keepdims=True)
    rank0 = jnp.sum(one0 * pre0, axis=0, keepdims=True).astype(jnp.int32)
    rank1 = jnp.sum(one1 * pre1, axis=0, keepdims=True).astype(jnp.int32)
    return rank0, rank1


def table_kernel(ids_ref, out_ref):
    parts, shards, _, lanes = out_ref.shape
    rows = ids_ref.shape[1]
    ids = ids_ref[...]
    found = jnp.zeros((shards, lanes), F32)
    for k, rank in enumerate(ranks(ids, shards * 4)):
        block = ids[k : k + 1, :]
        other = (ids[1 - k : 2 - k, :] + 1).astype(F32)
        target = jnp.where(iota((shards, rows), 0) == block // 4, other, 0.0).astype(BF)
        place = iota((lanes, rows), 0) == (block % 4) * CAP + rank
        found = found + dot_nt(target, jnp.where(place, 1.0, 0.0).astype(BF))
    found = jnp.broadcast_to((found.astype(jnp.int32) - 1)[:, None, :], (shards, CAP, lanes))
    for copy in range(parts):
        out_ref[copy] = found


def table(ids, parts, shards):
    return pl.pallas_call(
        table_kernel,
        out_shape=jax.ShapeDtypeStruct((parts, shards, CAP, 128), jnp.int32),
        compiler_params=params(),
        cost_estimate=cost(2e7, 2**20),
        name="slot_table",
    )(ids)


def names_kernel(table_ref, out_ref):
    sources = table_ref.shape[0]
    here = out_ref.shape[0] // sources
    row = table_ref[:, 0:1, :].astype(F32)
    shape = (sources, here, 128)
    kept = jnp.where(iota(shape, 1) == iota(shape, 2), jnp.broadcast_to(row, shape), 0.0)
    name = jnp.sum(kept, axis=2, keepdims=True)
    out_ref[...] = jnp.broadcast_to(name, shape).reshape(sources * here, 128).astype(BF)


def names(tables, here):
    sources = tables.shape[0]
    step = 16
    return pl.pallas_call(
        names_kernel,
        grid=(sources // step,),
        in_specs=[pl.BlockSpec((step, CAP, 128), lambda i: (i, 0, 0))],
        out_specs=pl.BlockSpec((step * here, 128), lambda i: (i, 0)),
        out_shape=jax.ShapeDtypeStruct((sources * here, 128), BF),
        compiler_params=params(),
        cost_estimate=cost(2e7, 2**21),
        name="slot_names",
    )(tables)


def route_kernel(ids_ref, resid_ref, bias_ref, out_ref, pick_ref):
    slots, rows = pick_ref.shape

    @pl.when(pl.program_id(0) == 0)
    def _():
        ids = ids_ref[...]
        rank0, rank1 = ranks(ids, slots // CAP)
        slot = iota((slots, rows), 0)
        is0 = slot == ids[0:1, :] * CAP + rank0
        is1 = slot == ids[1:2, :] * CAP + rank1
        pick_ref[...] = jnp.where(is0 | is1, 1.0, 0.0).astype(BF)

    centered = (resid_ref[...].astype(F32) - bias_ref[...]).astype(BF)
    step = 256
    for at in range(0, slots, step):
        out_ref[0, at : at + step, :] = dot(pick_ref[at : at + step, :], centered).astype(BF)


def route(ids, resid, dec_b, parts, slots):
    rows, width = resid.shape
    cols = width // parts
    return pl.pallas_call(
        route_kernel,
        grid=(parts,),
        in_specs=[
            pl.BlockSpec(ids.shape, lambda i: (0, 0)),
            pl.BlockSpec((rows, cols), lambda i: (0, i)),
            pl.BlockSpec((1, cols), lambda i: (0, i)),
        ],
        out_specs=pl.BlockSpec((1, slots, cols), lambda i: (i, 0, 0)),
        out_shape=jax.ShapeDtypeStruct((parts, slots, cols), BF),
        scratch_shapes=[pltpu.VMEM((slots, rows), BF)],
        compiler_params=params(),
        cost_estimate=cost(2 * slots * rows * width, 10 * 2**20),
        name="route_rows",
    )(ids, resid, dec_b.reshape(1, width))


def encode_kernel(rows_ref, weight_ref, bias_ref, pre_ref, proj_ref):
    count, _, cols = rows_ref.shape
    low = iota((1, 1, 128), 2) < LAT
    for p in range(2):
        rows = rows_ref[:, p * 16 : (p + 1) * 16, :].reshape(count * 16, cols)
        both = dot_nt(rows, weight_ref[p]).reshape(count, 2, CAP, 256)
        pre = jnp.where(low, both[:, 0, :, :128], both[:, 1, :, :128])
        pre_ref[:, p * CAP : (p + 1) * CAP, :] = pre + bias_ref[p : p + 1, :][None]
        proj = jnp.where(low, both[:, 0, :, 128:], both[:, 1, :, 128:])
        proj_ref[:, p * CAP : (p + 1) * CAP, :] = proj


def encode(arrived, weights, bias):
    sources, here, cols = arrived.shape
    step = 32
    shape = jax.ShapeDtypeStruct((sources, 2 * CAP, 128), F32)
    return pl.pallas_call(
        encode_kernel,
        grid=(sources // step,),
        in_specs=[
            pl.BlockSpec((step, here, cols), lambda i: (i, 0, 0)),
            pl.BlockSpec(weights.shape, lambda i: (0, 0, 0)),
            pl.BlockSpec(bias.shape, lambda i: (0, 0)),
        ],
        out_specs=[pl.BlockSpec((step, 2 * CAP, 128), lambda i: (i, 0, 0))] * 2,
        out_shape=[shape, shape],
        compiler_params=params(),
        cost_estimate=cost(2 * sources * here * cols * 256, 11 * 2**20),
        name="encode_rows",
    )(arrived, weights, bias)


def activate_kernel(ids_ref, columns_ref, pre_ref, rows_ref, msg_ref):
    packed = pre_ref.shape[1]
    rows = ids_ref.shape[1]
    slots = 2 * packed
    ids = ids_ref[...]
    rank0, rank1 = ranks(ids, slots // CAP)
    total = pre_ref[0] + pre_ref[1] + pre_ref[2] + pre_ref[3]
    acts = jnp.maximum(total, 0.0).astype(BF)
    slot = iota((slots, rows), 0)
    found = []
    for k, rank in ((0, rank0), (1, rank1)):
        block = ids[k : k + 1, :]
        half = block % 2
        at = (block // 2) * CAP + rank
        here = jnp.where(slot == half * packed + at, 1.0, 0.0).astype(BF)
        found.append(dot_tn(here[:packed], acts)[:, :LAT] + dot_tn(here[packed:], acts)[:, LAT:])
    first, second = found
    straight = jnp.concatenate([first, second], axis=1).astype(BF)
    crossed = jnp.concatenate([second, first], axis=1).astype(BF)
    lane = iota((rows, 128), 1)
    named = jnp.where(lane == 0, columns_ref[:, 0:1], jnp.where(lane == 1, columns_ref[:, 1:2], 0))
    group = jnp.concatenate([straight, named.astype(F32).astype(BF)], axis=1)
    for copy in range(rows_ref.shape[0]):
        rows_ref[copy] = group
    pick0 = jnp.where(slot == ids[0:1, :] * CAP + rank0, 1.0, 0.0).astype(BF)
    pick1 = jnp.where(slot == ids[1:2, :] * CAP + rank1, 1.0, 0.0).astype(BF)
    msg = (dot(pick0, straight) + dot(pick1, crossed)).astype(BF)
    for copy in range(msg_ref.shape[0]):
        msg_ref[copy] = msg


def activate(ids, columns, partial):
    parts, packed, lanes = partial.shape
    rows = ids.shape[1]
    return pl.pallas_call(
        activate_kernel,
        out_shape=[
            jax.ShapeDtypeStruct((parts, rows, 2 * lanes), BF),
            jax.ShapeDtypeStruct((parts, 2 * packed, lanes), BF),
        ],
        compiler_params=params(),
        cost_estimate=cost(8 * packed * rows * lanes, 3 * 2**20),
        name="activate_rows",
    )(ids, columns, partial)


def doubled(pair):
    source, target = iota((128, 256), 0), iota((128, 256), 1)
    copy = source == (target // 128) * LAT + target % LAT
    return dot(pair, jnp.where(copy, 1.0, 0.0).astype(BF)).astype(BF)


def lane_block(group):
    return (iota((1, 128), 1) // LAT + group * 2).astype(F32).astype(BF)


def own_expanded(own):
    count = own.shape[0]
    twice = jnp.concatenate([own, own], axis=1)
    mine = (iota((count, 256), 0) // CAP) % 4 == iota((count, 256), 1) // LAT
    return jnp.where(mine, twice.astype(F32), 0.0).astype(BF)


def recon_kernel(
    acts_ref, dec_ref, own_dec_ref, bias_ref, out_ref, gram_ref, twice_ref, name0_ref, name1_ref, acc_ref
):
    at = pl.program_id(0)
    rows = acts_ref.shape[0]
    chunk = dec_ref.shape[0]

    @pl.when(at == 0)
    def _():
        twice_ref[...] = doubled(acts_ref[:, :128])
        ids = acts_ref[:, 128:].astype(F32)
        name0_ref[...] = jnp.broadcast_to(ids[:, 0:1], (rows, 128)).astype(BF)
        name1_ref[...] = jnp.broadcast_to(ids[:, 1:2], (rows, 128)).astype(BF)
        acc_ref[...] = jnp.broadcast_to(bias_ref[...], acc_ref.shape)

    spread = []
    zero = jnp.zeros((rows, 128), BF)
    for q in range(chunk // 128):
        block = lane_block(at * (chunk // 128) + q)
        one = jnp.where(name0_ref[...] == block, twice_ref[:, :128], zero)
        spread.append(jnp.where(name1_ref[...] == block, twice_ref[:, 128:], one))
    acc_ref[...] += dot(jnp.concatenate(spread, axis=1), dec_ref[...])
    gram_ref[...] = dot_nt(dec_ref[...], own_dec_ref[...]).astype(BF)

    @pl.when(at == pl.num_programs(0) - 1)
    def _():
        out_ref[...] = acc_ref[...].astype(BF)


def reconstruct(acts, dec_all, own_dec, bias):
    rows = acts.shape[0]
    latents, cols = dec_all.shape
    chunk = 1024
    return pl.pallas_call(
        recon_kernel,
        grid=(latents // chunk,),
        in_specs=[
            pl.BlockSpec(acts.shape, lambda i: (0, 0)),
            pl.BlockSpec((chunk, cols), lambda i: (i, 0)),
            pl.BlockSpec(own_dec.shape, lambda i: (0, 0)),
            pl.BlockSpec((1, cols), lambda i: (0, 0)),
        ],
        out_specs=[
            pl.BlockSpec((rows, cols), lambda i: (0, 0)),
            pl.BlockSpec((chunk, own_dec.shape[0]), lambda i: (i, 0)),
        ],
        out_shape=[
            jax.ShapeDtypeStruct((rows, cols), BF),
            jax.ShapeDtypeStruct((latents, own_dec.shape[0]), BF),
        ],
        scratch_shapes=[
            pltpu.VMEM((rows, 256), BF),
            pltpu.VMEM((rows, 128), BF),
            pltpu.VMEM((rows, 128), BF),
            pltpu.VMEM((rows, cols), F32),
        ],
        compiler_params=params(),
        cost_estimate=cost(2 * latents * cols * (rows + own_dec.shape[0]), 24 * 2**20),
        name="reconstruct_rows",
    )(acts, dec_all, own_dec, bias)


def gate_kernel(scale, msg_ref, other_ref, gram_ref, own_gram_ref, proj_ref, out_ref):
    count = msg_ref.shape[0]
    twice = doubled(msg_ref[...])
    names = other_ref[...]
    zero = jnp.zeros((count, 128), BF)
    total = dot(own_expanded(twice[:, :128]), own_gram_ref[...])
    chunk = 1024
    for at in range(0, gram_ref.shape[0], chunk):
        spread = [
            jnp.where(names == lane_block(group), twice[:, 128:], zero)
            for group in range(at // 128, (at + chunk) // 128)
        ]
        total = total + dot(jnp.concatenate(spread, axis=1), gram_ref[at : at + chunk, :])
    total = total.reshape(count // 32, 4, CAP, 256)
    low = iota((1, 1, 128), 2) < LAT
    packed = []
    for p in range(2):
        lanes = slice(p * 128, (p + 1) * 128)
        packed.append(jnp.where(low, total[:, 2 * p, :, lanes], total[:, 2 * p + 1, :, lanes]))
    out_ref[...] = ((jnp.concatenate(packed, axis=1) - proj_ref[...]) * scale).astype(BF)


def gate_partial(scale, msg, other, gram, own_gram, proj):
    count, lanes = msg.shape
    step = 512
    return pl.pallas_call(
        lambda *refs: gate_kernel(scale, *refs),
        grid=(count // step,),
        in_specs=[
            pl.BlockSpec((step, lanes), lambda i: (i, 0)),
            pl.BlockSpec((step, lanes), lambda i: (i, 0)),
            pl.BlockSpec(gram.shape, lambda i: (0, 0)),
            pl.BlockSpec(own_gram.shape, lambda i: (0, 0)),
            pl.BlockSpec((step // 32, 2 * CAP, 128), lambda i: (i, 0, 0)),
        ],
        out_specs=pl.BlockSpec((step // 32, 2 * CAP, 128), lambda i: (i, 0, 0)),
        out_shape=jax.ShapeDtypeStruct(proj.shape, BF),
        compiler_params=params(),
        cost_estimate=cost(2 * count * gram.shape[0] * gram.shape[1], 10 * 2**20),
        name="gate_partial",
    )(msg, other, gram, own_gram, proj)


def mix_kernel(msg_ref, name_ref, dec_ref, own_dec_ref, out_ref, own_ref, twice_ref):
    at = pl.program_id(0)
    count = msg_ref.shape[0]
    chunk = dec_ref.shape[0]

    @pl.when(at == 0)
    def _():
        twice = doubled(msg_ref[...])
        twice_ref[...] = twice[:, 128:]
        own = own_expanded(twice[:, :128])
        own_ref[...] = own.T
        out_ref[...] = dot(dot(own_ref[...], own).astype(BF), own_dec_ref[...])

    zero = jnp.zeros((count, 128), BF)
    spread = []
    for q in range(chunk // 128):
        block = lane_block(at * (chunk // 128) + q)
        spread.append(jnp.where(name_ref[...] == block, twice_ref[...], zero))
    mixed = dot(own_ref[...], jnp.concatenate(spread, axis=1)).astype(BF)
    out_ref[...] += dot(mixed, dec_ref[...])


def mix(msg, other, dec_all, own_dec):
    count, lanes = msg.shape
    latents, cols = dec_all.shape
    chunk = 512
    return pl.pallas_call(
        mix_kernel,
        grid=(latents // chunk,),
        in_specs=[
            pl.BlockSpec(msg.shape, lambda i: (0, 0)),
            pl.BlockSpec(other.shape, lambda i: (0, 0)),
            pl.BlockSpec((chunk, cols), lambda i: (i, 0)),
            pl.BlockSpec(own_dec.shape, lambda i: (0, 0)),
        ],
        out_specs=pl.BlockSpec(own_dec.shape, lambda i: (0, 0)),
        out_shape=jax.ShapeDtypeStruct(own_dec.shape, F32),
        scratch_shapes=[
            pltpu.VMEM((256, count), BF),
            pltpu.VMEM((count, 128), BF),
        ],
        compiler_params=params(),
        cost_estimate=cost(2 * latents * 256 * (count + cols), 20 * 2**20),
        name="mix_decoder",
    )(msg, other, dec_all, own_dec)


def grads_kernel(scale, gate_ref, msg_ref, rows_ref, mixed_ref, enc_ref, dec_ref, acc_ref):
    at = pl.program_id(0)
    count = msg_ref.shape[0]
    sources = count // 32
    own = own_expanded(doubled(msg_ref[...])[:, :128])
    total = gate_ref[0].astype(F32)
    for part in range(1, gate_ref.shape[0]):
        total = total + gate_ref[part].astype(F32)
    low = iota((1, 1, 128), 2) < LAT
    zero = jnp.zeros((sources, CAP, 128), F32)
    spread = []
    for p in range(2):
        piece = total[:, p * CAP : (p + 1) * CAP, :]
        for even in (True, False):
            kept = jnp.where(low if even else ~low, piece, 0.0)
            pair = [kept, zero] if p == 0 else [zero, kept]
            spread.append(jnp.concatenate(pair, axis=2))
    wide = jnp.concatenate(spread, axis=1).reshape(count, 256)
    wide = jnp.where(own.astype(F32) > 0, wide, 0.0).astype(BF)

    @pl.when(at == 0)
    def _():
        acc_ref[...] = jnp.zeros_like(acc_ref)

    acc_ref[...] += dot_tn(jnp.concatenate([wide, own], axis=1), rows_ref[...])

    @pl.when(at == pl.num_programs(0) - 1)
    def _():
        enc_ref[...] = acc_ref[:256, :]
        dec_ref[...] = (mixed_ref[...] - acc_ref[256:, :]) * scale


def grads(scale, gates, msg, rows, mixed):
    count, lanes = msg.shape
    cols = rows.shape[1]
    step = 512
    shape = jax.ShapeDtypeStruct(mixed.shape, F32)
    return pl.pallas_call(
        lambda *refs: grads_kernel(scale, *refs),
        grid=(count // step,),
        in_specs=[
            pl.BlockSpec((gates.shape[0], step // 32, 2 * CAP, 128), lambda i: (0, i, 0, 0)),
            pl.BlockSpec((step, lanes), lambda i: (i, 0)),
            pl.BlockSpec((step, cols), lambda i: (i, 0)),
            pl.BlockSpec(mixed.shape, lambda i: (0, 0)),
        ],
        out_specs=[pl.BlockSpec(mixed.shape, lambda i: (0, 0))] * 2,
        out_shape=[shape, shape],
        scratch_shapes=[pltpu.VMEM((512, cols), F32)],
        compiler_params=params(),
        cost_estimate=cost(4 * count * cols * 256, 16 * 2**20),
        name="dictionary_grads",
    )(gates, msg, rows, mixed)


def body(resid, block_ids, enc_w, enc_b, dec_w, dec_b):
    tok_rows, width = resid.shape
    parts = lax.axis_size("dp")
    shards = lax.axis_size("dict")
    local = enc_w.shape[0]
    here = local // LAT
    slots = here * shards * CAP
    cols = width // parts
    everyone = ("dp", "dict")
    devices = parts * shards
    blocks = here * shards
    scale = (blocks / (tok_rows * devices * block_ids.shape[1])) ** 0.5
    at_x = lax.axis_index("dp")
    at_dict = lax.axis_index("dict")

    ids = block_ids.T
    tables = lax.all_to_all(
        table(ids, parts, shards).reshape(devices, CAP, 128), everyone, 0, 0, tiled=True
    )
    outgoing = route(ids, resid, dec_b, parts, slots)
    arrived = lax.all_to_all(
        outgoing.reshape(devices, here * CAP, cols), everyone, 0, 0, tiled=True
    )

    enc_x = lax.dynamic_slice(enc_w, (0, at_x * cols), (local, cols))
    dec_x = lax.dynamic_slice(dec_w, (0, at_x * cols), (local, cols))
    bias_x = lax.dynamic_slice(dec_b, (at_x * cols,), (cols,)).reshape(1, cols)
    dec_all = lax.all_gather(dec_x, "dict", axis=0, tiled=True)
    other = names(tables, here * CAP)

    weights = jnp.concatenate(
        [enc_x.reshape(2, 2 * LAT, cols), dec_x.reshape(2, 2 * LAT, cols)], axis=1
    )
    bias = jnp.where(at_x == 0, enc_b, 0.0).reshape(2, 2 * LAT)
    pre, proj = encode(arrived, weights, bias)
    partial = lax.all_to_all(pre, everyone, 0, 0, tiled=True)
    acts, msg = activate(ids, block_ids, partial.reshape(parts, shards * 2 * CAP, 128))
    group_acts = lax.all_to_all(acts, "dp", 0, 0, tiled=True)
    message = lax.all_to_all(
        msg.reshape(devices, here * CAP, 128), everyone, 0, 0, tiled=True
    ).reshape(devices * here * CAP, 128)

    recon_x, gram = reconstruct(group_acts.reshape(parts * tok_rows, 256), dec_all, dec_x, bias_x)
    recon = lax.all_to_all(recon_x, "dp", 0, 1, tiled=True)

    own_gram = lax.dynamic_slice(gram, (at_dict * local, 0), (local, local))
    gate = gate_partial(scale, message, other, gram, own_gram, proj)
    gates = lax.all_gather(gate, "dp", axis=0, tiled=False)
    mixed = mix(message, other, dec_all, dec_x)
    enc_grad, dec_grad = grads(
        scale, gates, message, arrived.reshape(devices * here * CAP, cols), mixed
    )
    return (recon, enc_grad, dec_grad)


def solution(mesh):
    placed = (
        P(("dp", "dict"), None),
        P(("dp", "dict"), None),
        P("dict", None),
        P("dict"),
        P("dict", None),
        P(),
    )
    return jax.shard_map(
        body,
        mesh=mesh,
        in_specs=placed,
        out_specs=(P(("dp", "dict"), None), P("dict", "dp"), P("dict", "dp")),
        check_vma=False,
    )
```

```python
import jax
import jax.numpy as jnp
from jax import lax
from jax.experimental import pallas as pl
from jax.experimental.pallas import tpu as pltpu
from jax.sharding import PartitionSpec as P

LAT = 64
CAP = 8
BF = jnp.bfloat16
F32 = jnp.float32
VMEM_LIMIT = 56 * 1024 * 1024


def params(**more):
    return pltpu.CompilerParams(vmem_limit_bytes=VMEM_LIMIT, **more)


def cost(flops, moved):
    return pl.CostEstimate(flops=int(flops), bytes_accessed=int(moved), transcendentals=0)


def dot(a, b):
    return jnp.dot(a, b, preferred_element_type=F32)


def dot_tn(a, b):
    return lax.dot_general(a, b, (((0,), (0,)), ((), ())), preferred_element_type=F32)


def dot_nt(a, b):
    return lax.dot_general(a, b, (((1,), (1,)), ((), ())), preferred_element_type=F32)


def iota(shape, axis):
    return lax.broadcasted_iota(jnp.int32, shape, axis)


def ranks(ids, blocks):
    rows = ids.shape[1]
    block = iota((blocks, rows), 0)
    one0 = (block == ids[0:1, :]).astype(F32)
    one1 = (block == ids[1:2, :]).astype(F32)
    before = (iota((rows, rows), 0) < iota((rows, rows), 1)).astype(BF)
    pre0 = dot(one0.astype(BF), before)
    pre1 = dot(one1.astype(BF), before) + jnp.sum(one0, axis=1, keepdims=True)
    rank0 = jnp.sum(one0 * pre0, axis=0, keepdims=True).astype(jnp.int32)
    rank1 = jnp.sum(one1 * pre1, axis=0, keepdims=True).astype(jnp.int32)
    return rank0, rank1


def slot_table(ids, shards, lanes=128):
    rows = ids.shape[1]
    found = jnp.zeros((shards, lanes), F32)
    for k, rank in enumerate(ranks(ids, shards * 4)):
        block = ids[k : k + 1, :]
        other = (ids[1 - k : 2 - k, :] + 1).astype(F32)
        target = jnp.where(iota((shards, rows), 0) == block // 4, other, 0.0).astype(BF)
        place = iota((lanes, rows), 0) == (block % 4) * CAP + rank
        found = found + dot_nt(target, jnp.where(place, 1.0, 0.0).astype(BF))
    return found - 1.0


def slot_names(table):
    sources = table.shape[0]
    shape = (sources, 32, 128)
    row = jnp.concatenate([table, table], axis=1).astype(F32)
    kept = jnp.where(iota(shape, 1) == iota(shape, 2), row, 0.0).astype(BF)
    return dot(kept.reshape(sources * 32, 128), jnp.ones((128, 128), BF)).astype(BF)


def route_kernel(ids_ref, resid_ref, bias_ref, out_ref, pick_ref):
    slots, rows = pick_ref.shape

    @pl.when(pl.program_id(0) == 0)
    def _():
        ids = ids_ref[...]
        rank0, rank1 = ranks(ids, slots // CAP)
        slot = iota((slots, rows), 0)
        is0 = slot == ids[0:1, :] * CAP + rank0
        is1 = slot == ids[1:2, :] * CAP + rank1
        pick_ref[...] = jnp.where(is0 | is1, 1.0, 0.0).astype(BF)

    centered = (resid_ref[...].astype(F32) - bias_ref[...]).astype(BF)
    step = 256
    for at in range(0, slots, step):
        out_ref[0, at : at + step, :] = dot(pick_ref[at : at + step, :], centered).astype(BF)


def route(ids, resid, dec_b, parts, slots):
    rows, width = resid.shape
    cols = width // parts
    return pl.pallas_call(
        route_kernel,
        grid=(parts,),
        in_specs=[
            pl.BlockSpec(ids.shape, lambda i: (0, 0)),
            pl.BlockSpec((rows, cols), lambda i: (0, i)),
            pl.BlockSpec((1, cols), lambda i: (0, i)),
        ],
        out_specs=pl.BlockSpec((1, slots, cols), lambda i: (i, 0, 0)),
        out_shape=jax.ShapeDtypeStruct((parts, slots, cols), BF),
        scratch_shapes=[pltpu.VMEM((slots, rows), BF)],
        compiler_params=params(),
        cost_estimate=cost(2 * slots * rows * width, 10 * 2**20),
        name="route_rows",
    )(ids, resid, dec_b.reshape(1, width))


def encode_kernel(rows_ref, weight_ref, bias_ref, pre_ref, proj_ref):
    count, _, cols = rows_ref.shape
    low = iota((1, 1, 128), 2) < LAT
    for p in range(2):
        rows = rows_ref[:, p * 16 : (p + 1) * 16, :].reshape(count * 16, cols)
        both = dot_nt(rows, weight_ref[p]).reshape(count, 2, CAP, 256)
        pre = jnp.where(low, both[:, 0, :, :128], both[:, 1, :, :128])
        pre_ref[:, p * CAP : (p + 1) * CAP, :] = pre + bias_ref[p : p + 1, :][None]
        proj = jnp.where(low, both[:, 0, :, 128:], both[:, 1, :, 128:])
        proj_ref[:, p * CAP : (p + 1) * CAP, :] = proj


def encode(arrived, weights, bias):
    sources, here, cols = arrived.shape
    step = 32
    shape = jax.ShapeDtypeStruct((sources, 2 * CAP, 128), F32)
    return pl.pallas_call(
        encode_kernel,
        grid=(sources // step,),
        in_specs=[
            pl.BlockSpec((step, here, cols), lambda i: (i, 0, 0)),
            pl.BlockSpec(weights.shape, lambda i: (0, 0, 0)),
            pl.BlockSpec(bias.shape, lambda i: (0, 0)),
        ],
        out_specs=[pl.BlockSpec((step, 2 * CAP, 128), lambda i: (i, 0, 0))] * 2,
        out_shape=[shape, shape],
        compiler_params=params(),
        cost_estimate=cost(2 * sources * here * cols * 256, 11 * 2**20),
        name="encode_rows",
    )(arrived, weights, bias)


def activate_kernel(ids_ref, columns_ref, pre_ref, rows_ref, msg_ref):
    shards = msg_ref.shape[1]
    packed = pre_ref.shape[1]
    rows = ids_ref.shape[1]
    slots = 2 * packed
    ids = ids_ref[...]
    rank0, rank1 = ranks(ids, slots // CAP)
    total = pre_ref[0] + pre_ref[1] + pre_ref[2] + pre_ref[3]
    acts = jnp.maximum(total, 0.0).astype(BF)
    slot = iota((slots, rows), 0)
    found = []
    for k, rank in ((0, rank0), (1, rank1)):
        block = ids[k : k + 1, :]
        half = block % 2
        at = (block // 2) * CAP + rank
        here = jnp.where(slot == half * packed + at, 1.0, 0.0).astype(BF)
        found.append(dot_tn(here[:packed], acts)[:, :LAT] + dot_tn(here[packed:], acts)[:, LAT:])
    first, second = found
    straight = jnp.concatenate([first, second], axis=1).astype(BF)
    crossed = jnp.concatenate([second, first], axis=1).astype(BF)
    lane = iota((rows, 128), 1)
    named = jnp.where(lane == 0, columns_ref[:, 0:1], jnp.where(lane == 1, columns_ref[:, 1:2], 0))
    group = jnp.concatenate([straight, named.astype(F32).astype(BF)], axis=1)
    for copy in range(rows_ref.shape[0]):
        rows_ref[copy] = group
    pick0 = jnp.where(slot == ids[0:1, :] * CAP + rank0, 1.0, 0.0).astype(BF)
    pick1 = jnp.where(slot == ids[1:2, :] * CAP + rank1, 1.0, 0.0).astype(BF)
    msg = (dot(pick0, straight) + dot(pick1, crossed)).astype(BF)
    msg = msg.reshape(shards, slots // shards, 128)
    table = slot_table(ids, shards)
    table = jnp.broadcast_to(table[:, None, :], (shards, 16, 128)).astype(BF)
    for copy in range(msg_ref.shape[0]):
        msg_ref[copy, :, : slots // shards, :] = msg
        msg_ref[copy, :, slots // shards :, :] = table


def activate(ids, columns, partial, shards):
    parts, packed, lanes = partial.shape
    rows = ids.shape[1]
    return pl.pallas_call(
        activate_kernel,
        out_shape=[
            jax.ShapeDtypeStruct((parts, rows, 2 * lanes), BF),
            jax.ShapeDtypeStruct((parts, shards, 2 * packed // shards + 16, lanes), BF),
        ],
        compiler_params=params(),
        cost_estimate=cost(8 * packed * rows * lanes, 3 * 2**20),
        name="activate_rows",
    )(ids, columns, partial)


def doubled(pair):
    source, target = iota((128, 256), 0), iota((128, 256), 1)
    copy = source == (target // 128) * LAT + target % LAT
    return dot(pair, jnp.where(copy, 1.0, 0.0).astype(BF)).astype(BF)


def lane_block(group):
    return (iota((1, 128), 1) // LAT + group * 2).astype(F32).astype(BF)


def own_expanded(own):
    count = own.shape[0]
    twice = jnp.concatenate([own, own], axis=1)
    mine = (iota((count, 256), 0) // CAP) % 4 == iota((count, 256), 1) // LAT
    return jnp.where(mine, twice.astype(F32), 0.0).astype(BF)


def recon_kernel(
    acts_ref, dec_ref, own_dec_ref, bias_ref, out_ref, gram_ref, twice_ref, name0_ref, name1_ref, acc_ref
):
    at = pl.program_id(0)
    rows = acts_ref.shape[0]
    chunk = dec_ref.shape[0]

    @pl.when(at == 0)
    def _():
        twice_ref[...] = doubled(acts_ref[:, :128])
        ids = acts_ref[:, 128:].astype(F32)
        name0_ref[...] = jnp.broadcast_to(ids[:, 0:1], (rows, 128)).astype(BF)
        name1_ref[...] = jnp.broadcast_to(ids[:, 1:2], (rows, 128)).astype(BF)
        acc_ref[...] = jnp.broadcast_to(bias_ref[...], acc_ref.shape)

    spread = []
    zero = jnp.zeros((rows, 128), BF)
    for q in range(chunk // 128):
        block = lane_block(at * (chunk // 128) + q)
        one = jnp.where(name0_ref[...] == block, twice_ref[:, :128], zero)
        spread.append(jnp.where(name1_ref[...] == block, twice_ref[:, 128:], one))
    acc_ref[...] += dot(jnp.concatenate(spread, axis=1), dec_ref[...])
    gram_ref[...] = dot_nt(dec_ref[...], own_dec_ref[...]).astype(BF)

    @pl.when(at == pl.num_programs(0) - 1)
    def _():
        out_ref[...] = acc_ref[...].astype(BF)


def reconstruct(acts, dec_all, own_dec, bias):
    rows = acts.shape[0]
    latents, cols = dec_all.shape
    chunk = 1024
    return pl.pallas_call(
        recon_kernel,
        grid=(latents // chunk,),
        in_specs=[
            pl.BlockSpec(acts.shape, lambda i: (0, 0)),
            pl.BlockSpec((chunk, cols), lambda i: (i, 0)),
            pl.BlockSpec(own_dec.shape, lambda i: (0, 0)),
            pl.BlockSpec((1, cols), lambda i: (0, 0)),
        ],
        out_specs=[
            pl.BlockSpec((rows, cols), lambda i: (0, 0)),
            pl.BlockSpec((chunk, own_dec.shape[0]), lambda i: (i, 0)),
        ],
        out_shape=[
            jax.ShapeDtypeStruct((rows, cols), BF),
            jax.ShapeDtypeStruct((latents, own_dec.shape[0]), BF),
        ],
        scratch_shapes=[
            pltpu.VMEM((rows, 256), BF),
            pltpu.VMEM((rows, 128), BF),
            pltpu.VMEM((rows, 128), BF),
            pltpu.VMEM((rows, cols), F32),
        ],
        compiler_params=params(),
        cost_estimate=cost(2 * latents * cols * (rows + own_dec.shape[0]), 24 * 2**20),
        name="reconstruct_rows",
    )(acts, dec_all, own_dec, bias)


def gate_kernel(scale, msg_ref, gram_ref, own_gram_ref, proj_ref, out_ref):
    count = msg_ref.shape[0] * 32
    twice = doubled(msg_ref[:, :32, :].reshape(count, 128))
    names = slot_names(msg_ref[:, 32:, :])
    zero = jnp.zeros((count, 128), BF)
    total = dot(own_expanded(twice[:, :128]), own_gram_ref[...])
    chunk = 1024
    for at in range(0, gram_ref.shape[0], chunk):
        spread = [
            jnp.where(names == lane_block(group), twice[:, 128:], zero)
            for group in range(at // 128, (at + chunk) // 128)
        ]
        total = total + dot(jnp.concatenate(spread, axis=1), gram_ref[at : at + chunk, :])
    total = total.reshape(count // 32, 4, CAP, 256)
    low = iota((1, 1, 128), 2) < LAT
    packed = []
    for p in range(2):
        lanes = slice(p * 128, (p + 1) * 128)
        packed.append(jnp.where(low, total[:, 2 * p, :, lanes], total[:, 2 * p + 1, :, lanes]))
    out_ref[...] = ((jnp.concatenate(packed, axis=1) - proj_ref[...]) * scale).astype(BF)


def gate_partial(scale, msg, gram, own_gram, proj):
    sources, tall, lanes = msg.shape
    count = sources * 32
    step = 512
    return pl.pallas_call(
        lambda *refs: gate_kernel(scale, *refs),
        grid=(count // step,),
        in_specs=[
            pl.BlockSpec((step // 32, tall, lanes), lambda i: (i, 0, 0)),
            pl.BlockSpec(gram.shape, lambda i: (0, 0)),
            pl.BlockSpec(own_gram.shape, lambda i: (0, 0)),
            pl.BlockSpec((step // 32, 2 * CAP, 128), lambda i: (i, 0, 0)),
        ],
        out_specs=pl.BlockSpec((step // 32, 2 * CAP, 128), lambda i: (i, 0, 0)),
        out_shape=jax.ShapeDtypeStruct(proj.shape, BF),
        compiler_params=params(),
        cost_estimate=cost(2 * count * gram.shape[0] * gram.shape[1], 10 * 2**20),
        name="gate_partial",
    )(msg, gram, own_gram, proj)


def mix_kernel(msg_ref, dec_ref, own_dec_ref, out_ref, own_ref, twice_ref, name_ref):
    at = pl.program_id(0)
    count = msg_ref.shape[0] * 32
    chunk = dec_ref.shape[0]

    @pl.when(at == 0)
    def _():
        twice = doubled(msg_ref[:, :32, :].reshape(count, 128))
        twice_ref[...] = twice[:, 128:]
        name_ref[...] = slot_names(msg_ref[:, 32:, :])
        own = own_expanded(twice[:, :128])
        own_ref[...] = own.T
        out_ref[...] = dot(dot(own_ref[...], own).astype(BF), own_dec_ref[...])

    zero = jnp.zeros((count, 128), BF)
    spread = []
    for q in range(chunk // 128):
        block = lane_block(at * (chunk // 128) + q)
        spread.append(jnp.where(name_ref[...] == block, twice_ref[...], zero))
    mixed = dot(own_ref[...], jnp.concatenate(spread, axis=1)).astype(BF)
    out_ref[...] += dot(mixed, dec_ref[...])


def mix(msg, dec_all, own_dec):
    count = msg.shape[0] * 32
    latents, cols = dec_all.shape
    chunk = 512
    return pl.pallas_call(
        mix_kernel,
        grid=(latents // chunk,),
        in_specs=[
            pl.BlockSpec(msg.shape, lambda i: (0, 0, 0)),
            pl.BlockSpec((chunk, cols), lambda i: (i, 0)),
            pl.BlockSpec(own_dec.shape, lambda i: (0, 0)),
        ],
        out_specs=pl.BlockSpec(own_dec.shape, lambda i: (0, 0)),
        out_shape=jax.ShapeDtypeStruct(own_dec.shape, F32),
        scratch_shapes=[
            pltpu.VMEM((256, count), BF),
            pltpu.VMEM((count, 128), BF),
            pltpu.VMEM((count, 128), BF),
        ],
        compiler_params=params(),
        cost_estimate=cost(2 * latents * 256 * (count + cols), 20 * 2**20),
        name="mix_decoder",
    )(msg, dec_all, own_dec)


def grads_kernel(scale, gate_ref, msg_ref, rows_ref, mixed_ref, enc_ref, dec_ref, acc_ref):
    at = pl.program_id(0)
    sources = msg_ref.shape[0]
    count = sources * 32
    own = own_expanded(doubled(msg_ref[:, :32, :].reshape(count, 128))[:, :128])
    total = gate_ref[0].astype(F32)
    for part in range(1, gate_ref.shape[0]):
        total = total + gate_ref[part].astype(F32)
    low = iota((1, 1, 128), 2) < LAT
    zero = jnp.zeros((sources, CAP, 128), F32)
    spread = []
    for p in range(2):
        piece = total[:, p * CAP : (p + 1) * CAP, :]
        for even in (True, False):
            kept = jnp.where(low if even else ~low, piece, 0.0)
            pair = [kept, zero] if p == 0 else [zero, kept]
            spread.append(jnp.concatenate(pair, axis=2))
    wide = jnp.concatenate(spread, axis=1).reshape(count, 256)
    wide = jnp.where(own.astype(F32) > 0, wide, 0.0).astype(BF)

    @pl.when(at == 0)
    def _():
        acc_ref[...] = jnp.zeros_like(acc_ref)

    acc_ref[...] += dot_tn(jnp.concatenate([wide, own], axis=1), rows_ref[...])

    @pl.when(at == pl.num_programs(0) - 1)
    def _():
        enc_ref[...] = acc_ref[:256, :]
        dec_ref[...] = (mixed_ref[...] - acc_ref[256:, :]) * scale


def grads(scale, gates, msg, rows, mixed):
    sources, tall, lanes = msg.shape
    count = sources * 32
    cols = rows.shape[1]
    step = 512
    shape = jax.ShapeDtypeStruct(mixed.shape, F32)
    return pl.pallas_call(
        lambda *refs: grads_kernel(scale, *refs),
        grid=(count // step,),
        in_specs=[
            pl.BlockSpec((gates.shape[0], step // 32, 2 * CAP, 128), lambda i: (0, i, 0, 0)),
            pl.BlockSpec((step // 32, tall, lanes), lambda i: (i, 0, 0)),
            pl.BlockSpec((step, cols), lambda i: (i, 0)),
            pl.BlockSpec(mixed.shape, lambda i: (0, 0)),
        ],
        out_specs=[pl.BlockSpec(mixed.shape, lambda i: (0, 0))] * 2,
        out_shape=[shape, shape],
        scratch_shapes=[pltpu.VMEM((512, cols), F32)],
        compiler_params=params(),
        cost_estimate=cost(4 * count * cols * 256, 16 * 2**20),
        name="dictionary_grads",
    )(gates, msg, rows, mixed)


def body(resid, block_ids, enc_w, enc_b, dec_w, dec_b):
    tok_rows, width = resid.shape
    parts = lax.axis_size("dp")
    shards = lax.axis_size("dict")
    local = enc_w.shape[0]
    here = local // LAT
    slots = here * shards * CAP
    cols = width // parts
    everyone = ("dp", "dict")
    devices = parts * shards
    blocks = here * shards
    scale = (blocks / (tok_rows * devices * block_ids.shape[1])) ** 0.5
    at_x = lax.axis_index("dp")
    at_dict = lax.axis_index("dict")

    ids = block_ids.T
    outgoing = route(ids, resid, dec_b, parts, slots)
    arrived = lax.all_to_all(
        outgoing.reshape(devices, here * CAP, cols), everyone, 0, 0, tiled=True
    )

    enc_x = lax.dynamic_slice(enc_w, (0, at_x * cols), (local, cols))
    dec_x = lax.dynamic_slice(dec_w, (0, at_x * cols), (local, cols))
    bias_x = lax.dynamic_slice(dec_b, (at_x * cols,), (cols,)).reshape(1, cols)
    dec_all = lax.all_gather(dec_x, "dict", axis=0, tiled=True)

    weights = jnp.concatenate(
        [enc_x.reshape(2, 2 * LAT, cols), dec_x.reshape(2, 2 * LAT, cols)], axis=1
    )
    bias = jnp.where(at_x == 0, enc_b, 0.0).reshape(2, 2 * LAT)
    pre, proj = encode(arrived, weights, bias)
    partial = lax.all_to_all(pre, everyone, 0, 0, tiled=True)
    acts, msg = activate(ids, block_ids, partial.reshape(parts, shards * 2 * CAP, 128), shards)
    group_acts = lax.all_to_all(acts, "dp", 0, 0, tiled=True)
    message = lax.all_to_all(
        msg.reshape(devices, here * CAP + 16, 128), everyone, 0, 0, tiled=True
    )

    recon_x, gram = reconstruct(group_acts.reshape(parts * tok_rows, 256), dec_all, dec_x, bias_x)
    recon = lax.all_to_all(recon_x, "dp", 0, 0, tiled=True)

    own_gram = lax.dynamic_slice(gram, (at_dict * local, 0), (local, local))
    gate = gate_partial(scale, message, gram, own_gram, proj)
    gates = lax.all_gather(gate, "dp", axis=0, tiled=False)
    later, recon, gate = lax.optimization_barrier((message, recon, gate))
    mixed = mix(later, dec_all, dec_x)
    recon = recon.reshape(parts, tok_rows, cols).transpose(1, 0, 2).reshape(tok_rows, width)
    enc_grad, dec_grad = grads(
        scale, gates, message, arrived.reshape(devices * here * CAP, cols), mixed
    )
    return (recon, enc_grad, dec_grad)


def solution(mesh):
    placed = (
        P(("dp", "dict"), None),
        P(("dp", "dict"), None),
        P("dict", None),
        P("dict"),
        P("dict", None),
        P(),
    )
    return jax.shard_map(
        body,
        mesh=mesh,
        in_specs=placed,
        out_specs=(P(("dp", "dict"), None), P("dict", "dp"), P("dict", "dp")),
        check_vma=False,
    )
```

```python
import functools

import jax
import jax.numpy as jnp
from jax import lax
from jax.experimental import pallas as pl
from jax.experimental.pallas import tpu as pltpu
from jax.sharding import PartitionSpec as P

LAT = 64
CAP = 8
BF = jnp.bfloat16
F32 = jnp.float32
VMEM_LIMIT = 56 * 1024 * 1024


def params(**more):
    return pltpu.CompilerParams(vmem_limit_bytes=VMEM_LIMIT, **more)


def cost(flops, moved):
    return pl.CostEstimate(flops=int(flops), bytes_accessed=int(moved), transcendentals=0)


def dot(a, b):
    return jnp.dot(a, b, preferred_element_type=F32)


def dot_tn(a, b):
    return lax.dot_general(a, b, (((0,), (0,)), ((), ())), preferred_element_type=F32)


def dot_nt(a, b):
    return lax.dot_general(a, b, (((1,), (1,)), ((), ())), preferred_element_type=F32)


def iota(shape, axis):
    return lax.broadcasted_iota(jnp.int32, shape, axis)


def ranks(ids, blocks):
    rows = ids.shape[1]
    block = iota((blocks, rows), 0)
    one0 = (block == ids[0:1, :]).astype(F32)
    one1 = (block == ids[1:2, :]).astype(F32)
    before = (iota((rows, rows), 0) < iota((rows, rows), 1)).astype(BF)
    pre0 = dot(one0.astype(BF), before)
    pre1 = dot(one1.astype(BF), before) + jnp.sum(one0, axis=1, keepdims=True)
    rank0 = jnp.sum(one0 * pre0, axis=0, keepdims=True).astype(jnp.int32)
    rank1 = jnp.sum(one1 * pre1, axis=0, keepdims=True).astype(jnp.int32)
    return rank0, rank1


def slot_table(ids, shards, lanes=128):
    rows = ids.shape[1]
    found = jnp.zeros((shards, lanes), F32)
    for k, rank in enumerate(ranks(ids, shards * 4)):
        block = ids[k : k + 1, :]
        other = (ids[1 - k : 2 - k, :] + 1).astype(F32)
        target = jnp.where(iota((shards, rows), 0) == block // 4, other, 0.0).astype(BF)
        place = iota((lanes, rows), 0) == (block % 4) * CAP + rank
        found = found + dot_nt(target, jnp.where(place, 1.0, 0.0).astype(BF))
    return found - 1.0


def slot_names(table):
    sources = table.shape[0]
    shape = (sources, 32, 128)
    row = jnp.concatenate([table, table], axis=1).astype(F32)
    kept = jnp.where(iota(shape, 1) == iota(shape, 2), row, 0.0).astype(BF)
    return dot(kept.reshape(sources * 32, 128), jnp.ones((128, 128), BF)).astype(BF)


def route_kernel(ids_ref, resid_ref, bias_ref, out_ref, pick_ref):
    slots, rows = pick_ref.shape

    @pl.when(pl.program_id(0) == 0)
    def _():
        ids = ids_ref[...]
        rank0, rank1 = ranks(ids, slots // CAP)
        slot = iota((slots, rows), 0)
        is0 = slot == ids[0:1, :] * CAP + rank0
        is1 = slot == ids[1:2, :] * CAP + rank1
        pick_ref[...] = jnp.where(is0 | is1, 1.0, 0.0).astype(BF)

    centered = (resid_ref[...].astype(F32) - bias_ref[...]).astype(BF)
    step = 256
    for at in range(0, slots, step):
        out_ref[0, at : at + step, :] = dot(pick_ref[at : at + step, :], centered).astype(BF)


def route(ids, resid, dec_b, parts, slots):
    rows, width = resid.shape
    cols = width // parts
    return pl.pallas_call(
        route_kernel,
        grid=(parts,),
        in_specs=[
            pl.BlockSpec(ids.shape, lambda i: (0, 0)),
            pl.BlockSpec((rows, cols), lambda i: (0, i)),
            pl.BlockSpec((1, cols), lambda i: (0, i)),
        ],
        out_specs=pl.BlockSpec((1, slots, cols), lambda i: (i, 0, 0)),
        out_shape=jax.ShapeDtypeStruct((parts, slots, cols), BF),
        scratch_shapes=[pltpu.VMEM((slots, rows), BF)],
        compiler_params=params(),
        cost_estimate=cost(2 * slots * rows * width, 10 * 2**20),
        name="route_rows",
    )(ids, resid, dec_b.reshape(1, width))


def encode_kernel(scale, rows_ref, weight_ref, bias_ref, pre_ref, proj_ref):
    count, _, cols = rows_ref.shape
    projected = []
    low = iota((1, 1, 128), 2) < LAT
    for p in range(2):
        rows = rows_ref[:, p * 16 : (p + 1) * 16, :].reshape(count * 16, cols)
        both = dot_nt(rows, weight_ref[p]).reshape(count, 2, CAP, 256)
        pre = jnp.where(low, both[:, 0, :, :128], both[:, 1, :, :128])
        pre_ref[:, p * CAP : (p + 1) * CAP, :] = pre + bias_ref[p : p + 1, :][None]
        projected.append(jnp.where(low, both[:, 0, :, 128:], both[:, 1, :, 128:]) * scale)
    proj_ref[...] = jnp.concatenate(projected, axis=1).astype(BF)


def encode(scale, arrived, weights, bias):
    sources, here, cols = arrived.shape
    step = 32
    shape = (sources, 2 * CAP, 128)
    return pl.pallas_call(
        functools.partial(encode_kernel, scale),
        grid=(sources // step,),
        in_specs=[
            pl.BlockSpec((step, here, cols), lambda i: (i, 0, 0)),
            pl.BlockSpec(weights.shape, lambda i: (0, 0, 0)),
            pl.BlockSpec(bias.shape, lambda i: (0, 0)),
        ],
        out_specs=[pl.BlockSpec((step, 2 * CAP, 128), lambda i: (i, 0, 0))] * 2,
        out_shape=[jax.ShapeDtypeStruct(shape, F32), jax.ShapeDtypeStruct(shape, BF)],
        compiler_params=params(),
        cost_estimate=cost(2 * sources * here * cols * 256, 11 * 2**20),
        name="encode_rows",
    )(arrived, weights, bias)


def activate_kernel(ids_ref, pre_ref, group_ref, msg_ref):
    shards = msg_ref.shape[1]
    packed = pre_ref.shape[1]
    rows = ids_ref.shape[1]
    slots = 2 * packed
    ids = ids_ref[...]
    rank0, rank1 = ranks(ids, slots // CAP)
    total = pre_ref[0] + pre_ref[1] + pre_ref[2] + pre_ref[3]
    acts = jnp.maximum(total, 0.0).astype(BF)
    slot = iota((slots, rows), 0)
    found = []
    for k, rank in ((0, rank0), (1, rank1)):
        block = ids[k : k + 1, :]
        half = block % 2
        at = (block // 2) * CAP + rank
        here = jnp.where(slot == half * packed + at, 1.0, 0.0).astype(BF)
        found.append(dot_tn(here[:packed], acts)[:, :LAT] + dot_tn(here[packed:], acts)[:, LAT:])
    first, second = found
    straight = jnp.concatenate([first, second], axis=1).astype(BF)
    crossed = jnp.concatenate([second, first], axis=1).astype(BF)
    group_ref[:packed, :] = acts
    halves = [ids[:, :128], ids[:, 128:], jnp.zeros((12, 128), jnp.int32)]
    group_ref[packed:, :] = jnp.concatenate(halves, axis=0).astype(F32).astype(BF)
    pick0 = jnp.where(slot == ids[0:1, :] * CAP + rank0, 1.0, 0.0).astype(BF)
    pick1 = jnp.where(slot == ids[1:2, :] * CAP + rank1, 1.0, 0.0).astype(BF)
    msg = (dot(pick0, straight) + dot(pick1, crossed)).astype(BF)
    msg = msg.reshape(shards, slots // shards, 128)
    table = slot_table(ids, shards)
    table = jnp.broadcast_to(table[:, None, :], (shards, 16, 128)).astype(BF)
    for copy in range(msg_ref.shape[0]):
        msg_ref[copy, :, : slots // shards, :] = msg
        msg_ref[copy, :, slots // shards :, :] = table


def activate(ids, partial, shards):
    parts, packed, lanes = partial.shape
    rows = ids.shape[1]
    return pl.pallas_call(
        activate_kernel,
        out_shape=[
            jax.ShapeDtypeStruct((packed + 16, lanes), BF),
            jax.ShapeDtypeStruct((parts, shards, 2 * packed // shards + 16, lanes), BF),
        ],
        compiler_params=params(),
        cost_estimate=cost(8 * packed * rows * lanes, 3 * 2**20),
        name="activate_rows",
    )(ids, partial)


def doubled(pair):
    source, target = iota((128, 256), 0), iota((128, 256), 1)
    copy = source == (target // 128) * LAT + target % LAT
    return dot(pair, jnp.where(copy, 1.0, 0.0).astype(BF)).astype(BF)


def lane_block(group):
    return (iota((1, 128), 1) // LAT + group * 2).astype(F32).astype(BF)


def own_expanded(own):
    count = own.shape[0]
    twice = jnp.concatenate([own, own], axis=1)
    mine = (iota((count, 256), 0) // CAP) % 4 == iota((count, 256), 1) // LAT
    return jnp.where(mine, twice.astype(F32), 0.0).astype(BF)


def spread(packed):
    low = iota((1, 1, 128), 2) < LAT
    zero = jnp.zeros((packed.shape[0], CAP, 128), F32)
    rows = []
    for p in range(2):
        piece = packed[:, p * CAP : (p + 1) * CAP, :]
        for q in range(2):
            kept = jnp.where(low if q == 0 else ~low, piece, 0.0)
            rows.append(jnp.concatenate([kept, zero] if p == 0 else [zero, kept], axis=2))
    return jnp.concatenate(rows, axis=1).reshape(packed.shape[0] * 32, 256)


def gathered(wide):
    wide = wide.reshape(wide.shape[0] // 32, 4, CAP, 256)
    low = iota((1, 1, 128), 2) < LAT
    packed = []
    for p in range(2):
        lanes = slice(p * 128, (p + 1) * 128)
        packed.append(jnp.where(low, wide[:, 2 * p, :, lanes], wide[:, 2 * p + 1, :, lanes]))
    return jnp.concatenate(packed, axis=1)


def home_kernel(scale, *refs):
    group, (dec_ref, bias_ref, recon_ref, gate_ref, pick_ref, part_ref) = refs[:4], refs[4:]
    at = pl.program_id(0)
    steps = pl.num_programs(0) // 2
    slots, rows = pick_ref.shape[1:]
    packed = slots // 2
    per = dec_ref.shape[0] // 256

    @pl.when(at == 0)
    def _():
        slot = iota((slots, rows), 0)
        for d in range(4):
            halves = group[d][packed:, :].astype(F32).astype(jnp.int32)
            ids = jnp.concatenate([halves[0:2], halves[2:4]], axis=1)
            rank0, rank1 = ranks(ids, slots // CAP)
            here = (slot == ids[0:1, :] * CAP + rank0) | (slot == ids[1:2, :] * CAP + rank1)
            pick_ref[d] = jnp.where(here, 1.0, 0.0).astype(BF)

    @pl.when(at < steps)
    def _():
        for g in range(per):
            shard = at * per + g
            source = pl.ds(pl.multiple_of(shard * 16, 16), 16)
            target = pl.ds(pl.multiple_of(shard * 32, 32), 32)
            acts = jnp.stack([group[d][source, :].astype(F32) for d in range(4)])
            part = dot(spread(acts).astype(BF), dec_ref[g * 256 : (g + 1) * 256, :]).astype(BF)
            for d in range(4):
                part_ref[d, target, :] = part[d * 32 : (d + 1) * 32]

    @pl.when(at == steps)
    def _():
        for d in range(4):
            total = dot_tn(pick_ref[d], part_ref[d])
            recon_ref[d * rows : (d + 1) * rows, :] = (total + bias_ref[...]).astype(BF)
            part_ref[d] = dot(pick_ref[d], total.astype(BF)).astype(BF)

    @pl.when(at >= steps)
    def _():
        for g in range(per):
            shard = (at - steps) * per + g
            source = pl.ds(pl.multiple_of(shard * 32, 32), 32)
            total = jnp.concatenate([part_ref[d, source, :] for d in range(4)], axis=0)
            wide = dot_nt(total, dec_ref[g * 256 : (g + 1) * 256, :])
            gate_ref[:, pl.ds(pl.multiple_of(g * 16, 16), 16), :] = (gathered(wide) * scale).astype(BF)


def home(scale, group, dec_all, bias):
    latents, cols = dec_all.shape
    tall, lanes = group[0].shape
    packed = tall - 16
    rows = 256
    chunk = 1024
    steps = latents // chunk
    per = chunk // 256
    return pl.pallas_call(
        functools.partial(home_kernel, scale),
        grid=(2 * steps,),
        in_specs=[pl.BlockSpec((tall, lanes), lambda i: (0, 0))] * 4
        + [
            pl.BlockSpec((chunk, cols), lambda i: (i % steps, 0)),
            pl.BlockSpec((1, cols), lambda i: (0, 0)),
        ],
        out_specs=[
            pl.BlockSpec((4 * rows, cols), lambda i: (0, 0)),
            pl.BlockSpec((4, 16 * per, lanes), lambda i: (0, jnp.maximum(i - steps, 0), 0)),
        ],
        out_shape=[
            jax.ShapeDtypeStruct((4 * rows, cols), BF),
            jax.ShapeDtypeStruct((4, packed, lanes), BF),
        ],
        scratch_shapes=[
            pltpu.VMEM((4, 2 * packed, rows), BF),
            pltpu.VMEM((4, 2 * packed, cols), BF),
        ],
        compiler_params=params(),
        cost_estimate=cost(8 * latents * cols * 128, 36 * 2**20),
        name="home_rows",
    )(*group, dec_all, bias)


def mix_kernel(msg_ref, dec_ref, own_dec_ref, out_ref, own_ref, twice_ref, name_ref):
    at = pl.program_id(0)
    count = msg_ref.shape[0] * 32
    chunk = dec_ref.shape[0]

    @pl.when(at == 0)
    def _():
        twice = doubled(msg_ref[:, :32, :].reshape(count, 128))
        twice_ref[...] = twice[:, 128:]
        name_ref[...] = slot_names(msg_ref[:, 32:, :])
        own = own_expanded(twice[:, :128])
        own_ref[...] = own.T
        out_ref[...] = dot(dot(own_ref[...], own).astype(BF), own_dec_ref[...])

    zero = jnp.zeros((count, 128), BF)
    spread = []
    for q in range(chunk // 128):
        block = lane_block(at * (chunk // 128) + q)
        spread.append(jnp.where(name_ref[...] == block, twice_ref[...], zero))
    mixed = dot(own_ref[...], jnp.concatenate(spread, axis=1)).astype(BF)
    out_ref[...] += dot(mixed, dec_ref[...])


def mix(msg, dec_all, own_dec):
    count = msg.shape[0] * 32
    latents, cols = dec_all.shape
    chunk = 512
    return pl.pallas_call(
        mix_kernel,
        grid=(latents // chunk,),
        in_specs=[
            pl.BlockSpec(msg.shape, lambda i: (0, 0, 0)),
            pl.BlockSpec((chunk, cols), lambda i: (i, 0)),
            pl.BlockSpec(own_dec.shape, lambda i: (0, 0)),
        ],
        out_specs=pl.BlockSpec(own_dec.shape, lambda i: (0, 0)),
        out_shape=jax.ShapeDtypeStruct(own_dec.shape, F32),
        scratch_shapes=[
            pltpu.VMEM((256, count), BF),
            pltpu.VMEM((count, 128), BF),
            pltpu.VMEM((count, 128), BF),
        ],
        compiler_params=params(),
        cost_estimate=cost(2 * latents * 256 * (count + cols), 20 * 2**20),
        name="mix_decoder",
    )(msg, dec_all, own_dec)


def grads_kernel(scale, gate_ref, proj_ref, msg_ref, rows_ref, mixed_ref, enc_ref, dec_ref, acc_ref):
    at = pl.program_id(0)
    sources = msg_ref.shape[0]
    count = sources * 32
    own = own_expanded(doubled(msg_ref[:, :32, :].reshape(count, 128))[:, :128])
    total = gate_ref[...].astype(F32)
    for part in range(proj_ref.shape[0]):
        total = total - proj_ref[part].astype(F32)
    wide = jnp.where(own.astype(F32) > 0, spread(total), 0.0).astype(BF)

    @pl.when(at == 0)
    def _():
        acc_ref[...] = jnp.zeros_like(acc_ref)

    acc_ref[...] += dot_tn(jnp.concatenate([wide, own], axis=1), rows_ref[...])

    @pl.when(at == pl.num_programs(0) - 1)
    def _():
        enc_ref[...] = acc_ref[:256, :]
        dec_ref[...] = (mixed_ref[...] - acc_ref[256:, :]) * scale


def grads(scale, gate, proj, msg, rows, mixed):
    sources, tall, lanes = msg.shape
    count = sources * 32
    cols = rows.shape[1]
    step = 512
    shape = jax.ShapeDtypeStruct(mixed.shape, F32)
    return pl.pallas_call(
        lambda *refs: grads_kernel(scale, *refs),
        grid=(count // step,),
        in_specs=[
            pl.BlockSpec((step // 32, 2 * CAP, 128), lambda i: (i, 0, 0)),
            pl.BlockSpec((proj.shape[0], step // 32, 2 * CAP, 128), lambda i: (0, i, 0, 0)),
            pl.BlockSpec((step // 32, tall, lanes), lambda i: (i, 0, 0)),
            pl.BlockSpec((step, cols), lambda i: (i, 0)),
            pl.BlockSpec(mixed.shape, lambda i: (0, 0)),
        ],
        out_specs=[pl.BlockSpec(mixed.shape, lambda i: (0, 0))] * 2,
        out_shape=[shape, shape],
        scratch_shapes=[pltpu.VMEM((512, cols), F32)],
        compiler_params=params(),
        cost_estimate=cost(4 * count * cols * 256, 16 * 2**20),
        name="dictionary_grads",
    )(gate, proj, msg, rows, mixed)


def shifted(value, by, parts):
    if by == 0:
        return value
    return lax.ppermute(value, "dp", [(i, (i + by) % parts) for i in range(parts)])


def body(resid, block_ids, enc_w, enc_b, dec_w, dec_b):
    tok_rows, width = resid.shape
    parts = lax.axis_size("dp")
    shards = lax.axis_size("dict")
    local = enc_w.shape[0]
    here = local // LAT
    slots = here * shards * CAP
    cols = width // parts
    everyone = ("dp", "dict")
    devices = parts * shards
    blocks = here * shards
    scale = (blocks / (tok_rows * devices * block_ids.shape[1])) ** 0.5
    at_x = lax.axis_index("dp")

    ids = block_ids.T
    outgoing = route(ids, resid, dec_b, parts, slots)
    arrived = lax.all_to_all(
        outgoing.reshape(devices, here * CAP, cols), everyone, 0, 0, tiled=True
    )

    enc_x = lax.dynamic_slice(enc_w, (0, at_x * cols), (local, cols))
    dec_x = lax.dynamic_slice(dec_w, (0, at_x * cols), (local, cols))
    bias_x = lax.dynamic_slice(dec_b, (at_x * cols,), (cols,)).reshape(1, cols)
    dec_all = lax.all_gather(dec_x, "dict", axis=0, tiled=True)

    weights = jnp.concatenate(
        [enc_x.reshape(2, 2 * LAT, cols), dec_x.reshape(2, 2 * LAT, cols)], axis=1
    )
    bias = jnp.where(at_x == 0, enc_b, 0.0).reshape(2, 2 * LAT)
    pre, proj = encode(scale, arrived, weights, bias)
    partial = lax.all_to_all(pre, everyone, 0, 0, tiled=True)
    projs = lax.all_gather(proj, "dp", axis=0, tiled=False)
    acts, msg = activate(ids, partial.reshape(parts, shards * 2 * CAP, 128), shards)
    group = [shifted(acts, d, parts) for d in range(parts)]
    message = lax.all_to_all(
        msg.reshape(devices, here * CAP + 16, 128), everyone, 0, 0, tiled=True
    )

    recon_x, gate = home(scale, group, dec_all, bias_x)
    total = gate[0].astype(F32)
    for d in range(1, parts):
        total = total + shifted(gate[d], -d, parts).astype(F32)
    total = total.astype(BF).reshape(1, shards, 2 * CAP, 128)
    total = jnp.broadcast_to(total, (parts, shards, 2 * CAP, 128))
    gates = lax.all_to_all(total.reshape(devices, 2 * CAP, 128), everyone, 0, 0, tiled=True)

    recon = jnp.zeros((tok_rows, width), BF)
    for d in range(parts):
        piece = shifted(recon_x[d * tok_rows : (d + 1) * tok_rows], -d, parts)
        recon = lax.dynamic_update_slice(recon, piece, (0, ((at_x + d) % parts) * cols))

    mixed = mix(message, dec_all, dec_x)
    enc_grad, dec_grad = grads(
        scale, gates, projs, message, arrived.reshape(devices * here * CAP, cols), mixed
    )
    return (recon, enc_grad, dec_grad)


def solution(mesh):
    placed = (
        P(("dp", "dict"), None),
        P(("dp", "dict"), None),
        P("dict", None),
        P("dict"),
        P("dict", None),
        P(),
    )
    return jax.shard_map(
        body,
        mesh=mesh,
        in_specs=placed,
        out_specs=(P(("dp", "dict"), None), P("dict", "dp"), P("dict", "dp")),
        check_vma=False,
    )
```

```python
import functools

import jax
import jax.numpy as jnp
from jax import lax
from jax.experimental import pallas as pl
from jax.experimental.pallas import tpu as pltpu
from jax.sharding import PartitionSpec as P

LAT = 64
CAP = 8
BF = jnp.bfloat16
F32 = jnp.float32
PIECES = 4
VMEM_LIMIT = 56 * 1024 * 1024


def params(**more):
    return pltpu.CompilerParams(vmem_limit_bytes=VMEM_LIMIT, **more)


def cost(flops, moved):
    return pl.CostEstimate(flops=int(flops), bytes_accessed=int(moved), transcendentals=0)


def dot(a, b):
    return jnp.dot(a, b, preferred_element_type=F32)


def dot_tn(a, b):
    return lax.dot_general(a, b, (((0,), (0,)), ((), ())), preferred_element_type=F32)


def dot_nt(a, b):
    return lax.dot_general(a, b, (((1,), (1,)), ((), ())), preferred_element_type=F32)


def iota(shape, axis):
    return lax.broadcasted_iota(jnp.int32, shape, axis)


def ranks(ids, blocks):
    rows = ids.shape[1]
    block = iota((blocks, rows), 0)
    one0 = (block == ids[0:1, :]).astype(F32)
    one1 = (block == ids[1:2, :]).astype(F32)
    before = (iota((rows, rows), 0) < iota((rows, rows), 1)).astype(BF)
    pre0 = dot(one0.astype(BF), before)
    pre1 = dot(one1.astype(BF), before) + jnp.sum(one0, axis=1, keepdims=True)
    rank0 = jnp.sum(one0 * pre0, axis=0, keepdims=True).astype(jnp.int32)
    rank1 = jnp.sum(one1 * pre1, axis=0, keepdims=True).astype(jnp.int32)
    return rank0, rank1


def slot_table(ids, shards, lanes=128):
    rows = ids.shape[1]
    found = jnp.zeros((shards, lanes), F32)
    for k, rank in enumerate(ranks(ids, shards * 4)):
        block = ids[k : k + 1, :]
        other = (ids[1 - k : 2 - k, :] + 1).astype(F32)
        target = jnp.where(iota((shards, rows), 0) == block // 4, other, 0.0).astype(BF)
        place = iota((lanes, rows), 0) == (block % 4) * CAP + rank
        found = found + dot_nt(target, jnp.where(place, 1.0, 0.0).astype(BF))
    return found - 1.0


def slot_names(table):
    sources = table.shape[0]
    shape = (sources, 32, 128)
    row = jnp.concatenate([table, table], axis=1).astype(F32)
    kept = jnp.where(iota(shape, 1) == iota(shape, 2), row, 0.0).astype(BF)
    return dot(kept.reshape(sources * 32, 128), jnp.ones((128, 128), BF)).astype(BF)


def route_kernel(ids_ref, resid_ref, bias_ref, out_ref, pick_ref):
    slots, rows = pick_ref.shape

    @pl.when(pl.program_id(0) == 0)
    def _():
        ids = ids_ref[...]
        rank0, rank1 = ranks(ids, slots // CAP)
        slot = iota((slots, rows), 0)
        is0 = slot == ids[0:1, :] * CAP + rank0
        is1 = slot == ids[1:2, :] * CAP + rank1
        pick_ref[...] = jnp.where(is0 | is1, 1.0, 0.0).astype(BF)

    centered = (resid_ref[...].astype(F32) - bias_ref[...]).astype(BF)
    step = 256
    for at in range(0, slots, step):
        out_ref[0, at : at + step, :] = dot(pick_ref[at : at + step, :], centered).astype(BF)


def route(ids, resid, dec_b, parts, slots):
    rows, width = resid.shape
    cols = width // parts
    return pl.pallas_call(
        route_kernel,
        grid=(parts,),
        in_specs=[
            pl.BlockSpec(ids.shape, lambda i: (0, 0)),
            pl.BlockSpec((rows, cols), lambda i: (0, i)),
            pl.BlockSpec((1, cols), lambda i: (0, i)),
        ],
        out_specs=pl.BlockSpec((1, slots, cols), lambda i: (i, 0, 0)),
        out_shape=jax.ShapeDtypeStruct((parts, slots, cols), BF),
        scratch_shapes=[pltpu.VMEM((slots, rows), BF)],
        compiler_params=params(),
        cost_estimate=cost(2 * slots * rows * width, 10 * 2**20),
        name="route_rows",
    )(ids, resid, dec_b.reshape(1, width))


def encode_kernel(scale, rows_hbm, weight_ref, bias_ref, pre_ref, proj_ref, rows_ref, sems):
    pieces = sems.shape[0]
    sources, _, cols = rows_ref.shape
    count = sources // pieces
    low = iota((1, 1, 128), 2) < LAT

    def fetch(piece):
        at = pl.ds(piece * count, count)
        return pltpu.make_async_copy(rows_hbm.at[at], rows_ref.at[at], sems.at[piece])

    for piece in range(pieces):
        fetch(piece).start()
    for piece in range(pieces):
        fetch(piece).wait()
        here = slice(piece * count, (piece + 1) * count)
        projected = []
        for p in range(2):
            rows = rows_ref[here, p * 16 : (p + 1) * 16, :].reshape(count * 16, cols)
            both = dot(rows, weight_ref[p]).reshape(count, 2, CAP, 256)
            pre = jnp.where(low, both[:, 0, :, :128], both[:, 1, :, :128])
            pre_ref[here, p * CAP : (p + 1) * CAP, :] = pre + bias_ref[p : p + 1, :][None]
            projected.append(jnp.where(low, both[:, 0, :, 128:], both[:, 1, :, 128:]) * scale)
        proj_ref[here] = jnp.concatenate(projected, axis=1).astype(BF)


def encode(scale, arrived, weights, bias):
    sources, here, cols = arrived.shape
    shape = (sources, 2 * CAP, 128)
    vmem = pl.BlockSpec(memory_space=pltpu.VMEM)
    return pl.pallas_call(
        functools.partial(encode_kernel, scale),
        in_specs=[pl.BlockSpec(memory_space=pl.ANY), vmem, vmem],
        out_specs=[vmem, vmem],
        out_shape=[jax.ShapeDtypeStruct(shape, F32), jax.ShapeDtypeStruct(shape, BF)],
        scratch_shapes=[pltpu.VMEM(arrived.shape, BF), pltpu.SemaphoreType.DMA((PIECES,))],
        compiler_params=params(),
        cost_estimate=cost(2 * sources * here * cols * 256, 11 * 2**20),
        name="encode_rows",
    )(arrived, weights, bias)


def activate_kernel(ids_ref, pre_ref, group_ref, msg_ref):
    shards = msg_ref.shape[1]
    packed = pre_ref.shape[1]
    rows = ids_ref.shape[1]
    slots = 2 * packed
    ids = ids_ref[...]
    rank0, rank1 = ranks(ids, slots // CAP)
    total = pre_ref[0] + pre_ref[1] + pre_ref[2] + pre_ref[3]
    acts = jnp.maximum(total, 0.0).astype(BF)
    slot = iota((slots, rows), 0)
    found = []
    for k, rank in ((0, rank0), (1, rank1)):
        block = ids[k : k + 1, :]
        half = block % 2
        at = (block // 2) * CAP + rank
        here = jnp.where(slot == half * packed + at, 1.0, 0.0).astype(BF)
        found.append(dot_tn(here[:packed], acts)[:, :LAT] + dot_tn(here[packed:], acts)[:, LAT:])
    first, second = found
    straight = jnp.concatenate([first, second], axis=1).astype(BF)
    crossed = jnp.concatenate([second, first], axis=1).astype(BF)
    group_ref[:packed, :] = acts
    halves = [ids[:, :128], ids[:, 128:], jnp.zeros((12, 128), jnp.int32)]
    group_ref[packed:, :] = jnp.concatenate(halves, axis=0).astype(F32).astype(BF)
    pick0 = jnp.where(slot == ids[0:1, :] * CAP + rank0, 1.0, 0.0).astype(BF)
    pick1 = jnp.where(slot == ids[1:2, :] * CAP + rank1, 1.0, 0.0).astype(BF)
    msg = (dot(pick0, straight) + dot(pick1, crossed)).astype(BF)
    msg = msg.reshape(shards, slots // shards, 128)
    table = slot_table(ids, shards)
    table = jnp.broadcast_to(table[:, None, :], (shards, 16, 128)).astype(BF)
    for copy in range(msg_ref.shape[0]):
        msg_ref[copy, :, : slots // shards, :] = msg
        msg_ref[copy, :, slots // shards :, :] = table


def activate(ids, partial, shards):
    parts, packed, lanes = partial.shape
    rows = ids.shape[1]
    return pl.pallas_call(
        activate_kernel,
        out_shape=[
            jax.ShapeDtypeStruct((packed + 16, lanes), BF),
            jax.ShapeDtypeStruct((parts, shards, 2 * packed // shards + 16, lanes), BF),
        ],
        compiler_params=params(),
        cost_estimate=cost(8 * packed * rows * lanes, 3 * 2**20),
        name="activate_rows",
    )(ids, partial)


def doubled(pair):
    source, target = iota((128, 256), 0), iota((128, 256), 1)
    copy = source == (target // 128) * LAT + target % LAT
    return dot(pair, jnp.where(copy, 1.0, 0.0).astype(BF)).astype(BF)


def lane_block(group):
    return (iota((1, 128), 1) // LAT + group * 2).astype(F32).astype(BF)


def own_expanded(own):
    count = own.shape[0]
    twice = jnp.concatenate([own, own], axis=1)
    mine = (iota((count, 256), 0) // CAP) % 4 == iota((count, 256), 1) // LAT
    return jnp.where(mine, twice.astype(F32), 0.0).astype(BF)


def spread(packed):
    low = iota((1, 1, 128), 2) < LAT
    zero = jnp.zeros((packed.shape[0], CAP, 128), F32)
    rows = []
    for p in range(2):
        piece = packed[:, p * CAP : (p + 1) * CAP, :]
        for q in range(2):
            kept = jnp.where(low if q == 0 else ~low, piece, 0.0)
            rows.append(jnp.concatenate([kept, zero] if p == 0 else [zero, kept], axis=2))
    return jnp.concatenate(rows, axis=1).reshape(packed.shape[0] * 32, 256)


def gathered(wide):
    wide = wide.reshape(wide.shape[0] // 32, 4, CAP, 256)
    low = iota((1, 1, 128), 2) < LAT
    packed = []
    for p in range(2):
        lanes = slice(p * 128, (p + 1) * 128)
        packed.append(jnp.where(low, wide[:, 2 * p, :, lanes], wide[:, 2 * p + 1, :, lanes]))
    return jnp.concatenate(packed, axis=1)


def home_kernel(scale, parts, *refs):
    group, (dec_hbm, bias_ref), refs = refs[:parts], refs[parts : parts + 2], refs[parts + 2 :]
    recon, gates, (pick_ref, part_ref, dec_ref, sems) = refs[:parts], refs[parts : 2 * parts], refs[2 * parts :]
    slots, rows = pick_ref.shape[1:]
    packed = slots // 2
    pieces = sems.shape[0]
    tall = dec_ref.shape[0] // pieces
    per = tall // 256

    def fetch(piece):
        at = pl.ds(pl.multiple_of(piece * tall, tall), tall)
        return pltpu.make_async_copy(dec_hbm.at[at], dec_ref.at[at], sems.at[piece])

    for piece in range(pieces):
        fetch(piece).start()

    slot = iota((slots, rows), 0)
    for d in range(parts):
        halves = group[d][packed:, :].astype(F32).astype(jnp.int32)
        ids = jnp.concatenate([halves[0:2], halves[2:4]], axis=1)
        rank0, rank1 = ranks(ids, slots // CAP)
        here = (slot == ids[0:1, :] * CAP + rank0) | (slot == ids[1:2, :] * CAP + rank1)
        pick_ref[d] = jnp.where(here, 1.0, 0.0).astype(BF)

    def aligned(start, size):
        return pl.ds(pl.multiple_of(start * size, size), size)

    @pl.loop(0, pieces)
    def _(piece):
        fetch(piece).wait()
        for g in range(per):
            shard = piece * per + g
            acts = jnp.stack([group[d][aligned(shard, 16), :].astype(F32) for d in range(parts)])
            part = dot(spread(acts).astype(BF), dec_ref[aligned(shard, 256), :]).astype(BF)
            for d in range(parts):
                part_ref[d, aligned(shard, 32), :] = part[d * 32 : (d + 1) * 32]

    for d in range(parts):
        total = dot_tn(pick_ref[d], part_ref[d])
        recon[d][...] = (total + bias_ref[...]).astype(BF)
        part_ref[d] = dot(pick_ref[d], total.astype(BF)).astype(BF)

    @pl.loop(0, pieces)
    def _(piece):
        for g in range(per):
            shard = piece * per + g
            total = jnp.concatenate([part_ref[d, aligned(shard, 32), :] for d in range(parts)], axis=0)
            wide = dot_nt(total, dec_ref[aligned(shard, 256), :])
            gate = (gathered(wide) * scale).astype(BF)
            for d in range(parts):
                gates[d][aligned(shard, 16), :] = gate[d]


def home(scale, group, dec_all, bias):
    latents, cols = dec_all.shape
    tall, lanes = group[0].shape
    parts = len(group)
    packed = tall - 16
    rows = 256
    vmem = pl.BlockSpec(memory_space=pltpu.VMEM)
    return pl.pallas_call(
        functools.partial(home_kernel, scale, parts),
        in_specs=[vmem] * parts + [pl.BlockSpec(memory_space=pl.ANY), vmem],
        out_specs=[vmem] * (2 * parts),
        out_shape=[jax.ShapeDtypeStruct((rows, cols), BF)] * parts
        + [jax.ShapeDtypeStruct((packed, lanes), BF)] * parts,
        scratch_shapes=[
            pltpu.VMEM((parts, 2 * packed, rows), BF),
            pltpu.VMEM((parts, 2 * packed, cols), BF),
            pltpu.VMEM((latents, cols), BF),
            pltpu.SemaphoreType.DMA((8,)),
        ],
        compiler_params=params(),
        cost_estimate=cost(8 * latents * cols * 128, 20 * 2**20),
        name="home_rows",
    )(*group, dec_all, bias)


def assemble_kernel(at_ref, *refs):
    pieces, out, sems = refs[:-2], refs[-2], refs[-1]
    cols = pieces[0].shape[1]
    copies = []
    for d, piece in enumerate(pieces):
        place = pl.multiple_of(((at_ref[0] + d) % len(pieces)) * cols, cols)
        copies.append(pltpu.make_async_copy(piece, out.at[:, pl.ds(place, cols)], sems.at[d]))
    for copy in copies:
        copy.start()
    for copy in copies:
        copy.wait()


def assemble(at, pieces):
    rows, cols = pieces[0].shape
    return pl.pallas_call(
        assemble_kernel,
        in_specs=[pl.BlockSpec(memory_space=pltpu.SMEM)]
        + [pl.BlockSpec(memory_space=pltpu.VMEM)] * len(pieces),
        out_specs=pl.BlockSpec(memory_space=pl.ANY),
        out_shape=jax.ShapeDtypeStruct((rows, cols * len(pieces)), BF),
        scratch_shapes=[pltpu.SemaphoreType.DMA((len(pieces),))],
        compiler_params=params(),
        cost_estimate=cost(0, 2**22),
        name="assemble_recon",
    )(at.astype(jnp.int32).reshape(1), *pieces)


def mix_kernel(msg_ref, dec_ref, own_dec_ref, out_ref, own_ref, twice_ref, name_ref):
    at = pl.program_id(0)
    sources = msg_ref.shape[0]
    count = sources * 32
    chunk = dec_ref.shape[0]

    @pl.when(at == 0)
    def _():
        twice = doubled(msg_ref[:, :32, :].reshape(count, 128)).astype(F32).reshape(sources, 4, CAP, 256)
        name = slot_names(msg_ref[:, 32:, :]).astype(F32).reshape(sources, 4, CAP, 128)
        for b in range(4):
            rows = twice[:, b].reshape(sources * CAP, 256).astype(BF)
            name_ref[b] = name[:, b].reshape(sources * CAP, 128).astype(BF)
            twice_ref[b] = rows[:, 128:]
            own = rows[:, :128].T[:LAT]
            own_ref[b] = own
            mixed = dot(own, rows[:, :128])[:, :LAT].astype(BF)
            here = slice(b * LAT, (b + 1) * LAT)
            out_ref[here, :] = dot(mixed, own_dec_ref[here, :])

    zero = jnp.zeros((sources * CAP, 128), BF)
    mixed = []
    for b in range(4):
        wide = []
        for q in range(chunk // 128):
            block = lane_block(at * (chunk // 128) + q)
            wide.append(jnp.where(name_ref[b] == block, twice_ref[b], zero))
        mixed.append(dot(own_ref[b], jnp.concatenate(wide, axis=1)).astype(BF))
    out_ref[...] += dot(jnp.concatenate(mixed, axis=0), dec_ref[...])


def mix(msg, dec_all, own_dec):
    per = msg.shape[0] * CAP
    count = 4 * per
    latents, cols = dec_all.shape
    chunk = 1024
    return pl.pallas_call(
        mix_kernel,
        grid=(latents // chunk,),
        in_specs=[
            pl.BlockSpec(msg.shape, lambda i: (0, 0, 0)),
            pl.BlockSpec((chunk, cols), lambda i: (i, 0)),
            pl.BlockSpec(own_dec.shape, lambda i: (0, 0)),
        ],
        out_specs=pl.BlockSpec(own_dec.shape, lambda i: (0, 0)),
        out_shape=jax.ShapeDtypeStruct(own_dec.shape, F32),
        scratch_shapes=[
            pltpu.VMEM((4, LAT, per), BF),
            pltpu.VMEM((4, per, 128), BF),
            pltpu.VMEM((4, per, 128), BF),
        ],
        compiler_params=params(),
        cost_estimate=cost(2 * latents * 256 * (count + cols), 20 * 2**20),
        name="mix_decoder",
    )(msg, dec_all, own_dec)


def grads_kernel(
    scale, gate_hbm, proj_hbm, msg_hbm, rows_hbm, mixed_hbm, enc_ref, dec_ref,
    gate_ref, proj_ref, msg_ref, rows_ref, mixed_ref, acc_ref, sems, last
):
    pieces = sems.shape[0]
    sources = msg_ref.shape[0] // pieces
    count = sources * 32

    def fetch(piece):
        at = pl.ds(piece * sources, sources)
        tall = pl.ds(piece * count, count)
        return [
            pltpu.make_async_copy(msg_hbm.at[at], msg_ref.at[at], sems.at[piece, 0]),
            pltpu.make_async_copy(gate_hbm.at[at], gate_ref.at[at], sems.at[piece, 1]),
            pltpu.make_async_copy(proj_hbm.at[:, at], proj_ref.at[:, at], sems.at[piece, 2]),
            pltpu.make_async_copy(rows_hbm.at[tall], rows_ref.at[tall], sems.at[piece, 3]),
        ]

    mixed_copy = pltpu.make_async_copy(mixed_hbm, mixed_ref, last)
    for piece in range(pieces):
        for copy in fetch(piece):
            copy.start()
    mixed_copy.start()
    for piece in range(pieces):
        for copy in fetch(piece):
            copy.wait()
        here = slice(piece * sources, (piece + 1) * sources)
        own = own_expanded(doubled(msg_ref[here, :32, :].reshape(count, 128))[:, :128])
        total = gate_ref[here].astype(F32)
        for part in range(proj_ref.shape[0]):
            total = total - proj_ref[part, here].astype(F32)
        wide = jnp.where(own.astype(F32) > 0, spread(total), 0.0).astype(BF)
        both = jnp.concatenate([wide, own], axis=1)
        more = dot_tn(both, rows_ref[piece * count : (piece + 1) * count, :])
        if piece == 0:
            acc_ref[...] = more
        elif piece < pieces - 1:
            acc_ref[...] += more
        else:
            more = acc_ref[...] + more
            enc_ref[...] = more[:256, :]
            mixed_copy.wait()
            dec_ref[...] = (mixed_ref[...] - more[256:, :]) * scale


def grads(scale, gate, proj, msg, rows, mixed):
    cols = rows.shape[1]
    shape = jax.ShapeDtypeStruct(mixed.shape, F32)
    vmem = pl.BlockSpec(memory_space=pltpu.VMEM)
    arrays = (gate, proj, msg, rows, mixed)
    return pl.pallas_call(
        functools.partial(grads_kernel, scale),
        in_specs=[pl.BlockSpec(memory_space=pl.ANY)] * len(arrays),
        out_specs=[vmem, vmem],
        out_shape=[shape, shape],
        scratch_shapes=[pltpu.VMEM(array.shape, array.dtype) for array in arrays]
        + [
            pltpu.VMEM((512, cols), F32),
            pltpu.SemaphoreType.DMA((PIECES, 4)),
            pltpu.SemaphoreType.DMA,
        ],
        compiler_params=params(),
        cost_estimate=cost(4 * msg.shape[0] * 32 * cols * 256, 16 * 2**20),
        name="dictionary_grads",
    )(*arrays)


def shifted(value, by, parts):
    if by == 0:
        return value
    return lax.ppermute(value, "dp", [(i, (i + by) % parts) for i in range(parts)])


def body(resid, block_ids, enc_w, enc_b, dec_w, dec_b):
    tok_rows, width = resid.shape
    parts = lax.axis_size("dp")
    shards = lax.axis_size("dict")
    local = enc_w.shape[0]
    here = local // LAT
    slots = here * shards * CAP
    cols = width // parts
    everyone = ("dp", "dict")
    devices = parts * shards
    blocks = here * shards
    scale = (blocks / (tok_rows * devices * block_ids.shape[1])) ** 0.5
    at_x = lax.axis_index("dp")

    ids = block_ids.T
    outgoing = route(ids, resid, dec_b, parts, slots)
    arrived = lax.all_to_all(
        outgoing.reshape(devices, here * CAP, cols), everyone, 0, 0, tiled=True
    )

    enc_x = lax.dynamic_slice(enc_w, (0, at_x * cols), (local, cols))
    dec_x = lax.dynamic_slice(dec_w, (0, at_x * cols), (local, cols))
    bias_x = lax.dynamic_slice(dec_b, (at_x * cols,), (cols,)).reshape(1, cols)
    dec_all = lax.all_gather(dec_x, "dict", axis=0, tiled=True)

    weights = jnp.concatenate(
        [enc_x.reshape(2, 2 * LAT, cols), dec_x.reshape(2, 2 * LAT, cols)], axis=1
    ).transpose(0, 2, 1)
    bias = jnp.where(at_x == 0, enc_b, 0.0).reshape(2, 2 * LAT)
    pre, proj = encode(scale, arrived, weights, bias)
    partial = lax.all_to_all(pre, everyone, 0, 0, tiled=True)
    projs = lax.all_gather(proj, "dp", axis=0, tiled=False)
    acts, msg = activate(ids, partial.reshape(parts, shards * 2 * CAP, 128), shards)
    group = [shifted(acts, d, parts) for d in range(parts)]
    message = lax.all_to_all(
        msg.reshape(devices, here * CAP + 16, 128), everyone, 0, 0, tiled=True
    )

    made = home(scale, group, dec_all, bias_x)
    total = made[parts].astype(F32)
    for d in range(1, parts):
        total = total + shifted(made[parts + d], -d, parts).astype(F32)
    total = total.astype(BF).reshape(1, shards, 2 * CAP, 128)
    total = jnp.broadcast_to(total, (parts, shards, 2 * CAP, 128))
    gates = lax.all_to_all(total.reshape(devices, 2 * CAP, 128), everyone, 0, 0, tiled=True)
    recon = assemble(at_x, [shifted(made[d], -d, parts) for d in range(parts)])

    mixed = mix(message, dec_all, dec_x)
    enc_grad, dec_grad = grads(
        scale, gates, projs, message, arrived.reshape(devices * here * CAP, cols), mixed
    )
    return (recon, enc_grad, dec_grad)


def solution(mesh):
    placed = (
        P(("dp", "dict"), None),
        P(("dp", "dict"), None),
        P("dict", None),
        P("dict"),
        P("dict", None),
        P(),
    )
    return jax.shard_map(
        body,
        mesh=mesh,
        in_specs=placed,
        out_specs=(P(("dp", "dict"), None), P("dict", "dp"), P("dict", "dp")),
        check_vma=False,
    )
```

```python
import functools

import jax
import jax.numpy as jnp
from jax import lax
from jax.experimental import pallas as pl
from jax.experimental.pallas import tpu as pltpu
from jax.sharding import PartitionSpec as P

LAT = 64
CAP = 8
BF = jnp.bfloat16
F32 = jnp.float32
PIECES = 4
VMEM_LIMIT = 56 * 1024 * 1024


def params(**more):
    return pltpu.CompilerParams(vmem_limit_bytes=VMEM_LIMIT, **more)


def cost(flops, moved):
    return pl.CostEstimate(flops=int(flops), bytes_accessed=int(moved), transcendentals=0)


def dot(a, b):
    return jnp.dot(a, b, preferred_element_type=F32)


def dot_tn(a, b):
    return lax.dot_general(a, b, (((0,), (0,)), ((), ())), preferred_element_type=F32)


def dot_nt(a, b):
    return lax.dot_general(a, b, (((1,), (1,)), ((), ())), preferred_element_type=F32)


def iota(shape, axis):
    return lax.broadcasted_iota(jnp.int32, shape, axis)


def ranks(ids, blocks):
    rows = ids.shape[1]
    block = iota((blocks, rows), 0)
    one0 = (block == ids[0:1, :]).astype(F32)
    one1 = (block == ids[1:2, :]).astype(F32)
    before = (iota((rows, rows), 0) < iota((rows, rows), 1)).astype(BF)
    pre0 = dot(one0.astype(BF), before)
    pre1 = dot(one1.astype(BF), before) + jnp.sum(one0, axis=1, keepdims=True)
    rank0 = jnp.sum(one0 * pre0, axis=0, keepdims=True).astype(jnp.int32)
    rank1 = jnp.sum(one1 * pre1, axis=0, keepdims=True).astype(jnp.int32)
    return rank0, rank1


def slot_table(ids, shards, lanes=128):
    rows = ids.shape[1]
    found = jnp.zeros((shards, lanes), F32)
    for k, rank in enumerate(ranks(ids, shards * 4)):
        block = ids[k : k + 1, :]
        other = (ids[1 - k : 2 - k, :] + 1).astype(F32)
        target = jnp.where(iota((shards, rows), 0) == block // 4, other, 0.0).astype(BF)
        place = iota((lanes, rows), 0) == (block % 4) * CAP + rank
        found = found + dot_nt(target, jnp.where(place, 1.0, 0.0).astype(BF))
    return found - 1.0


def slot_names(table):
    sources = table.shape[0]
    shape = (sources, 32, 128)
    row = jnp.concatenate([table, table], axis=1).astype(F32)
    kept = jnp.where(iota(shape, 1) == iota(shape, 2), row, 0.0).astype(BF)
    return dot(kept.reshape(sources * 32, 128), jnp.ones((128, 128), BF)).astype(BF)


def route_kernel(ids_ref, resid_ref, bias_ref, out_ref, pick_ref):
    slots, rows = pick_ref.shape

    @pl.when(pl.program_id(0) == 0)
    def _():
        ids = ids_ref[...]
        rank0, rank1 = ranks(ids, slots // CAP)
        slot = iota((slots, rows), 0)
        is0 = slot == ids[0:1, :] * CAP + rank0
        is1 = slot == ids[1:2, :] * CAP + rank1
        pick_ref[...] = jnp.where(is0 | is1, 1.0, 0.0).astype(BF)

    centered = (resid_ref[...].astype(F32) - bias_ref[...]).astype(BF)
    step = 256
    for at in range(0, slots, step):
        out_ref[0, at : at + step, :] = dot(pick_ref[at : at + step, :], centered).astype(BF)


def route(ids, resid, dec_b, parts, slots):
    rows, width = resid.shape
    cols = width // parts
    return pl.pallas_call(
        route_kernel,
        grid=(parts,),
        in_specs=[
            pl.BlockSpec(ids.shape, lambda i: (0, 0)),
            pl.BlockSpec((rows, cols), lambda i: (0, i)),
            pl.BlockSpec((1, cols), lambda i: (0, i)),
        ],
        out_specs=pl.BlockSpec((1, slots, cols), lambda i: (i, 0, 0)),
        out_shape=jax.ShapeDtypeStruct((parts, slots, cols), BF),
        scratch_shapes=[pltpu.VMEM((slots, rows), BF)],
        compiler_params=params(),
        cost_estimate=cost(2 * slots * rows * width, 10 * 2**20),
        name="route_rows",
    )(ids, resid, dec_b.reshape(1, width))


def encode_kernel(scale, rows_hbm, weight_ref, bias_ref, pre_ref, proj_ref, rows_ref, sems):
    pieces = sems.shape[0]
    sources, _, cols = rows_ref.shape
    count = sources // pieces
    low = iota((1, 1, 128), 2) < LAT

    def fetch(piece):
        at = pl.ds(piece * count, count)
        return pltpu.make_async_copy(rows_hbm.at[at], rows_ref.at[at], sems.at[piece])

    for piece in range(pieces):
        fetch(piece).start()
    for piece in range(pieces):
        fetch(piece).wait()
        here = slice(piece * count, (piece + 1) * count)
        projected = []
        for p in range(2):
            rows = rows_ref[here, p * 16 : (p + 1) * 16, :].reshape(count * 16, cols)
            both = dot(rows, weight_ref[p]).reshape(count, 2, CAP, 256)
            pre = jnp.where(low, both[:, 0, :, :128], both[:, 1, :, :128])
            pre_ref[here, p * CAP : (p + 1) * CAP, :] = pre + bias_ref[p : p + 1, :][None]
            projected.append(jnp.where(low, both[:, 0, :, 128:], both[:, 1, :, 128:]) * scale)
        proj_ref[here] = jnp.concatenate(projected, axis=1).astype(BF)


def encode(scale, arrived, weights, bias):
    sources, here, cols = arrived.shape
    shape = (sources, 2 * CAP, 128)
    vmem = pl.BlockSpec(memory_space=pltpu.VMEM)
    return pl.pallas_call(
        functools.partial(encode_kernel, scale),
        in_specs=[pl.BlockSpec(memory_space=pl.ANY), vmem, vmem],
        out_specs=[vmem, vmem],
        out_shape=[jax.ShapeDtypeStruct(shape, F32), jax.ShapeDtypeStruct(shape, BF)],
        scratch_shapes=[pltpu.VMEM(arrived.shape, BF), pltpu.SemaphoreType.DMA((PIECES,))],
        compiler_params=params(),
        cost_estimate=cost(2 * sources * here * cols * 256, 11 * 2**20),
        name="encode_rows",
    )(arrived, weights, bias)


def activate_kernel(ids_ref, pre_ref, group_ref, msg_ref):
    shards = msg_ref.shape[1]
    packed = pre_ref.shape[1]
    rows = ids_ref.shape[1]
    slots = 2 * packed
    ids = ids_ref[...]
    rank0, rank1 = ranks(ids, slots // CAP)
    total = pre_ref[0] + pre_ref[1] + pre_ref[2] + pre_ref[3]
    acts = jnp.maximum(total, 0.0).astype(BF)
    slot = iota((slots, rows), 0)
    found = []
    for k, rank in ((0, rank0), (1, rank1)):
        block = ids[k : k + 1, :]
        half = block % 2
        at = (block // 2) * CAP + rank
        here = jnp.where(slot == half * packed + at, 1.0, 0.0).astype(BF)
        found.append(dot_tn(here[:packed], acts)[:, :LAT] + dot_tn(here[packed:], acts)[:, LAT:])
    first, second = found
    straight = jnp.concatenate([first, second], axis=1).astype(BF)
    crossed = jnp.concatenate([second, first], axis=1).astype(BF)
    group_ref[:packed, :] = acts
    halves = [ids[:, :128], ids[:, 128:], jnp.zeros((12, 128), jnp.int32)]
    group_ref[packed:, :] = jnp.concatenate(halves, axis=0).astype(F32).astype(BF)
    pick0 = jnp.where(slot == ids[0:1, :] * CAP + rank0, 1.0, 0.0).astype(BF)
    pick1 = jnp.where(slot == ids[1:2, :] * CAP + rank1, 1.0, 0.0).astype(BF)
    msg = (dot(pick0, straight) + dot(pick1, crossed)).astype(BF)
    msg = msg.reshape(shards, slots // shards, 128)
    table = slot_table(ids, shards)
    table = jnp.broadcast_to(table[:, None, :], (shards, 16, 128)).astype(BF)
    for copy in range(msg_ref.shape[0]):
        msg_ref[copy, :, : slots // shards, :] = msg
        msg_ref[copy, :, slots // shards :, :] = table


def activate(ids, partial, shards):
    parts, packed, lanes = partial.shape
    rows = ids.shape[1]
    return pl.pallas_call(
        activate_kernel,
        out_shape=[
            jax.ShapeDtypeStruct((packed + 16, lanes), BF),
            jax.ShapeDtypeStruct((parts, shards, 2 * packed // shards + 16, lanes), BF),
        ],
        compiler_params=params(),
        cost_estimate=cost(8 * packed * rows * lanes, 3 * 2**20),
        name="activate_rows",
    )(ids, partial)


def doubled(pair):
    source, target = iota((128, 256), 0), iota((128, 256), 1)
    copy = source == (target // 128) * LAT + target % LAT
    return dot(pair, jnp.where(copy, 1.0, 0.0).astype(BF)).astype(BF)


def lane_block(group):
    return (iota((1, 128), 1) // LAT + group * 2).astype(F32).astype(BF)


def own_expanded(own):
    count = own.shape[0]
    twice = jnp.concatenate([own, own], axis=1)
    mine = (iota((count, 256), 0) // CAP) % 4 == iota((count, 256), 1) // LAT
    return jnp.where(mine, twice.astype(F32), 0.0).astype(BF)


def spread(packed):
    low = iota((1, 1, 128), 2) < LAT
    zero = jnp.zeros((packed.shape[0], CAP, 128), F32)
    rows = []
    for p in range(2):
        piece = packed[:, p * CAP : (p + 1) * CAP, :]
        for q in range(2):
            kept = jnp.where(low if q == 0 else ~low, piece, 0.0)
            rows.append(jnp.concatenate([kept, zero] if p == 0 else [zero, kept], axis=2))
    return jnp.concatenate(rows, axis=1).reshape(packed.shape[0] * 32, 256)


def gathered(wide):
    wide = wide.reshape(wide.shape[0] // 32, 4, CAP, 256)
    low = iota((1, 1, 128), 2) < LAT
    packed = []
    for p in range(2):
        lanes = slice(p * 128, (p + 1) * 128)
        packed.append(jnp.where(low, wide[:, 2 * p, :, lanes], wide[:, 2 * p + 1, :, lanes]))
    return jnp.concatenate(packed, axis=1)


def home_kernel(scale, parts, *refs):
    group, (place_ref, dec_hbm, bias_ref), refs = refs[:parts], refs[parts : parts + 3], refs[parts + 3 :]
    recon, gates, (pick_ref, part_ref, dec_ref, sems) = refs[:parts], refs[parts : 2 * parts], refs[2 * parts :]
    slots, rows = pick_ref.shape[1:]
    packed = slots // 2
    pieces = sems.shape[0]
    tall = dec_ref.shape[0] // pieces
    per = tall // 256

    def fetch(piece):
        at = pl.ds(pl.multiple_of(piece * tall, tall), tall)
        return pltpu.make_async_copy(dec_hbm.at[at], dec_ref.at[at], sems.at[piece])

    for piece in range(pieces):
        fetch(piece).start()

    slot = iota((slots, rows), 0)
    for d in range(parts):
        halves = group[d][packed:, :].astype(F32).astype(jnp.int32)
        ids = jnp.concatenate([halves[0:2], halves[2:4]], axis=1)
        rank0, rank1 = ranks(ids, slots // CAP)
        here = (slot == ids[0:1, :] * CAP + rank0) | (slot == ids[1:2, :] * CAP + rank1)
        pick_ref[d] = jnp.where(here, 1.0, 0.0).astype(BF)

    def aligned(start, size):
        return pl.ds(pl.multiple_of(start * size, size), size)

    @pl.loop(0, pieces)
    def _(piece):
        fetch(piece).wait()
        for g in range(per):
            shard = piece * per + g
            acts = jnp.stack([group[d][aligned(shard, 16), :].astype(F32) for d in range(parts)])
            part = dot(spread(acts).astype(BF), dec_ref[aligned(shard, 256), :]).astype(BF)
            for d in range(parts):
                part_ref[d, aligned(shard, 32), :] = part[d * 32 : (d + 1) * 32]

    bias = bias_ref[pl.ds(place_ref[0], 1), :]
    for d in range(parts):
        total = dot_tn(pick_ref[d], part_ref[d])
        recon[d][...] = (total + bias).astype(BF)
        part_ref[d] = dot(pick_ref[d], total.astype(BF)).astype(BF)

    @pl.loop(0, pieces)
    def _(piece):
        for g in range(per):
            shard = piece * per + g
            total = jnp.concatenate([part_ref[d, aligned(shard, 32), :] for d in range(parts)], axis=0)
            wide = dot_nt(total, dec_ref[aligned(shard, 256), :])
            gate = (gathered(wide) * scale).astype(BF)
            for d in range(parts):
                gates[d][aligned(shard, 16), :] = gate[d]


def home(scale, place, group, dec_all, bias):
    latents, cols = dec_all.shape
    tall, lanes = group[0].shape
    parts = len(group)
    packed = tall - 16
    rows = 256
    vmem = pl.BlockSpec(memory_space=pltpu.VMEM)
    return pl.pallas_call(
        functools.partial(home_kernel, scale, parts),
        in_specs=[vmem] * parts
        + [pl.BlockSpec(memory_space=pltpu.SMEM), pl.BlockSpec(memory_space=pl.ANY), vmem],
        out_specs=[vmem] * (2 * parts),
        out_shape=[jax.ShapeDtypeStruct((rows, cols), BF)] * parts
        + [jax.ShapeDtypeStruct((packed, lanes), BF)] * parts,
        scratch_shapes=[
            pltpu.VMEM((parts, 2 * packed, rows), BF),
            pltpu.VMEM((parts, 2 * packed, cols), BF),
            pltpu.VMEM((latents, cols), BF),
            pltpu.SemaphoreType.DMA((8,)),
        ],
        compiler_params=params(),
        cost_estimate=cost(8 * latents * cols * 128, 20 * 2**20),
        name="home_rows",
    )(*group, place, dec_all, bias)


def assemble_kernel(at_ref, *refs):
    pieces, out, sems = refs[:-2], refs[-2], refs[-1]
    cols = pieces[0].shape[1]
    copies = []
    for d, piece in enumerate(pieces):
        place = pl.multiple_of(((at_ref[0] + d) % len(pieces)) * cols, cols)
        copies.append(pltpu.make_async_copy(piece, out.at[:, pl.ds(place, cols)], sems.at[d]))
    for copy in copies:
        copy.start()
    for copy in copies:
        copy.wait()


def assemble(at, pieces):
    rows, cols = pieces[0].shape
    return pl.pallas_call(
        assemble_kernel,
        in_specs=[pl.BlockSpec(memory_space=pltpu.SMEM)]
        + [pl.BlockSpec(memory_space=pltpu.VMEM)] * len(pieces),
        out_specs=pl.BlockSpec(memory_space=pl.ANY),
        out_shape=jax.ShapeDtypeStruct((rows, cols * len(pieces)), BF),
        scratch_shapes=[pltpu.SemaphoreType.DMA((len(pieces),))],
        compiler_params=params(),
        cost_estimate=cost(0, 2**22),
        name="assemble_recon",
    )(at.astype(jnp.int32).reshape(1), *pieces)


def sum_kernel(*refs):
    out_ref = refs[-1]
    total = refs[0][...].astype(F32)
    for ref in refs[1:-1]:
        total = total + ref[...].astype(F32)
    for copy in range(out_ref.shape[0]):
        out_ref[copy] = total.astype(BF)


def summed(pieces, copies):
    return pl.pallas_call(
        sum_kernel,
        out_shape=jax.ShapeDtypeStruct((copies, *pieces[0].shape), BF),
        compiler_params=params(),
        cost_estimate=cost(0, 2**20),
        name="sum_pieces",
    )(*pieces)


def mix_kernel(msg_ref, dec_hbm, start_ref, out_ref, own_ref, other_ref, name_ref, dec_ref, sems):
    sources = msg_ref.shape[0]
    count = sources * 32
    steps = sems.shape[0]
    quarter = dec_ref.shape[0] // 4
    tall = quarter // steps

    def fetch(step, q):
        at = pl.ds(q * quarter + step * tall, tall)
        return pltpu.make_async_copy(dec_hbm.at[at], dec_ref.at[at], sems.at[step, q])

    for step in range(steps):
        for q in range(4):
            fetch(step, q).start()

    twice = doubled(msg_ref[:, :32, :].reshape(count, 128)).astype(F32).reshape(sources, 4, CAP, 256)
    block = slot_names(msg_ref[:, 32:, :]).astype(F32).reshape(sources, 4, CAP, 128)
    for b in range(4):
        rows = twice[:, b].reshape(sources * CAP, 256)
        other_ref[b] = rows[:, 128:].astype(BF)
        name = block[:, b].reshape(sources * CAP, 128)
        within = jnp.floor(name * (1.0 / 32.0))
        name_ref[b] = (name - 32.0 * within).astype(BF)
        wide = jnp.concatenate([rows[:, :128]] * 2, axis=1)
        lane = (iota((1, 256), 1) // LAT).astype(F32)
        own_ref[b] = jnp.where(jnp.concatenate([within] * 2, axis=1) == lane, wide, 0.0).astype(BF).T
        own = rows[:, :128].astype(BF)
        here = slice(b * LAT, (b + 1) * LAT)
        out_ref[here, :] = dot(dot_tn(own, own)[:LAT, :LAT].astype(BF), start_ref[here, :])

    zero = jnp.zeros((sources * CAP, 128), BF)
    for step in range(steps):
        mixed = []
        for b in range(4):
            wide = []
            for pair in range(tall // 128):
                name = iota((1, 128), 1) // LAT + 2 * pair + step * (tall // LAT)
                wide.append(jnp.where(name_ref[b] == name.astype(F32).astype(BF), other_ref[b], zero))
            mixed.append(dot(own_ref[b], jnp.concatenate(wide, axis=1)).astype(BF))
        total = out_ref[...]
        for q in range(4):
            fetch(step, q).wait()
            left = jnp.concatenate([mixed[b][q * LAT : (q + 1) * LAT] for b in range(4)], axis=0)
            start = q * quarter + step * tall
            total = total + dot(left, dec_ref[start : start + tall, :])
        out_ref[...] = total


def mix(msg, dec_all, own_dec):
    latents, cols = dec_all.shape
    per = msg.shape[0] * CAP
    vmem = pl.BlockSpec(memory_space=pltpu.VMEM)
    return pl.pallas_call(
        mix_kernel,
        in_specs=[vmem, pl.BlockSpec(memory_space=pl.ANY), vmem],
        out_specs=vmem,
        out_shape=jax.ShapeDtypeStruct(own_dec.shape, F32),
        scratch_shapes=[
            pltpu.VMEM((4, 4 * LAT, per), BF),
            pltpu.VMEM((4, per, 128), BF),
            pltpu.VMEM((4, per, 128), BF),
            pltpu.VMEM(dec_all.shape, BF),
            pltpu.SemaphoreType.DMA((4, 4)),
        ],
        compiler_params=params(),
        cost_estimate=cost(2 * latents * 256 * (per + cols), 20 * 2**20),
        name="mix_decoder",
    )(msg, dec_all, own_dec)


def grads_kernel(
    scale, gate_hbm, proj_hbm, msg_hbm, rows_hbm, mixed_hbm, enc_ref, dec_ref,
    gate_ref, proj_ref, msg_ref, rows_ref, mixed_ref, acc_ref, sems, last
):
    parts = proj_hbm.shape[0]
    sources = msg_ref.shape[0] // parts
    count = sources * 32
    cols = rows_ref.shape[1]

    def fetch(part):
        at = pl.ds(part * sources, sources)
        tall = pl.ds(part * count, count)
        return [
            pltpu.make_async_copy(msg_hbm.at[at], msg_ref.at[at], sems.at[part, 0]),
            pltpu.make_async_copy(gate_hbm.at[at], gate_ref.at[at], sems.at[part, 1]),
            pltpu.make_async_copy(proj_hbm.at[:, at], proj_ref.at[:, at], sems.at[part, 2]),
            pltpu.make_async_copy(rows_hbm.at[tall], rows_ref.at[tall], sems.at[part, 3]),
        ]

    mixed_copy = pltpu.make_async_copy(mixed_hbm, mixed_ref, last)
    for part in range(parts):
        for copy in fetch(part):
            copy.start()
    mixed_copy.start()
    for part in range(parts):
        for copy in fetch(part):
            copy.wait()
        here = slice(part * sources, (part + 1) * sources)
        own = own_expanded(doubled(msg_ref[here, :32, :].reshape(count, 128))[:, :128])
        total = gate_ref[here].astype(F32)
        for other in range(parts):
            total = total - proj_ref[other, here].astype(F32)
        wide = jnp.where(own.astype(F32) > 0, spread(total), 0.0).astype(BF)
        both = jnp.concatenate([wide, own], axis=1)
        more = dot_tn(both, rows_ref[part * count : (part + 1) * count, :])
        if part == 0:
            acc_ref[...] = more
        elif part < parts - 1:
            acc_ref[...] += more
        else:
            more = acc_ref[...] + more
            enc_ref[...] = more[:256, :]
            mixed_copy.wait()
            dec_ref[...] = (mixed_ref[...] - more[256:, :]) * scale


def grads(scale, gate, proj, msg, rows, mixed):
    cols = rows.shape[1]
    shape = jax.ShapeDtypeStruct(mixed.shape, F32)
    vmem = pl.BlockSpec(memory_space=pltpu.VMEM)
    arrays = (gate, proj, msg, rows, mixed)
    return pl.pallas_call(
        functools.partial(grads_kernel, scale),
        in_specs=[pl.BlockSpec(memory_space=pl.ANY)] * len(arrays),
        out_specs=[vmem, vmem],
        out_shape=[shape, shape],
        scratch_shapes=[pltpu.VMEM(array.shape, array.dtype) for array in arrays]
        + [
            pltpu.VMEM((512, cols), F32),
            pltpu.SemaphoreType.DMA((proj.shape[0], 4)),
            pltpu.SemaphoreType.DMA,
        ],
        compiler_params=params(),
        cost_estimate=cost(4 * msg.shape[0] * 32 * cols * 256, 16 * 2**20),
        name="dictionary_grads",
    )(*arrays)


def shifted(value, by, parts):
    if by == 0:
        return value
    return lax.ppermute(value, "dp", [(i, (i + by) % parts) for i in range(parts)])


def body(resid, block_ids, enc_w, enc_b, dec_w, dec_b):
    tok_rows, width = resid.shape
    parts = lax.axis_size("dp")
    shards = lax.axis_size("dict")
    local = enc_w.shape[0]
    here = local // LAT
    slots = here * shards * CAP
    cols = width // parts
    everyone = ("dp", "dict")
    devices = parts * shards
    blocks = here * shards
    scale = (blocks / (tok_rows * devices * block_ids.shape[1])) ** 0.5
    at_x = lax.axis_index("dp")

    ids = block_ids.T
    outgoing = route(ids, resid, dec_b, parts, slots)
    arrived = lax.all_to_all(
        outgoing.reshape(devices, here * CAP, cols), everyone, 0, 0, tiled=True
    )

    enc_x = lax.dynamic_slice(enc_w, (0, at_x * cols), (local, cols))
    dec_x = lax.dynamic_slice(dec_w, (0, at_x * cols), (local, cols))
    dec_all = lax.all_gather(dec_x, "dict", axis=0, tiled=True)

    weights = jnp.concatenate(
        [enc_x.reshape(2, 2 * LAT, cols), dec_x.reshape(2, 2 * LAT, cols)], axis=1
    ).transpose(0, 2, 1)
    bias = jnp.where(at_x == 0, enc_b, 0.0).reshape(2, 2 * LAT)
    pre, proj = encode(scale, arrived, weights, bias)
    partial = lax.all_to_all(pre, everyone, 0, 0, tiled=True)
    projs = lax.all_gather(proj, "dp", axis=0, tiled=False)
    acts, msg = activate(ids, partial.reshape(parts, shards * 2 * CAP, 128), shards)
    group = [shifted(acts, d, parts) for d in range(parts)]
    msg, *group = lax.optimization_barrier((msg, *group))
    message = lax.all_to_all(
        msg.reshape(devices, here * CAP + 16, 128), everyone, 0, 0, tiled=True
    )

    place = at_x.astype(jnp.int32).reshape(1)
    made = home(scale, place, group, dec_all, dec_b.reshape(parts, cols))
    total = summed([shifted(made[parts + d], -d, parts) for d in range(parts)], parts)
    gates = lax.all_to_all(total.reshape(devices, 2 * CAP, 128), everyone, 0, 0, tiled=True)
    recon = assemble(at_x, [shifted(made[d], -d, parts) for d in range(parts)])
    mixed = mix(message, dec_all, dec_x)
    enc_grad, dec_grad = grads(
        scale, gates, projs, message, arrived.reshape(devices * here * CAP, cols), mixed
    )
    return (recon, enc_grad, dec_grad)


def solution(mesh):
    placed = (
        P(("dp", "dict"), None),
        P(("dp", "dict"), None),
        P("dict", None),
        P("dict"),
        P("dict", None),
        P(),
    )
    return jax.shard_map(
        body,
        mesh=mesh,
        in_specs=placed,
        out_specs=(P(("dp", "dict"), None), P("dict", "dp"), P("dict", "dp")),
        check_vma=False,
    )
```

```python
import functools

import jax
import jax.numpy as jnp
from jax import lax
from jax.experimental import pallas as pl
from jax.experimental.pallas import tpu as pltpu
from jax.sharding import PartitionSpec as P

LAT = 64
CAP = 8
BF = jnp.bfloat16
F32 = jnp.float32
PIECES = 4
VMEM_LIMIT = 56 * 1024 * 1024


def params(**more):
    return pltpu.CompilerParams(vmem_limit_bytes=VMEM_LIMIT, **more)


def cost(flops, moved):
    return pl.CostEstimate(flops=int(flops), bytes_accessed=int(moved), transcendentals=0)


def dot(a, b):
    return jnp.dot(a, b, preferred_element_type=F32)


def dot_tn(a, b):
    return lax.dot_general(a, b, (((0,), (0,)), ((), ())), preferred_element_type=F32)


def dot_nt(a, b):
    return lax.dot_general(a, b, (((1,), (1,)), ((), ())), preferred_element_type=F32)


def iota(shape, axis):
    return lax.broadcasted_iota(jnp.int32, shape, axis)


def ranks(ids, blocks):
    rows = ids.shape[1]
    block = iota((blocks, rows), 0)
    one0 = (block == ids[0:1, :]).astype(F32)
    one1 = (block == ids[1:2, :]).astype(F32)
    before = (iota((rows, rows), 0) < iota((rows, rows), 1)).astype(BF)
    pre0 = dot(one0.astype(BF), before)
    pre1 = dot(one1.astype(BF), before) + jnp.sum(one0, axis=1, keepdims=True)
    rank0 = jnp.sum(one0 * pre0, axis=0, keepdims=True).astype(jnp.int32)
    rank1 = jnp.sum(one1 * pre1, axis=0, keepdims=True).astype(jnp.int32)
    return rank0, rank1


def slot_table(ids, shards, lanes=128):
    rows = ids.shape[1]
    found = jnp.zeros((shards, lanes), F32)
    for k, rank in enumerate(ranks(ids, shards * 4)):
        block = ids[k : k + 1, :]
        other = (ids[1 - k : 2 - k, :] + 1).astype(F32)
        target = jnp.where(iota((shards, rows), 0) == block // 4, other, 0.0).astype(BF)
        place = iota((lanes, rows), 0) == (block % 4) * CAP + rank
        found = found + dot_nt(target, jnp.where(place, 1.0, 0.0).astype(BF))
    return found - 1.0


def slot_names(table):
    sources = table.shape[0]
    shape = (sources, 32, 128)
    row = jnp.concatenate([table, table], axis=1).astype(F32)
    kept = jnp.where(iota(shape, 1) == iota(shape, 2), row, 0.0).astype(BF)
    return dot(kept.reshape(sources * 32, 128), jnp.ones((128, 128), BF)).astype(BF)


def route_kernel(ids_ref, resid_ref, bias_ref, out_hbm, pick_ref, out_ref, sems):
    parts, slots, cols = out_ref.shape
    rows = pick_ref.shape[1]
    ids = ids_ref[...]
    rank0, rank1 = ranks(ids, slots // CAP)
    slot = iota((slots, rows), 0)
    is0 = slot == ids[0:1, :] * CAP + rank0
    is1 = slot == ids[1:2, :] * CAP + rank1
    pick_ref[...] = jnp.where(is0 | is1, 1.0, 0.0).astype(BF)
    pieces = sems.shape[1]
    tall = slots // pieces

    def send(part, piece):
        at = pl.ds(piece * tall, tall)
        return pltpu.make_async_copy(out_ref.at[part, at], out_hbm.at[part, at], sems.at[part, piece])

    for part in range(parts):
        here = slice(part * cols, (part + 1) * cols)
        centered = (resid_ref[:, here].astype(F32) - bias_ref[:, here]).astype(BF)
        for piece in range(pieces):
            at = slice(piece * tall, (piece + 1) * tall)
            out_ref[part, at, :] = dot(pick_ref[at, :], centered).astype(BF)
            send(part, piece).start()
    for part in range(parts):
        for piece in range(pieces):
            send(part, piece).wait()


def route(ids, resid, dec_b, parts, slots):
    rows, width = resid.shape
    cols = width // parts
    vmem = pl.BlockSpec(memory_space=pltpu.VMEM)
    return pl.pallas_call(
        route_kernel,
        in_specs=[vmem] * 3,
        out_specs=pl.BlockSpec(memory_space=pl.ANY),
        out_shape=jax.ShapeDtypeStruct((parts, slots, cols), BF),
        scratch_shapes=[
            pltpu.VMEM((slots, rows), BF),
            pltpu.VMEM((parts, slots, cols), BF),
            pltpu.SemaphoreType.DMA((parts, 4)),
        ],
        compiler_params=params(),
        cost_estimate=cost(2 * slots * rows * width, 10 * 2**20),
        name="route_rows",
    )(ids, resid, dec_b.reshape(1, width))


def encode_kernel(scale, rows_hbm, weight_ref, bias_ref, pre_ref, proj_ref, rows_ref, sems):
    pieces = sems.shape[0]
    sources, _, cols = rows_ref.shape
    count = sources // pieces
    low = iota((1, 1, 128), 2) < LAT

    def fetch(piece):
        at = pl.ds(piece * count, count)
        return pltpu.make_async_copy(rows_hbm.at[at], rows_ref.at[at], sems.at[piece])

    for piece in range(pieces):
        fetch(piece).start()
    for piece in range(pieces):
        fetch(piece).wait()
        here = slice(piece * count, (piece + 1) * count)
        projected = []
        for p in range(2):
            rows = rows_ref[here, p * 16 : (p + 1) * 16, :].reshape(count * 16, cols)
            both = dot(rows, weight_ref[p]).reshape(count, 2, CAP, 256)
            pre = jnp.where(low, both[:, 0, :, :128], both[:, 1, :, :128])
            pre_ref[here, p * CAP : (p + 1) * CAP, :] = pre + bias_ref[p : p + 1, :][None]
            projected.append(jnp.where(low, both[:, 0, :, 128:], both[:, 1, :, 128:]) * scale)
        proj_ref[here] = jnp.concatenate(projected, axis=1).astype(BF)


def encode(scale, arrived, weights, bias):
    sources, here, cols = arrived.shape
    shape = (sources, 2 * CAP, 128)
    vmem = pl.BlockSpec(memory_space=pltpu.VMEM)
    return pl.pallas_call(
        functools.partial(encode_kernel, scale),
        in_specs=[pl.BlockSpec(memory_space=pl.ANY), vmem, vmem],
        out_specs=[vmem, vmem],
        out_shape=[jax.ShapeDtypeStruct(shape, F32), jax.ShapeDtypeStruct(shape, BF)],
        scratch_shapes=[pltpu.VMEM(arrived.shape, BF), pltpu.SemaphoreType.DMA((PIECES,))],
        compiler_params=params(),
        cost_estimate=cost(2 * sources * here * cols * 256, 11 * 2**20),
        name="encode_rows",
    )(arrived, weights, bias)


def activate_kernel(ids_ref, pre_ref, group_ref):
    packed = pre_ref.shape[1]
    ids = ids_ref[...]
    total = pre_ref[0] + pre_ref[1] + pre_ref[2] + pre_ref[3]
    group_ref[:packed, :] = jnp.maximum(total, 0.0).astype(BF)
    halves = [ids[:, :128], ids[:, 128:], jnp.zeros((12, 128), jnp.int32)]
    group_ref[packed:, :] = jnp.concatenate(halves, axis=0).astype(F32).astype(BF)


def activate(ids, partial):
    parts, packed, lanes = partial.shape
    return pl.pallas_call(
        activate_kernel,
        out_shape=jax.ShapeDtypeStruct((packed + 16, lanes), BF),
        compiler_params=params(),
        cost_estimate=cost(4 * packed * lanes, 2**20),
        name="activate_slots",
    )(ids, partial)


def message_kernel(ids_ref, acts_ref, msg_ref):
    shards = msg_ref.shape[1]
    packed = acts_ref.shape[0] - 16
    rows = ids_ref.shape[1]
    slots = 2 * packed
    ids = ids_ref[...]
    rank0, rank1 = ranks(ids, slots // CAP)
    acts = acts_ref[:packed, :]
    slot = iota((slots, rows), 0)
    found = []
    for k, rank in ((0, rank0), (1, rank1)):
        block = ids[k : k + 1, :]
        half = block % 2
        at = (block // 2) * CAP + rank
        here = jnp.where(slot == half * packed + at, 1.0, 0.0).astype(BF)
        found.append(dot_tn(here[:packed], acts)[:, :LAT] + dot_tn(here[packed:], acts)[:, LAT:])
    first, second = found
    straight = jnp.concatenate([first, second], axis=1).astype(BF)
    crossed = jnp.concatenate([second, first], axis=1).astype(BF)
    pick0 = jnp.where(slot == ids[0:1, :] * CAP + rank0, 1.0, 0.0).astype(BF)
    pick1 = jnp.where(slot == ids[1:2, :] * CAP + rank1, 1.0, 0.0).astype(BF)
    msg = (dot(pick0, straight) + dot(pick1, crossed)).astype(BF)
    msg = msg.reshape(shards, slots // shards, 128)
    table = slot_table(ids, shards)
    table = jnp.broadcast_to(table[:, None, :], (shards, 16, 128)).astype(BF)
    for copy in range(msg_ref.shape[0]):
        msg_ref[copy, :, : slots // shards, :] = msg
        msg_ref[copy, :, slots // shards :, :] = table


def messages(ids, acts, parts, shards):
    tall, lanes = acts.shape
    slots = 2 * (tall - 16)
    return pl.pallas_call(
        message_kernel,
        out_shape=jax.ShapeDtypeStruct((parts, shards, slots // shards + 16, lanes), BF),
        compiler_params=params(),
        cost_estimate=cost(8 * slots * ids.shape[1] * lanes, 2**21),
        name="make_messages",
    )(ids, acts)


def doubled(pair):
    source, target = iota((128, 256), 0), iota((128, 256), 1)
    copy = source == (target // 128) * LAT + target % LAT
    return dot(pair, jnp.where(copy, 1.0, 0.0).astype(BF)).astype(BF)


def lane_block(group):
    return (iota((1, 128), 1) // LAT + group * 2).astype(F32).astype(BF)


def own_expanded(own):
    count = own.shape[0]
    twice = jnp.concatenate([own, own], axis=1)
    mine = (iota((count, 256), 0) // CAP) % 4 == iota((count, 256), 1) // LAT
    return jnp.where(mine, twice.astype(F32), 0.0).astype(BF)


def spread(packed):
    low = iota((1, 1, 128), 2) < LAT
    zero = jnp.zeros((packed.shape[0], CAP, 128), F32)
    rows = []
    for p in range(2):
        piece = packed[:, p * CAP : (p + 1) * CAP, :]
        for q in range(2):
            kept = jnp.where(low if q == 0 else ~low, piece, 0.0)
            rows.append(jnp.concatenate([kept, zero] if p == 0 else [zero, kept], axis=2))
    return jnp.concatenate(rows, axis=1).reshape(packed.shape[0] * 32, 256)


def gathered(wide):
    wide = wide.reshape(wide.shape[0] // 32, 4, CAP, 256)
    low = iota((1, 1, 128), 2) < LAT
    packed = []
    for p in range(2):
        lanes = slice(p * 128, (p + 1) * 128)
        packed.append(jnp.where(low, wide[:, 2 * p, :, lanes], wide[:, 2 * p + 1, :, lanes]))
    return jnp.concatenate(packed, axis=1)


def home_kernel(scale, parts, *refs):
    group, (place_ref, dec_hbm, bias_ref), refs = refs[:parts], refs[parts : parts + 3], refs[parts + 3 :]
    recon, gates, (pick_ref, part_ref, dec_ref, sems) = refs[:parts], refs[parts : 2 * parts], refs[2 * parts :]
    slots, rows = pick_ref.shape[1:]
    packed = slots // 2
    pieces = sems.shape[0]
    tall = dec_ref.shape[0] // pieces
    per = tall // 256

    def fetch(piece):
        at = pl.ds(pl.multiple_of(piece * tall, tall), tall)
        return pltpu.make_async_copy(dec_hbm.at[at], dec_ref.at[at], sems.at[piece])

    for piece in range(pieces):
        fetch(piece).start()

    slot = iota((slots, rows), 0)
    for d in range(parts):
        halves = group[d][packed:, :].astype(F32).astype(jnp.int32)
        ids = jnp.concatenate([halves[0:2], halves[2:4]], axis=1)
        rank0, rank1 = ranks(ids, slots // CAP)
        here = (slot == ids[0:1, :] * CAP + rank0) | (slot == ids[1:2, :] * CAP + rank1)
        pick_ref[d] = jnp.where(here, 1.0, 0.0).astype(BF)

    def aligned(start, size):
        return pl.ds(pl.multiple_of(start * size, size), size)

    @pl.loop(0, pieces)
    def _(piece):
        fetch(piece).wait()
        for g in range(per):
            shard = piece * per + g
            acts = jnp.stack([group[d][aligned(shard, 16), :].astype(F32) for d in range(parts)])
            part = dot(spread(acts).astype(BF), dec_ref[aligned(shard, 256), :]).astype(BF)
            for d in range(parts):
                part_ref[d, aligned(shard, 32), :] = part[d * 32 : (d + 1) * 32]

    bias = bias_ref[pl.ds(place_ref[0], 1), :]
    for d in range(parts):
        total = dot_tn(pick_ref[d], part_ref[d])
        recon[d][...] = (total + bias).astype(BF)
        part_ref[d] = dot(pick_ref[d], total.astype(BF)).astype(BF)

    @pl.loop(0, pieces)
    def _(piece):
        for g in range(per):
            shard = piece * per + g
            total = jnp.concatenate([part_ref[d, aligned(shard, 32), :] for d in range(parts)], axis=0)
            wide = dot_nt(total, dec_ref[aligned(shard, 256), :])
            gate = (gathered(wide) * scale).astype(BF)
            for d in range(parts):
                gates[d][aligned(shard, 16), :] = gate[d]


def home(scale, place, group, dec_all, bias):
    latents, cols = dec_all.shape
    tall, lanes = group[0].shape
    parts = len(group)
    packed = tall - 16
    rows = 256
    vmem = pl.BlockSpec(memory_space=pltpu.VMEM)
    return pl.pallas_call(
        functools.partial(home_kernel, scale, parts),
        in_specs=[vmem] * parts
        + [pl.BlockSpec(memory_space=pltpu.SMEM), pl.BlockSpec(memory_space=pl.ANY), vmem],
        out_specs=[vmem] * (2 * parts),
        out_shape=[jax.ShapeDtypeStruct((rows, cols), BF)] * parts
        + [jax.ShapeDtypeStruct((packed, lanes), BF)] * parts,
        scratch_shapes=[
            pltpu.VMEM((parts, 2 * packed, rows), BF),
            pltpu.VMEM((parts, 2 * packed, cols), BF),
            pltpu.VMEM((latents, cols), BF),
            pltpu.SemaphoreType.DMA((8,)),
        ],
        compiler_params=params(),
        cost_estimate=cost(8 * latents * cols * 128, 20 * 2**20),
        name="home_rows",
    )(*group, place, dec_all, bias)


def assemble_kernel(at_ref, *refs):
    pieces, out, sems = refs[:-2], refs[-2], refs[-1]
    cols = pieces[0].shape[1]
    copies = []
    for d, piece in enumerate(pieces):
        place = pl.multiple_of(((at_ref[0] + d) % len(pieces)) * cols, cols)
        copies.append(pltpu.make_async_copy(piece, out.at[:, pl.ds(place, cols)], sems.at[d]))
    for copy in copies:
        copy.start()
    for copy in copies:
        copy.wait()


def assemble(at, pieces):
    rows, cols = pieces[0].shape
    return pl.pallas_call(
        assemble_kernel,
        in_specs=[pl.BlockSpec(memory_space=pltpu.SMEM)]
        + [pl.BlockSpec(memory_space=pltpu.VMEM)] * len(pieces),
        out_specs=pl.BlockSpec(memory_space=pl.ANY),
        out_shape=jax.ShapeDtypeStruct((rows, cols * len(pieces)), BF),
        scratch_shapes=[pltpu.SemaphoreType.DMA((len(pieces),))],
        compiler_params=params(),
        cost_estimate=cost(0, 2**22),
        name="assemble_recon",
    )(at.astype(jnp.int32).reshape(1), *pieces)


def sum_kernel(*refs):
    out_ref = refs[-1]
    total = refs[0][...].astype(F32)
    for ref in refs[1:-1]:
        total = total + ref[...].astype(F32)
    for copy in range(out_ref.shape[0]):
        out_ref[copy] = total.astype(BF)


def summed(pieces, copies):
    return pl.pallas_call(
        sum_kernel,
        out_shape=jax.ShapeDtypeStruct((copies, *pieces[0].shape), BF),
        compiler_params=params(),
        cost_estimate=cost(0, 2**20),
        name="sum_pieces",
    )(*pieces)


def mix_kernel(msg_ref, dec_hbm, start_ref, out_ref, own_ref, other_ref, name_ref, dec_ref, sems):
    sources = msg_ref.shape[0]
    count = sources * 32
    steps = sems.shape[0]
    quarter = dec_ref.shape[0] // 4
    tall = quarter // steps

    def fetch(step, q):
        at = pl.ds(q * quarter + step * tall, tall)
        return pltpu.make_async_copy(dec_hbm.at[at], dec_ref.at[at], sems.at[step, q])

    for step in range(steps):
        for q in range(4):
            fetch(step, q).start()

    twice = doubled(msg_ref[:, :32, :].reshape(count, 128)).astype(F32).reshape(sources, 4, CAP, 256)
    block = slot_names(msg_ref[:, 32:, :]).astype(F32).reshape(sources, 4, CAP, 128)
    for b in range(4):
        rows = twice[:, b].reshape(sources * CAP, 256)
        other_ref[b] = rows[:, 128:].astype(BF)
        name = block[:, b].reshape(sources * CAP, 128)
        within = jnp.floor(name * (1.0 / 32.0))
        name_ref[b] = (name - 32.0 * within).astype(BF)
        wide = jnp.concatenate([rows[:, :128]] * 2, axis=1)
        lane = (iota((1, 256), 1) // LAT).astype(F32)
        own_ref[b] = jnp.where(jnp.concatenate([within] * 2, axis=1) == lane, wide, 0.0).astype(BF).T
        own = rows[:, :128].astype(BF)
        here = slice(b * LAT, (b + 1) * LAT)
        out_ref[here, :] = dot(dot_tn(own, own)[:LAT, :LAT].astype(BF), start_ref[here, :])

    zero = jnp.zeros((sources * CAP, 128), BF)
    for step in range(steps):
        mixed = []
        for b in range(4):
            wide = []
            for pair in range(tall // 128):
                name = iota((1, 128), 1) // LAT + 2 * pair + step * (tall // LAT)
                wide.append(jnp.where(name_ref[b] == name.astype(F32).astype(BF), other_ref[b], zero))
            mixed.append(dot(own_ref[b], jnp.concatenate(wide, axis=1)).astype(BF))
        total = out_ref[...]
        for q in range(4):
            fetch(step, q).wait()
            left = jnp.concatenate([mixed[b][q * LAT : (q + 1) * LAT] for b in range(4)], axis=0)
            start = q * quarter + step * tall
            total = total + dot(left, dec_ref[start : start + tall, :])
        out_ref[...] = total


def mix(msg, dec_all, own_dec):
    latents, cols = dec_all.shape
    per = msg.shape[0] * CAP
    vmem = pl.BlockSpec(memory_space=pltpu.VMEM)
    return pl.pallas_call(
        mix_kernel,
        in_specs=[vmem, pl.BlockSpec(memory_space=pl.ANY), vmem],
        out_specs=vmem,
        out_shape=jax.ShapeDtypeStruct(own_dec.shape, F32),
        scratch_shapes=[
            pltpu.VMEM((4, 4 * LAT, per), BF),
            pltpu.VMEM((4, per, 128), BF),
            pltpu.VMEM((4, per, 128), BF),
            pltpu.VMEM(dec_all.shape, BF),
            pltpu.SemaphoreType.DMA((4, 4)),
        ],
        compiler_params=params(),
        cost_estimate=cost(1, 1),
        name="mix_decoder",
    )(msg, dec_all, own_dec)


def grads_kernel(
    scale, gate_hbm, proj_hbm, msg_hbm, rows_hbm, mixed_hbm, enc_ref, dec_ref,
    gate_ref, proj_ref, msg_ref, rows_ref, mixed_ref, acc_ref, sems, last
):
    parts = proj_hbm.shape[0]
    sources = msg_ref.shape[0] // parts
    count = sources * 32
    cols = rows_ref.shape[1]

    def fetch(part):
        at = pl.ds(part * sources, sources)
        tall = pl.ds(part * count, count)
        return [
            pltpu.make_async_copy(msg_hbm.at[at], msg_ref.at[at], sems.at[part, 0]),
            pltpu.make_async_copy(gate_hbm.at[at], gate_ref.at[at], sems.at[part, 1]),
            pltpu.make_async_copy(proj_hbm.at[:, at], proj_ref.at[:, at], sems.at[part, 2]),
            pltpu.make_async_copy(rows_hbm.at[tall], rows_ref.at[tall], sems.at[part, 3]),
        ]

    mixed_copy = pltpu.make_async_copy(mixed_hbm, mixed_ref, last)
    for part in range(parts):
        for copy in fetch(part):
            copy.start()
    mixed_copy.start()
    for part in range(parts):
        for copy in fetch(part):
            copy.wait()
        here = slice(part * sources, (part + 1) * sources)
        own = own_expanded(doubled(msg_ref[here, :32, :].reshape(count, 128))[:, :128])
        total = gate_ref[here].astype(F32)
        for other in range(parts):
            total = total - proj_ref[other, here].astype(F32)
        wide = jnp.where(own.astype(F32) > 0, spread(total), 0.0).astype(BF)
        both = jnp.concatenate([wide, own], axis=1)
        more = dot_tn(both, rows_ref[part * count : (part + 1) * count, :])
        if part == 0:
            acc_ref[...] = more
        elif part < parts - 1:
            acc_ref[...] += more
        else:
            more = acc_ref[...] + more
            enc_ref[...] = more[:256, :]
            mixed_copy.wait()
            dec_ref[...] = (mixed_ref[...] - more[256:, :]) * scale


def grads(scale, gate, proj, msg, rows, mixed):
    cols = rows.shape[1]
    shape = jax.ShapeDtypeStruct(mixed.shape, F32)
    vmem = pl.BlockSpec(memory_space=pltpu.VMEM)
    arrays = (gate, proj, msg, rows, mixed)
    return pl.pallas_call(
        functools.partial(grads_kernel, scale),
        in_specs=[pl.BlockSpec(memory_space=pl.ANY)] * len(arrays),
        out_specs=[vmem, vmem],
        out_shape=[shape, shape],
        scratch_shapes=[pltpu.VMEM(array.shape, array.dtype) for array in arrays]
        + [
            pltpu.VMEM((512, cols), F32),
            pltpu.SemaphoreType.DMA((proj.shape[0], 4)),
            pltpu.SemaphoreType.DMA,
        ],
        compiler_params=params(),
        cost_estimate=cost(4 * msg.shape[0] * 32 * cols * 256, 16 * 2**20),
        name="dictionary_grads",
    )(*arrays)


def shifted(value, by, parts):
    if by == 0:
        return value
    return lax.ppermute(value, "dp", [(i, (i + by) % parts) for i in range(parts)])


def body(resid, block_ids, enc_w, enc_b, dec_w, dec_b):
    tok_rows, width = resid.shape
    parts = lax.axis_size("dp")
    shards = lax.axis_size("dict")
    local = enc_w.shape[0]
    here = local // LAT
    slots = here * shards * CAP
    cols = width // parts
    everyone = ("dp", "dict")
    devices = parts * shards
    blocks = here * shards
    scale = (blocks / (tok_rows * devices * block_ids.shape[1])) ** 0.5
    at_x = lax.axis_index("dp")

    ids = block_ids.T
    outgoing = route(ids, resid, dec_b, parts, slots)
    arrived = lax.all_to_all(
        outgoing.reshape(devices, here * CAP, cols), everyone, 0, 0, tiled=True
    )

    enc_x = lax.dynamic_slice(enc_w, (0, at_x * cols), (local, cols))
    dec_x = lax.dynamic_slice(dec_w, (0, at_x * cols), (local, cols))
    dec_all = lax.all_gather(dec_x, "dict", axis=0, tiled=True)

    weights = jnp.concatenate(
        [enc_x.reshape(2, 2 * LAT, cols), dec_x.reshape(2, 2 * LAT, cols)], axis=1
    ).transpose(0, 2, 1)
    bias = jnp.where(at_x == 0, enc_b, 0.0).reshape(2, 2 * LAT)
    pre, proj = encode(scale, arrived, weights, bias)
    partial = lax.all_to_all(pre, everyone, 0, 0, tiled=True)
    projs = lax.all_gather(proj, "dp", axis=0, tiled=False)
    acts = activate(ids, partial.reshape(parts, shards * 2 * CAP, 128))
    msg = messages(ids, acts, parts, shards)
    group = [shifted(acts, d, parts) for d in range(parts)]
    msg, *group = lax.optimization_barrier((msg, *group))
    message = lax.all_to_all(
        msg.reshape(devices, here * CAP + 16, 128), everyone, 0, 0, tiled=True
    )

    place = at_x.astype(jnp.int32).reshape(1)
    made = home(scale, place, group, dec_all, dec_b.reshape(parts, cols))
    total = summed([shifted(made[parts + d], -d, parts) for d in range(parts)], parts)
    gates = lax.all_to_all(total.reshape(devices, 2 * CAP, 128), everyone, 0, 0, tiled=True)
    total, *made = lax.optimization_barrier((total, *made[:parts]))
    pieces = [shifted(made[d], -d, parts) for d in range(parts)]
    mixed = mix(message, dec_all, dec_x)
    enc_grad, dec_grad = grads(
        scale, gates, projs, message, arrived.reshape(devices * here * CAP, cols), mixed
    )
    recon = assemble(at_x, pieces)
    return (recon, enc_grad, dec_grad)


def solution(mesh):
    placed = (
        P(("dp", "dict"), None),
        P(("dp", "dict"), None),
        P("dict", None),
        P("dict"),
        P("dict", None),
        P(),
    )
    return jax.shard_map(
        body,
        mesh=mesh,
        in_specs=placed,
        out_specs=(P(("dp", "dict"), None), P("dict", "dp"), P("dict", "dp")),
        check_vma=False,
    )
```

```python
import functools

import jax
import jax.numpy as jnp
from jax import lax
from jax.experimental import pallas as pl
from jax.experimental.pallas import tpu as pltpu
from jax.sharding import PartitionSpec as P

LAT = 64
CAP = 8
BF = jnp.bfloat16
F32 = jnp.float32
PIECES = 4
VMEM_LIMIT = 56 * 1024 * 1024


def params(**more):
    return pltpu.CompilerParams(vmem_limit_bytes=VMEM_LIMIT, **more)


def cost(flops, moved):
    return pl.CostEstimate(flops=int(flops), bytes_accessed=int(moved), transcendentals=0)


def dot(a, b):
    return jnp.dot(a, b, preferred_element_type=F32)


def dot_tn(a, b):
    return lax.dot_general(a, b, (((0,), (0,)), ((), ())), preferred_element_type=F32)


def dot_nt(a, b):
    return lax.dot_general(a, b, (((1,), (1,)), ((), ())), preferred_element_type=F32)


def iota(shape, axis):
    return lax.broadcasted_iota(jnp.int32, shape, axis)


def ranks(ids, blocks):
    rows = ids.shape[1]
    block = iota((blocks, rows), 0)
    one0 = (block == ids[0:1, :]).astype(F32)
    one1 = (block == ids[1:2, :]).astype(F32)
    before = (iota((rows, rows), 0) < iota((rows, rows), 1)).astype(BF)
    pre0 = dot(one0.astype(BF), before)
    pre1 = dot(one1.astype(BF), before) + jnp.sum(one0, axis=1, keepdims=True)
    rank0 = jnp.sum(one0 * pre0, axis=0, keepdims=True).astype(jnp.int32)
    rank1 = jnp.sum(one1 * pre1, axis=0, keepdims=True).astype(jnp.int32)
    return rank0, rank1


def slot_table(ids, shards, lanes=128):
    rows = ids.shape[1]
    found = jnp.zeros((shards, lanes), F32)
    for k, rank in enumerate(ranks(ids, shards * 4)):
        block = ids[k : k + 1, :]
        other = (ids[1 - k : 2 - k, :] + 1).astype(F32)
        target = jnp.where(iota((shards, rows), 0) == block // 4, other, 0.0).astype(BF)
        place = iota((lanes, rows), 0) == (block % 4) * CAP + rank
        found = found + dot_nt(target, jnp.where(place, 1.0, 0.0).astype(BF))
    return found - 1.0


def slot_names(table):
    sources = table.shape[0]
    shape = (sources, 32, 128)
    row = jnp.concatenate([table, table], axis=1).astype(F32)
    kept = jnp.where(iota(shape, 1) == iota(shape, 2), row, 0.0).astype(BF)
    return dot(kept.reshape(sources * 32, 128), jnp.ones((128, 128), BF)).astype(BF)


def route_kernel(ids_ref, resid_ref, bias_ref, out_hbm, pick_ref, out_ref, sems):
    parts, slots, cols = out_ref.shape
    rows = pick_ref.shape[1]
    ids = ids_ref[...]
    rank0, rank1 = ranks(ids, slots // CAP)
    slot = iota((slots, rows), 0)
    is0 = slot == ids[0:1, :] * CAP + rank0
    is1 = slot == ids[1:2, :] * CAP + rank1
    pick_ref[...] = jnp.where(is0 | is1, 1.0, 0.0).astype(BF)
    pieces = sems.shape[1]
    tall = slots // pieces

    def send(part, piece):
        at = pl.ds(piece * tall, tall)
        return pltpu.make_async_copy(out_ref.at[part, at], out_hbm.at[part, at], sems.at[part, piece])

    for part in range(parts):
        here = slice(part * cols, (part + 1) * cols)
        centered = (resid_ref[:, here].astype(F32) - bias_ref[:, here]).astype(BF)
        for piece in range(pieces):
            at = slice(piece * tall, (piece + 1) * tall)
            out_ref[part, at, :] = dot(pick_ref[at, :], centered).astype(BF)
            send(part, piece).start()
    for part in range(parts):
        for piece in range(pieces):
            send(part, piece).wait()


def route(ids, resid, dec_b, parts, slots):
    rows, width = resid.shape
    cols = width // parts
    vmem = pl.BlockSpec(memory_space=pltpu.VMEM)
    return pl.pallas_call(
        route_kernel,
        in_specs=[vmem] * 3,
        out_specs=pl.BlockSpec(memory_space=pl.ANY),
        out_shape=jax.ShapeDtypeStruct((parts, slots, cols), BF),
        scratch_shapes=[
            pltpu.VMEM((slots, rows), BF),
            pltpu.VMEM((parts, slots, cols), BF),
            pltpu.SemaphoreType.DMA((parts, 4)),
        ],
        compiler_params=params(),
        cost_estimate=cost(2 * slots * rows * width, 10 * 2**20),
        name="route_rows",
    )(ids, resid, dec_b.reshape(1, width))


def encode_kernel(scale, rows_hbm, weight_ref, bias_ref, pre_ref, proj_ref, rows_ref, sems):
    pieces = sems.shape[0]
    sources, _, cols = rows_ref.shape
    count = sources // pieces
    low = iota((1, 1, 128), 2) < LAT

    def fetch(piece):
        at = pl.ds(piece * count, count)
        return pltpu.make_async_copy(rows_hbm.at[at], rows_ref.at[at], sems.at[piece])

    for piece in range(pieces):
        fetch(piece).start()
    for piece in range(pieces):
        fetch(piece).wait()
        here = slice(piece * count, (piece + 1) * count)
        projected = []
        for p in range(2):
            rows = rows_ref[here, p * 16 : (p + 1) * 16, :].reshape(count * 16, cols)
            both = dot(rows, weight_ref[p]).reshape(count, 2, CAP, 256)
            pre = jnp.where(low, both[:, 0, :, :128], both[:, 1, :, :128])
            pre_ref[here, p * CAP : (p + 1) * CAP, :] = pre + bias_ref[p : p + 1, :][None]
            projected.append(jnp.where(low, both[:, 0, :, 128:], both[:, 1, :, 128:]) * scale)
        proj_ref[here] = jnp.concatenate(projected, axis=1).astype(BF)


def encode(scale, arrived, weights, bias):
    sources, here, cols = arrived.shape
    shape = (sources, 2 * CAP, 128)
    vmem = pl.BlockSpec(memory_space=pltpu.VMEM)
    return pl.pallas_call(
        functools.partial(encode_kernel, scale),
        in_specs=[pl.BlockSpec(memory_space=pl.ANY), vmem, vmem],
        out_specs=[vmem, vmem],
        out_shape=[jax.ShapeDtypeStruct(shape, F32), jax.ShapeDtypeStruct(shape, BF)],
        scratch_shapes=[pltpu.VMEM(arrived.shape, BF), pltpu.SemaphoreType.DMA((PIECES,))],
        compiler_params=params(),
        cost_estimate=cost(2 * sources * here * cols * 256, 11 * 2**20),
        name="encode_rows",
    )(arrived, weights, bias)


def activate_kernel(ids_ref, pre_ref, group_ref):
    packed = pre_ref.shape[1]
    ids = ids_ref[...]
    total = pre_ref[0] + pre_ref[1] + pre_ref[2] + pre_ref[3]
    group_ref[:packed, :] = jnp.maximum(total, 0.0).astype(BF)
    halves = [ids[:, :128], ids[:, 128:], jnp.zeros((12, 128), jnp.int32)]
    group_ref[packed:, :] = jnp.concatenate(halves, axis=0).astype(F32).astype(BF)


def activate(ids, partial):
    parts, packed, lanes = partial.shape
    return pl.pallas_call(
        activate_kernel,
        out_shape=jax.ShapeDtypeStruct((packed + 16, lanes), BF),
        compiler_params=params(),
        cost_estimate=cost(4 * packed * lanes, 2**20),
        name="activate_slots",
    )(ids, partial)


def message_kernel(ids_ref, acts_ref, msg_ref):
    shards = msg_ref.shape[1]
    packed = acts_ref.shape[0] - 16
    rows = ids_ref.shape[1]
    slots = 2 * packed
    ids = ids_ref[...]
    rank0, rank1 = ranks(ids, slots // CAP)
    acts = acts_ref[:packed, :]
    slot = iota((slots, rows), 0)
    found = []
    for k, rank in ((0, rank0), (1, rank1)):
        block = ids[k : k + 1, :]
        half = block % 2
        at = (block // 2) * CAP + rank
        here = jnp.where(slot == half * packed + at, 1.0, 0.0).astype(BF)
        found.append(dot_tn(here[:packed], acts)[:, :LAT] + dot_tn(here[packed:], acts)[:, LAT:])
    first, second = found
    straight = jnp.concatenate([first, second], axis=1).astype(BF)
    crossed = jnp.concatenate([second, first], axis=1).astype(BF)
    pick0 = jnp.where(slot == ids[0:1, :] * CAP + rank0, 1.0, 0.0).astype(BF)
    pick1 = jnp.where(slot == ids[1:2, :] * CAP + rank1, 1.0, 0.0).astype(BF)
    msg = (dot(pick0, straight) + dot(pick1, crossed)).astype(BF)
    msg = msg.reshape(shards, slots // shards, 128)
    table = slot_table(ids, shards)
    table = jnp.broadcast_to(table[:, None, :], (shards, 16, 128)).astype(BF)
    for copy in range(msg_ref.shape[0]):
        msg_ref[copy, :, : slots // shards, :] = msg
        msg_ref[copy, :, slots // shards :, :] = table


def messages(ids, acts, parts, shards):
    tall, lanes = acts.shape
    slots = 2 * (tall - 16)
    return pl.pallas_call(
        message_kernel,
        out_shape=jax.ShapeDtypeStruct((parts, shards, slots // shards + 16, lanes), BF),
        compiler_params=params(),
        cost_estimate=cost(8 * slots * ids.shape[1] * lanes, 2**21),
        name="make_messages",
    )(ids, acts)


def doubled(pair):
    source, target = iota((128, 256), 0), iota((128, 256), 1)
    copy = source == (target // 128) * LAT + target % LAT
    return dot(pair, jnp.where(copy, 1.0, 0.0).astype(BF)).astype(BF)


def lane_block(group):
    return (iota((1, 128), 1) // LAT + group * 2).astype(F32).astype(BF)


def own_expanded(own):
    count = own.shape[0]
    twice = jnp.concatenate([own, own], axis=1)
    mine = (iota((count, 256), 0) // CAP) % 4 == iota((count, 256), 1) // LAT
    return jnp.where(mine, twice.astype(F32), 0.0).astype(BF)


def spread(packed):
    low = iota((1, 1, 128), 2) < LAT
    zero = jnp.zeros((packed.shape[0], CAP, 128), F32)
    rows = []
    for p in range(2):
        piece = packed[:, p * CAP : (p + 1) * CAP, :]
        for q in range(2):
            kept = jnp.where(low if q == 0 else ~low, piece, 0.0)
            rows.append(jnp.concatenate([kept, zero] if p == 0 else [zero, kept], axis=2))
    return jnp.concatenate(rows, axis=1).reshape(packed.shape[0] * 32, 256)


def gathered(wide):
    wide = wide.reshape(wide.shape[0] // 32, 4, CAP, 256)
    low = iota((1, 1, 128), 2) < LAT
    packed = []
    for p in range(2):
        lanes = slice(p * 128, (p + 1) * 128)
        packed.append(jnp.where(low, wide[:, 2 * p, :, lanes], wide[:, 2 * p + 1, :, lanes]))
    return jnp.concatenate(packed, axis=1)


def home_kernel(scale, parts, *refs):
    group, (place_ref, dec_hbm, bias_ref), refs = refs[:parts], refs[parts : parts + 3], refs[parts + 3 :]
    recon, gates, (pick_ref, part_ref, dec_ref, sems) = refs[:parts], refs[parts : 2 * parts], refs[2 * parts :]
    slots, rows = pick_ref.shape[1:]
    packed = slots // 2
    pieces = sems.shape[0]
    tall = dec_ref.shape[0] // pieces
    per = tall // 256

    def fetch(piece):
        at = pl.ds(pl.multiple_of(piece * tall, tall), tall)
        return pltpu.make_async_copy(dec_hbm.at[at], dec_ref.at[at], sems.at[piece])

    for piece in range(pieces):
        fetch(piece).start()

    slot = iota((slots, rows), 0)
    for d in range(parts):
        halves = group[d][packed:, :].astype(F32).astype(jnp.int32)
        ids = jnp.concatenate([halves[0:2], halves[2:4]], axis=1)
        rank0, rank1 = ranks(ids, slots // CAP)
        here = (slot == ids[0:1, :] * CAP + rank0) | (slot == ids[1:2, :] * CAP + rank1)
        pick_ref[d] = jnp.where(here, 1.0, 0.0).astype(BF)

    def aligned(start, size):
        return pl.ds(pl.multiple_of(start * size, size), size)

    @pl.loop(0, pieces)
    def _(piece):
        fetch(piece).wait()
        for g in range(per):
            shard = piece * per + g
            acts = jnp.stack([group[d][aligned(shard, 16), :].astype(F32) for d in range(parts)])
            part = dot(spread(acts).astype(BF), dec_ref[aligned(shard, 256), :]).astype(BF)
            for d in range(parts):
                part_ref[d, aligned(shard, 32), :] = part[d * 32 : (d + 1) * 32]

    bias = bias_ref[pl.ds(place_ref[0], 1), :]
    for d in range(parts):
        total = dot_tn(pick_ref[d], part_ref[d])
        recon[d][...] = (total + bias).astype(BF)
        part_ref[d] = dot(pick_ref[d], total.astype(BF)).astype(BF)

    @pl.loop(0, pieces)
    def _(piece):
        for g in range(per):
            shard = piece * per + g
            total = jnp.concatenate([part_ref[d, aligned(shard, 32), :] for d in range(parts)], axis=0)
            wide = dot_nt(total, dec_ref[aligned(shard, 256), :])
            gate = (gathered(wide) * scale).astype(BF)
            for d in range(parts):
                gates[d][aligned(shard, 16), :] = gate[d]


def home(scale, place, group, dec_all, bias):
    latents, cols = dec_all.shape
    tall, lanes = group[0].shape
    parts = len(group)
    packed = tall - 16
    rows = 256
    vmem = pl.BlockSpec(memory_space=pltpu.VMEM)
    return pl.pallas_call(
        functools.partial(home_kernel, scale, parts),
        in_specs=[vmem] * parts
        + [pl.BlockSpec(memory_space=pltpu.SMEM), pl.BlockSpec(memory_space=pl.ANY), vmem],
        out_specs=[vmem] * (2 * parts),
        out_shape=[jax.ShapeDtypeStruct((rows, cols), BF)] * parts
        + [jax.ShapeDtypeStruct((packed, lanes), BF)] * parts,
        scratch_shapes=[
            pltpu.VMEM((parts, 2 * packed, rows), BF),
            pltpu.VMEM((parts, 2 * packed, cols), BF),
            pltpu.VMEM((latents, cols), BF),
            pltpu.SemaphoreType.DMA((4,)),
        ],
        compiler_params=params(),
        cost_estimate=cost(8 * latents * cols * 128, 20 * 2**20),
        name="home_rows",
    )(*group, place, dec_all, bias)


def assemble_kernel(at_ref, *refs):
    pieces, out, sems = refs[:-2], refs[-2], refs[-1]
    cols = pieces[0].shape[1]
    copies = []
    for d, piece in enumerate(pieces):
        place = pl.multiple_of(((at_ref[0] + d) % len(pieces)) * cols, cols)
        copies.append(pltpu.make_async_copy(piece, out.at[:, pl.ds(place, cols)], sems.at[d]))
    for copy in copies:
        copy.start()
    for copy in copies:
        copy.wait()


def assemble(at, pieces):
    rows, cols = pieces[0].shape
    return pl.pallas_call(
        assemble_kernel,
        in_specs=[pl.BlockSpec(memory_space=pltpu.SMEM)]
        + [pl.BlockSpec(memory_space=pltpu.VMEM)] * len(pieces),
        out_specs=pl.BlockSpec(memory_space=pl.ANY),
        out_shape=jax.ShapeDtypeStruct((rows, cols * len(pieces)), BF),
        scratch_shapes=[pltpu.SemaphoreType.DMA((len(pieces),))],
        compiler_params=params(),
        cost_estimate=cost(0, 2**22),
        name="assemble_recon",
    )(at.astype(jnp.int32).reshape(1), *pieces)


def sum_kernel(*refs):
    out_ref = refs[-1]
    total = refs[0][...].astype(F32)
    for ref in refs[1:-1]:
        total = total + ref[...].astype(F32)
    for copy in range(out_ref.shape[0]):
        out_ref[copy] = total.astype(BF)


def summed(pieces, copies):
    return pl.pallas_call(
        sum_kernel,
        out_shape=jax.ShapeDtypeStruct((copies, *pieces[0].shape), BF),
        compiler_params=params(),
        cost_estimate=cost(0, 2**20),
        name="sum_pieces",
    )(*pieces)


def mix_kernel(msg_ref, dec_hbm, start_ref, out_ref, own_ref, other_ref, name_ref, dec_ref, sems):
    sources = msg_ref.shape[0]
    count = sources * 32
    steps = sems.shape[0]
    quarter = dec_ref.shape[0] // 4
    tall = quarter // steps

    def fetch(step, q):
        at = pl.ds(q * quarter + step * tall, tall)
        return pltpu.make_async_copy(dec_hbm.at[at], dec_ref.at[at], sems.at[step, q])

    for step in range(steps):
        for q in range(4):
            fetch(step, q).start()

    twice = doubled(msg_ref[:, :32, :].reshape(count, 128)).astype(F32).reshape(sources, 4, CAP, 256)
    block = slot_names(msg_ref[:, 32:, :]).astype(F32).reshape(sources, 4, CAP, 128)
    for b in range(4):
        rows = twice[:, b].reshape(sources * CAP, 256)
        other_ref[b] = rows[:, 128:].astype(BF)
        name = block[:, b].reshape(sources * CAP, 128)
        within = jnp.floor(name * (1.0 / 32.0))
        name_ref[b] = (name - 32.0 * within).astype(BF)
        wide = jnp.concatenate([rows[:, :128]] * 2, axis=1)
        lane = (iota((1, 256), 1) // LAT).astype(F32)
        own_ref[b] = jnp.where(jnp.concatenate([within] * 2, axis=1) == lane, wide, 0.0).astype(BF).T
        own = rows[:, :128].astype(BF)
        here = slice(b * LAT, (b + 1) * LAT)
        out_ref[here, :] = dot(dot_tn(own, own)[:LAT, :LAT].astype(BF), start_ref[here, :])

    zero = jnp.zeros((sources * CAP, 128), BF)
    for step in range(steps):
        mixed = []
        for b in range(4):
            wide = []
            for pair in range(tall // 128):
                name = iota((1, 128), 1) // LAT + 2 * pair + step * (tall // LAT)
                wide.append(jnp.where(name_ref[b] == name.astype(F32).astype(BF), other_ref[b], zero))
            mixed.append(dot(own_ref[b], jnp.concatenate(wide, axis=1)).astype(BF))
        total = out_ref[...]
        for q in range(4):
            fetch(step, q).wait()
            left = jnp.concatenate([mixed[b][q * LAT : (q + 1) * LAT] for b in range(4)], axis=0)
            start = q * quarter + step * tall
            total = total + dot(left, dec_ref[start : start + tall, :])
        out_ref[...] = total


def mix(msg, dec_all, own_dec):
    latents, cols = dec_all.shape
    per = msg.shape[0] * CAP
    vmem = pl.BlockSpec(memory_space=pltpu.VMEM)
    return pl.pallas_call(
        mix_kernel,
        in_specs=[vmem, pl.BlockSpec(memory_space=pl.ANY), vmem],
        out_specs=vmem,
        out_shape=jax.ShapeDtypeStruct(own_dec.shape, F32),
        scratch_shapes=[
            pltpu.VMEM((4, 4 * LAT, per), BF),
            pltpu.VMEM((4, per, 128), BF),
            pltpu.VMEM((4, per, 128), BF),
            pltpu.VMEM(dec_all.shape, BF),
            pltpu.SemaphoreType.DMA((1, 4)),
        ],
        compiler_params=params(),
        cost_estimate=cost(1, 1),
        name="mix_decoder",
    )(msg, dec_all, own_dec)


def grads_kernel(
    scale, gate_hbm, proj_hbm, msg_hbm, rows_hbm, mixed_hbm, enc_ref, dec_ref,
    gate_ref, proj_ref, msg_ref, rows_ref, mixed_ref, acc_ref, sems, last
):
    parts = proj_hbm.shape[0]
    sources = msg_ref.shape[0] // parts
    count = sources * 32
    cols = rows_ref.shape[1]

    def fetch(part):
        at = pl.ds(part * sources, sources)
        tall = pl.ds(part * count, count)
        return [
            pltpu.make_async_copy(msg_hbm.at[at], msg_ref.at[at], sems.at[part, 0]),
            pltpu.make_async_copy(gate_hbm.at[at], gate_ref.at[at], sems.at[part, 1]),
            pltpu.make_async_copy(proj_hbm.at[:, at], proj_ref.at[:, at], sems.at[part, 2]),
            pltpu.make_async_copy(rows_hbm.at[tall], rows_ref.at[tall], sems.at[part, 3]),
        ]

    mixed_copy = pltpu.make_async_copy(mixed_hbm, mixed_ref, last)
    for part in range(parts):
        for copy in fetch(part):
            copy.start()
    mixed_copy.start()
    for part in range(parts):
        for copy in fetch(part):
            copy.wait()
        here = slice(part * sources, (part + 1) * sources)
        own = own_expanded(doubled(msg_ref[here, :32, :].reshape(count, 128))[:, :128])
        total = gate_ref[here].astype(F32)
        for other in range(parts):
            total = total - proj_ref[other, here].astype(F32)
        wide = jnp.where(own.astype(F32) > 0, spread(total), 0.0).astype(BF)
        both = jnp.concatenate([wide, own], axis=1)
        more = dot_tn(both, rows_ref[part * count : (part + 1) * count, :])
        if part == 0:
            acc_ref[...] = more
        elif part < parts - 1:
            acc_ref[...] += more
        else:
            more = acc_ref[...] + more
            enc_ref[...] = more[:256, :]
            mixed_copy.wait()
            dec_ref[...] = (mixed_ref[...] - more[256:, :]) * scale


def grads(scale, gate, proj, msg, rows, mixed):
    cols = rows.shape[1]
    shape = jax.ShapeDtypeStruct(mixed.shape, F32)
    vmem = pl.BlockSpec(memory_space=pltpu.VMEM)
    arrays = (gate, proj, msg, rows, mixed)
    return pl.pallas_call(
        functools.partial(grads_kernel, scale),
        in_specs=[pl.BlockSpec(memory_space=pl.ANY)] * len(arrays),
        out_specs=[vmem, vmem],
        out_shape=[shape, shape],
        scratch_shapes=[pltpu.VMEM(array.shape, array.dtype) for array in arrays]
        + [
            pltpu.VMEM((512, cols), F32),
            pltpu.SemaphoreType.DMA((proj.shape[0], 4)),
            pltpu.SemaphoreType.DMA,
        ],
        compiler_params=params(),
        cost_estimate=cost(4 * msg.shape[0] * 32 * cols * 256, 16 * 2**20),
        name="dictionary_grads",
    )(*arrays)


def shifted(value, by, parts):
    if by == 0:
        return value
    return lax.ppermute(value, "dp", [(i, (i + by) % parts) for i in range(parts)])


def body(resid, block_ids, enc_w, enc_b, dec_w, dec_b):
    tok_rows, width = resid.shape
    parts = lax.axis_size("dp")
    shards = lax.axis_size("dict")
    local = enc_w.shape[0]
    here = local // LAT
    slots = here * shards * CAP
    cols = width // parts
    everyone = ("dp", "dict")
    devices = parts * shards
    blocks = here * shards
    scale = (blocks / (tok_rows * devices * block_ids.shape[1])) ** 0.5
    at_x = lax.axis_index("dp")

    ids = block_ids.T
    outgoing = route(ids, resid, dec_b, parts, slots)
    arrived = lax.all_to_all(
        outgoing.reshape(devices, here * CAP, cols), everyone, 0, 0, tiled=True
    )

    enc_x = lax.dynamic_slice(enc_w, (0, at_x * cols), (local, cols))
    dec_x = lax.dynamic_slice(dec_w, (0, at_x * cols), (local, cols))
    dec_all = lax.all_gather(dec_x, "dict", axis=0, tiled=True)

    weights = jnp.concatenate(
        [enc_x.reshape(2, 2 * LAT, cols), dec_x.reshape(2, 2 * LAT, cols)], axis=1
    ).transpose(0, 2, 1)
    bias = jnp.where(at_x == 0, enc_b, 0.0).reshape(2, 2 * LAT)
    pre, proj = encode(scale, arrived, weights, bias)
    partial = lax.all_to_all(pre, everyone, 0, 0, tiled=True)
    projs = lax.all_gather(proj, "dp", axis=0, tiled=False)
    acts = activate(ids, partial.reshape(parts, shards * 2 * CAP, 128))
    msg = messages(ids, acts, parts, shards)
    group = [shifted(acts, d, parts) for d in range(parts)]
    msg, *group = lax.optimization_barrier((msg, *group))
    message = lax.all_to_all(
        msg.reshape(devices, here * CAP + 16, 128), everyone, 0, 0, tiled=True
    )

    place = at_x.astype(jnp.int32).reshape(1)
    made = home(scale, place, group, dec_all, dec_b.reshape(parts, cols))
    total = summed([shifted(made[parts + d], -d, parts) for d in range(parts)], parts)
    gates = lax.all_to_all(total.reshape(devices, 2 * CAP, 128), everyone, 0, 0, tiled=True)
    total, *made = lax.optimization_barrier((total, *made[:parts]))
    pieces = [shifted(made[d], -d, parts) for d in range(parts)]
    mixed = mix(message, dec_all, dec_x)
    enc_grad, dec_grad = grads(
        scale, gates, projs, message, arrived.reshape(devices * here * CAP, cols), mixed
    )
    recon = assemble(at_x, pieces)
    return (recon, enc_grad, dec_grad)


def solution(mesh):
    placed = (
        P(("dp", "dict"), None),
        P(("dp", "dict"), None),
        P("dict", None),
        P("dict"),
        P("dict", None),
        P(),
    )
    return jax.shard_map(
        body,
        mesh=mesh,
        in_specs=placed,
        out_specs=(P(("dp", "dict"), None), P("dict", "dp"), P("dict", "dp")),
        check_vma=False,
    )
```

```python
import functools

import jax
import jax.numpy as jnp
from jax import lax
from jax.experimental import pallas as pl
from jax.experimental.pallas import tpu as pltpu
from jax.sharding import PartitionSpec as P

LAT = 64
CAP = 8
BF = jnp.bfloat16
F32 = jnp.float32
PIECES = 4
VMEM_LIMIT = 56 * 1024 * 1024


def params(**more):
    return pltpu.CompilerParams(vmem_limit_bytes=VMEM_LIMIT, **more)


def cost(flops, moved):
    return pl.CostEstimate(flops=int(flops), bytes_accessed=int(moved), transcendentals=0)


def dot(a, b):
    return jnp.dot(a, b, preferred_element_type=F32)


def dot_tn(a, b):
    return lax.dot_general(a, b, (((0,), (0,)), ((), ())), preferred_element_type=F32)


def dot_nt(a, b):
    return lax.dot_general(a, b, (((1,), (1,)), ((), ())), preferred_element_type=F32)


def iota(shape, axis):
    return lax.broadcasted_iota(jnp.int32, shape, axis)


def ranks(ids, blocks):
    rows = ids.shape[1]
    block = iota((blocks, rows), 0)
    one0 = (block == ids[0:1, :]).astype(F32)
    one1 = (block == ids[1:2, :]).astype(F32)
    before = (iota((rows, rows), 0) < iota((rows, rows), 1)).astype(BF)
    pre0 = dot(one0.astype(BF), before)
    pre1 = dot(one1.astype(BF), before) + jnp.sum(one0, axis=1, keepdims=True)
    rank0 = jnp.sum(one0 * pre0, axis=0, keepdims=True).astype(jnp.int32)
    rank1 = jnp.sum(one1 * pre1, axis=0, keepdims=True).astype(jnp.int32)
    return rank0, rank1


def slot_table(ids, shards, lanes=128):
    rows = ids.shape[1]
    found = jnp.zeros((shards, lanes), F32)
    for k, rank in enumerate(ranks(ids, shards * 4)):
        block = ids[k : k + 1, :]
        other = (ids[1 - k : 2 - k, :] + 1).astype(F32)
        target = jnp.where(iota((shards, rows), 0) == block // 4, other, 0.0).astype(BF)
        place = iota((lanes, rows), 0) == (block % 4) * CAP + rank
        found = found + dot_nt(target, jnp.where(place, 1.0, 0.0).astype(BF))
    return found - 1.0


def slot_names(table):
    sources = table.shape[0]
    shape = (sources, 32, 128)
    row = jnp.concatenate([table, table], axis=1).astype(F32)
    kept = jnp.where(iota(shape, 1) == iota(shape, 2), row, 0.0).astype(BF)
    return dot(kept.reshape(sources * 32, 128), jnp.ones((128, 128), BF)).astype(BF)


def route_kernel(ids_ref, resid_ref, bias_ref, out_hbm, pick_ref, out_ref, sems):
    parts, slots, cols = out_ref.shape
    rows = pick_ref.shape[1]
    ids = ids_ref[...]
    rank0, rank1 = ranks(ids, slots // CAP)
    slot = iota((slots, rows), 0)
    is0 = slot == ids[0:1, :] * CAP + rank0
    is1 = slot == ids[1:2, :] * CAP + rank1
    pick_ref[...] = jnp.where(is0 | is1, 1.0, 0.0).astype(BF)
    pieces = sems.shape[1]
    tall = slots // pieces

    def send(part, piece):
        at = pl.ds(piece * tall, tall)
        return pltpu.make_async_copy(out_ref.at[part, at], out_hbm.at[part, at], sems.at[part, piece])

    for part in range(parts):
        here = slice(part * cols, (part + 1) * cols)
        centered = (resid_ref[:, here].astype(F32) - bias_ref[:, here]).astype(BF)
        for piece in range(pieces):
            at = slice(piece * tall, (piece + 1) * tall)
            out_ref[part, at, :] = dot(pick_ref[at, :], centered).astype(BF)
            send(part, piece).start()
    for part in range(parts):
        for piece in range(pieces):
            send(part, piece).wait()


def route(ids, resid, dec_b, parts, slots):
    rows, width = resid.shape
    cols = width // parts
    vmem = pl.BlockSpec(memory_space=pltpu.VMEM)
    return pl.pallas_call(
        route_kernel,
        in_specs=[vmem] * 3,
        out_specs=pl.BlockSpec(memory_space=pl.ANY),
        out_shape=jax.ShapeDtypeStruct((parts, slots, cols), BF),
        scratch_shapes=[
            pltpu.VMEM((slots, rows), BF),
            pltpu.VMEM((parts, slots, cols), BF),
            pltpu.SemaphoreType.DMA((parts, 4)),
        ],
        compiler_params=params(),
        cost_estimate=cost(2 * slots * rows * width, 10 * 2**20),
        name="route_rows",
    )(ids, resid, dec_b.reshape(1, width))


def encode_kernel(scale, rows_hbm, weight_ref, bias_ref, pre_ref, proj_ref, rows_ref, sems):
    pieces = sems.shape[0]
    sources, _, cols = rows_ref.shape
    count = sources // pieces
    low = iota((1, 1, 128), 2) < LAT

    def fetch(piece):
        at = pl.ds(piece * count, count)
        return pltpu.make_async_copy(rows_hbm.at[at], rows_ref.at[at], sems.at[piece])

    for piece in range(pieces):
        fetch(piece).start()
    for piece in range(pieces):
        fetch(piece).wait()
        here = slice(piece * count, (piece + 1) * count)
        projected = []
        for p in range(2):
            rows = rows_ref[here, p * 16 : (p + 1) * 16, :].reshape(count * 16, cols)
            both = dot(rows, weight_ref[p]).reshape(count, 2, CAP, 256)
            pre = jnp.where(low, both[:, 0, :, :128], both[:, 1, :, :128])
            pre_ref[here, p * CAP : (p + 1) * CAP, :] = pre + bias_ref[p : p + 1, :][None]
            projected.append(jnp.where(low, both[:, 0, :, 128:], both[:, 1, :, 128:]) * scale)
        proj_ref[here] = jnp.concatenate(projected, axis=1).astype(BF)


def encode(scale, arrived, weights, bias):
    sources, here, cols = arrived.shape
    shape = (sources, 2 * CAP, 128)
    vmem = pl.BlockSpec(memory_space=pltpu.VMEM)
    return pl.pallas_call(
        functools.partial(encode_kernel, scale),
        in_specs=[pl.BlockSpec(memory_space=pl.ANY), vmem, vmem],
        out_specs=[vmem, vmem],
        out_shape=[jax.ShapeDtypeStruct(shape, F32), jax.ShapeDtypeStruct(shape, BF)],
        scratch_shapes=[pltpu.VMEM(arrived.shape, BF), pltpu.SemaphoreType.DMA((PIECES,))],
        compiler_params=params(),
        cost_estimate=cost(2 * sources * here * cols * 256, 11 * 2**20),
        name="encode_rows",
    )(arrived, weights, bias)


def info_kernel(blocks, ids_ref, info_ref):
    ids = ids_ref[...]
    rank = jnp.concatenate(ranks(ids, blocks), axis=0)
    rows = [ids[:, :128], ids[:, 128:], rank[:, :128], rank[:, 128:], jnp.zeros((8, 128), jnp.int32)]
    info_ref[...] = jnp.concatenate(rows, axis=0).astype(F32).astype(BF)


def pair_info(ids, blocks):
    return pl.pallas_call(
        functools.partial(info_kernel, blocks),
        out_shape=jax.ShapeDtypeStruct((16, 128), BF),
        compiler_params=params(),
        cost_estimate=cost(2e7, 2**16),
        name="pair_info",
    )(ids)


def read_info(info):
    rows = info.astype(F32).astype(jnp.int32)
    ids = jnp.concatenate([rows[0:2], rows[2:4]], axis=1)
    return ids, jnp.concatenate([rows[4:6], rows[6:8]], axis=1)


def activate_kernel(info_ref, pre_ref, group_ref):
    packed = pre_ref.shape[1]
    total = pre_ref[0] + pre_ref[1] + pre_ref[2] + pre_ref[3]
    group_ref[:packed, :] = jnp.maximum(total, 0.0).astype(BF)
    group_ref[packed:, :] = info_ref[...]


def activate(info, partial):
    parts, packed, lanes = partial.shape
    return pl.pallas_call(
        activate_kernel,
        out_shape=jax.ShapeDtypeStruct((packed + 16, lanes), BF),
        compiler_params=params(),
        cost_estimate=cost(4 * packed * lanes, 2**20),
        name="activate_slots",
    )(info, partial)


def message_kernel(ids_ref, acts_ref, msg_ref):
    shards = msg_ref.shape[1]
    packed = acts_ref.shape[0] - 16
    rows = ids_ref.shape[1]
    slots = 2 * packed
    ids = ids_ref[...]
    rank0, rank1 = ranks(ids, slots // CAP)
    acts = acts_ref[:packed, :]
    slot = iota((slots, rows), 0)
    found = []
    for k, rank in ((0, rank0), (1, rank1)):
        block = ids[k : k + 1, :]
        half = block % 2
        at = (block // 2) * CAP + rank
        here = jnp.where(slot == half * packed + at, 1.0, 0.0).astype(BF)
        found.append(dot_tn(here[:packed], acts)[:, :LAT] + dot_tn(here[packed:], acts)[:, LAT:])
    first, second = found
    straight = jnp.concatenate([first, second], axis=1).astype(BF)
    crossed = jnp.concatenate([second, first], axis=1).astype(BF)
    pick0 = jnp.where(slot == ids[0:1, :] * CAP + rank0, 1.0, 0.0).astype(BF)
    pick1 = jnp.where(slot == ids[1:2, :] * CAP + rank1, 1.0, 0.0).astype(BF)
    msg = (dot(pick0, straight) + dot(pick1, crossed)).astype(BF)
    msg = msg.reshape(shards, slots // shards, 128)
    table = slot_table(ids, shards)
    table = jnp.broadcast_to(table[:, None, :], (shards, 16, 128)).astype(BF)
    for copy in range(msg_ref.shape[0]):
        msg_ref[copy, :, : slots // shards, :] = msg
        msg_ref[copy, :, slots // shards :, :] = table


def messages(ids, acts, parts, shards):
    tall, lanes = acts.shape
    slots = 2 * (tall - 16)
    return pl.pallas_call(
        message_kernel,
        out_shape=jax.ShapeDtypeStruct((parts, shards, slots // shards + 16, lanes), BF),
        compiler_params=params(),
        cost_estimate=cost(8 * slots * ids.shape[1] * lanes, 2**21),
        name="make_messages",
    )(ids, acts)


def doubled(pair):
    source, target = iota((128, 256), 0), iota((128, 256), 1)
    copy = source == (target // 128) * LAT + target % LAT
    return dot(pair, jnp.where(copy, 1.0, 0.0).astype(BF)).astype(BF)


def lane_block(group):
    return (iota((1, 128), 1) // LAT + group * 2).astype(F32).astype(BF)


def own_expanded(own):
    count = own.shape[0]
    twice = jnp.concatenate([own, own], axis=1)
    mine = (iota((count, 256), 0) // CAP) % 4 == iota((count, 256), 1) // LAT
    return jnp.where(mine, twice.astype(F32), 0.0).astype(BF)


def spread(packed):
    low = iota((1, 1, 128), 2) < LAT
    zero = jnp.zeros((packed.shape[0], CAP, 128), F32)
    rows = []
    for p in range(2):
        piece = packed[:, p * CAP : (p + 1) * CAP, :]
        for q in range(2):
            kept = jnp.where(low if q == 0 else ~low, piece, 0.0)
            rows.append(jnp.concatenate([kept, zero] if p == 0 else [zero, kept], axis=2))
    return jnp.concatenate(rows, axis=1).reshape(packed.shape[0] * 32, 256)


def gathered(wide):
    wide = wide.reshape(wide.shape[0] // 32, 4, CAP, 256)
    low = iota((1, 1, 128), 2) < LAT
    packed = []
    for p in range(2):
        lanes = slice(p * 128, (p + 1) * 128)
        packed.append(jnp.where(low, wide[:, 2 * p, :, lanes], wide[:, 2 * p + 1, :, lanes]))
    return jnp.concatenate(packed, axis=1)


def home_kernel(scale, parts, *refs):
    group, (place_ref, dec_hbm, bias_ref), refs = refs[:parts], refs[parts : parts + 3], refs[parts + 3 :]
    recon, gates, (pick_ref, part_ref, dec_ref, sems) = refs[:parts], refs[parts : 2 * parts], refs[2 * parts :]
    slots, rows = pick_ref.shape[1:]
    packed = slots // 2
    pieces = sems.shape[0]
    tall = dec_ref.shape[0] // pieces
    per = tall // 256

    def fetch(piece):
        at = pl.ds(pl.multiple_of(piece * tall, tall), tall)
        return pltpu.make_async_copy(dec_hbm.at[at], dec_ref.at[at], sems.at[piece])

    for piece in range(pieces):
        fetch(piece).start()

    slot = iota((slots, rows), 0)
    for d in range(parts):
        ids, rank = read_info(group[d][packed:, :])
        place = ids * CAP + rank
        here = (slot == place[0:1, :]) | (slot == place[1:2, :])
        pick_ref[d] = jnp.where(here, 1.0, 0.0).astype(BF)

    def aligned(start, size):
        return pl.ds(pl.multiple_of(start * size, size), size)

    @pl.loop(0, pieces)
    def _(piece):
        fetch(piece).wait()
        for g in range(per):
            shard = piece * per + g
            acts = jnp.stack([group[d][aligned(shard, 16), :].astype(F32) for d in range(parts)])
            part = dot(spread(acts).astype(BF), dec_ref[aligned(shard, 256), :]).astype(BF)
            for d in range(parts):
                part_ref[d, aligned(shard, 32), :] = part[d * 32 : (d + 1) * 32]

    bias = bias_ref[pl.ds(place_ref[0], 1), :]
    for d in range(parts):
        total = dot_tn(pick_ref[d], part_ref[d])
        recon[d][...] = (total + bias).astype(BF)
        part_ref[d] = dot(pick_ref[d], total.astype(BF)).astype(BF)

    @pl.loop(0, pieces)
    def _(piece):
        for g in range(per):
            shard = piece * per + g
            total = jnp.concatenate([part_ref[d, aligned(shard, 32), :] for d in range(parts)], axis=0)
            wide = dot_nt(total, dec_ref[aligned(shard, 256), :])
            gate = (gathered(wide) * scale).astype(BF)
            for d in range(parts):
                gates[d][aligned(shard, 16), :] = gate[d]


def home(scale, place, group, dec_all, bias):
    latents, cols = dec_all.shape
    tall, lanes = group[0].shape
    parts = len(group)
    packed = tall - 16
    rows = 256
    vmem = pl.BlockSpec(memory_space=pltpu.VMEM)
    return pl.pallas_call(
        functools.partial(home_kernel, scale, parts),
        in_specs=[vmem] * parts
        + [pl.BlockSpec(memory_space=pltpu.SMEM), pl.BlockSpec(memory_space=pl.ANY), vmem],
        out_specs=[vmem] * (2 * parts),
        out_shape=[jax.ShapeDtypeStruct((rows, cols), BF)] * parts
        + [jax.ShapeDtypeStruct((packed, lanes), BF)] * parts,
        scratch_shapes=[
            pltpu.VMEM((parts, 2 * packed, rows), BF),
            pltpu.VMEM((parts, 2 * packed, cols), BF),
            pltpu.VMEM((latents, cols), BF),
            pltpu.SemaphoreType.DMA((4,)),
        ],
        compiler_params=params(),
        cost_estimate=cost(8 * latents * cols * 128, 20 * 2**20),
        name="home_rows",
    )(*group, place, dec_all, bias)


def assemble_kernel(at_ref, *refs):
    pieces, out, sems = refs[:-2], refs[-2], refs[-1]
    cols = pieces[0].shape[1]
    copies = []
    for d, piece in enumerate(pieces):
        place = pl.multiple_of(((at_ref[0] + d) % len(pieces)) * cols, cols)
        copies.append(pltpu.make_async_copy(piece, out.at[:, pl.ds(place, cols)], sems.at[d]))
    for copy in copies:
        copy.start()
    for copy in copies:
        copy.wait()


def assemble(at, pieces):
    rows, cols = pieces[0].shape
    return pl.pallas_call(
        assemble_kernel,
        in_specs=[pl.BlockSpec(memory_space=pltpu.SMEM)]
        + [pl.BlockSpec(memory_space=pltpu.VMEM)] * len(pieces),
        out_specs=pl.BlockSpec(memory_space=pl.ANY),
        out_shape=jax.ShapeDtypeStruct((rows, cols * len(pieces)), BF),
        scratch_shapes=[pltpu.SemaphoreType.DMA((len(pieces),))],
        compiler_params=params(),
        cost_estimate=cost(0, 2**22),
        name="assemble_recon",
    )(at.astype(jnp.int32).reshape(1), *pieces)


def sum_kernel(*refs):
    out_ref = refs[-1]
    total = refs[0][...].astype(F32)
    for ref in refs[1:-1]:
        total = total + ref[...].astype(F32)
    for copy in range(out_ref.shape[0]):
        out_ref[copy] = total.astype(BF)


def summed(pieces, copies):
    return pl.pallas_call(
        sum_kernel,
        out_shape=jax.ShapeDtypeStruct((copies, *pieces[0].shape), BF),
        compiler_params=params(),
        cost_estimate=cost(0, 2**20),
        name="sum_pieces",
    )(*pieces)


def mix_kernel(msg_ref, dec_hbm, start_ref, out_ref, own_ref, other_ref, name_ref, dec_ref, sems):
    sources = msg_ref.shape[0]
    count = sources * 32
    steps = sems.shape[0]
    quarter = dec_ref.shape[0] // 4
    tall = quarter // steps

    def fetch(step, q):
        at = pl.ds(q * quarter + step * tall, tall)
        return pltpu.make_async_copy(dec_hbm.at[at], dec_ref.at[at], sems.at[step, q])

    for step in range(steps):
        for q in range(4):
            fetch(step, q).start()

    twice = doubled(msg_ref[:, :32, :].reshape(count, 128)).astype(F32).reshape(sources, 4, CAP, 256)
    block = slot_names(msg_ref[:, 32:, :]).astype(F32).reshape(sources, 4, CAP, 128)
    for b in range(4):
        rows = twice[:, b].reshape(sources * CAP, 256)
        other_ref[b] = rows[:, 128:].astype(BF)
        name = block[:, b].reshape(sources * CAP, 128)
        within = jnp.floor(name * (1.0 / 32.0))
        name_ref[b] = (name - 32.0 * within).astype(BF)
        wide = jnp.concatenate([rows[:, :128]] * 2, axis=1)
        lane = (iota((1, 256), 1) // LAT).astype(F32)
        own_ref[b] = jnp.where(jnp.concatenate([within] * 2, axis=1) == lane, wide, 0.0).astype(BF).T
        own = rows[:, :128].astype(BF)
        here = slice(b * LAT, (b + 1) * LAT)
        out_ref[here, :] = dot(dot_tn(own, own)[:LAT, :LAT].astype(BF), start_ref[here, :])

    zero = jnp.zeros((sources * CAP, 128), BF)
    for step in range(steps):
        mixed = []
        for b in range(4):
            wide = []
            for pair in range(tall // 128):
                name = iota((1, 128), 1) // LAT + 2 * pair + step * (tall // LAT)
                wide.append(jnp.where(name_ref[b] == name.astype(F32).astype(BF), other_ref[b], zero))
            mixed.append(dot(own_ref[b], jnp.concatenate(wide, axis=1)).astype(BF))
        total = out_ref[...]
        for q in range(4):
            fetch(step, q).wait()
            left = jnp.concatenate([mixed[b][q * LAT : (q + 1) * LAT] for b in range(4)], axis=0)
            start = q * quarter + step * tall
            total = total + dot(left, dec_ref[start : start + tall, :])
        out_ref[...] = total


def mix(msg, dec_all, own_dec):
    latents, cols = dec_all.shape
    per = msg.shape[0] * CAP
    vmem = pl.BlockSpec(memory_space=pltpu.VMEM)
    return pl.pallas_call(
        mix_kernel,
        in_specs=[vmem, pl.BlockSpec(memory_space=pl.ANY), vmem],
        out_specs=vmem,
        out_shape=jax.ShapeDtypeStruct(own_dec.shape, F32),
        scratch_shapes=[
            pltpu.VMEM((4, 4 * LAT, per), BF),
            pltpu.VMEM((4, per, 128), BF),
            pltpu.VMEM((4, per, 128), BF),
            pltpu.VMEM(dec_all.shape, BF),
            pltpu.SemaphoreType.DMA((1, 4)),
        ],
        compiler_params=params(),
        cost_estimate=cost(1, 1),
        name="mix_decoder",
    )(msg, dec_all, own_dec)


def grads_kernel(
    scale, gate_hbm, proj_hbm, msg_hbm, rows_hbm, mixed_hbm, enc_ref, dec_ref,
    gate_ref, proj_ref, msg_ref, rows_ref, mixed_ref, acc_ref, sems, last
):
    parts = proj_hbm.shape[0]
    sources = msg_ref.shape[0] // parts
    count = sources * 32
    cols = rows_ref.shape[1]

    def fetch(part):
        at = pl.ds(part * sources, sources)
        tall = pl.ds(part * count, count)
        return [
            pltpu.make_async_copy(msg_hbm.at[at], msg_ref.at[at], sems.at[part, 0]),
            pltpu.make_async_copy(gate_hbm.at[at], gate_ref.at[at], sems.at[part, 1]),
            pltpu.make_async_copy(proj_hbm.at[:, at], proj_ref.at[:, at], sems.at[part, 2]),
            pltpu.make_async_copy(rows_hbm.at[tall], rows_ref.at[tall], sems.at[part, 3]),
        ]

    mixed_copy = pltpu.make_async_copy(mixed_hbm, mixed_ref, last)
    for part in range(parts):
        for copy in fetch(part):
            copy.start()
    mixed_copy.start()
    for part in range(parts):
        for copy in fetch(part):
            copy.wait()
        here = slice(part * sources, (part + 1) * sources)
        own = own_expanded(doubled(msg_ref[here, :32, :].reshape(count, 128))[:, :128])
        total = gate_ref[here].astype(F32)
        for other in range(parts):
            total = total - proj_ref[other, here].astype(F32)
        wide = jnp.where(own.astype(F32) > 0, spread(total), 0.0).astype(BF)
        both = jnp.concatenate([wide, own], axis=1)
        more = dot_tn(both, rows_ref[part * count : (part + 1) * count, :])
        if part == 0:
            acc_ref[...] = more
        elif part < parts - 1:
            acc_ref[...] += more
        else:
            more = acc_ref[...] + more
            enc_ref[...] = more[:256, :]
            mixed_copy.wait()
            dec_ref[...] = (mixed_ref[...] - more[256:, :]) * scale


def grads(scale, gate, proj, msg, rows, mixed):
    cols = rows.shape[1]
    shape = jax.ShapeDtypeStruct(mixed.shape, F32)
    vmem = pl.BlockSpec(memory_space=pltpu.VMEM)
    arrays = (gate, proj, msg, rows, mixed)
    return pl.pallas_call(
        functools.partial(grads_kernel, scale),
        in_specs=[pl.BlockSpec(memory_space=pl.ANY)] * len(arrays),
        out_specs=[vmem, vmem],
        out_shape=[shape, shape],
        scratch_shapes=[pltpu.VMEM(array.shape, array.dtype) for array in arrays]
        + [
            pltpu.VMEM((512, cols), F32),
            pltpu.SemaphoreType.DMA((proj.shape[0], 4)),
            pltpu.SemaphoreType.DMA,
        ],
        compiler_params=params(),
        cost_estimate=cost(4 * msg.shape[0] * 32 * cols * 256, 16 * 2**20),
        name="dictionary_grads",
    )(*arrays)


def shifted(value, by, parts):
    if by == 0:
        return value
    return lax.ppermute(value, "dp", [(i, (i + by) % parts) for i in range(parts)])


def body(resid, block_ids, enc_w, enc_b, dec_w, dec_b):
    tok_rows, width = resid.shape
    parts = lax.axis_size("dp")
    shards = lax.axis_size("dict")
    local = enc_w.shape[0]
    here = local // LAT
    slots = here * shards * CAP
    cols = width // parts
    everyone = ("dp", "dict")
    devices = parts * shards
    blocks = here * shards
    scale = (blocks / (tok_rows * devices * block_ids.shape[1])) ** 0.5
    at_x = lax.axis_index("dp")

    ids = block_ids.T
    outgoing = route(ids, resid, dec_b, parts, slots)
    arrived = lax.all_to_all(
        outgoing.reshape(devices, here * CAP, cols), everyone, 0, 0, tiled=True
    )

    enc_x = lax.dynamic_slice(enc_w, (0, at_x * cols), (local, cols))
    dec_x = lax.dynamic_slice(dec_w, (0, at_x * cols), (local, cols))
    dec_all = lax.all_gather(dec_x, "dict", axis=0, tiled=True)

    weights = jnp.concatenate(
        [enc_x.reshape(2, 2 * LAT, cols), dec_x.reshape(2, 2 * LAT, cols)], axis=1
    ).transpose(0, 2, 1)
    bias = jnp.where(at_x == 0, enc_b, 0.0).reshape(2, 2 * LAT)
    pre, proj = encode(scale, arrived, weights, bias)
    partial = lax.all_to_all(pre, everyone, 0, 0, tiled=True)
    projs = lax.all_gather(proj, "dp", axis=0, tiled=False)
    acts = activate(pair_info(ids, here * shards), partial.reshape(parts, shards * 2 * CAP, 128))
    msg = messages(ids, acts, parts, shards)
    group = [shifted(acts, d, parts) for d in range(parts)]
    msg, *group = lax.optimization_barrier((msg, *group))
    message = lax.all_to_all(
        msg.reshape(devices, here * CAP + 16, 128), everyone, 0, 0, tiled=True
    )

    place = at_x.astype(jnp.int32).reshape(1)
    made = home(scale, place, group, dec_all, dec_b.reshape(parts, cols))
    total = summed([shifted(made[parts + d], -d, parts) for d in range(parts)], parts)
    gates = lax.all_to_all(total.reshape(devices, 2 * CAP, 128), everyone, 0, 0, tiled=True)
    total, *made = lax.optimization_barrier((total, *made[:parts]))
    pieces = [shifted(made[d], -d, parts) for d in range(parts)]
    mixed = mix(message, dec_all, dec_x)
    enc_grad, dec_grad = grads(
        scale, gates, projs, message, arrived.reshape(devices * here * CAP, cols), mixed
    )
    recon = assemble(at_x, pieces)
    return (recon, enc_grad, dec_grad)


def solution(mesh):
    placed = (
        P(("dp", "dict"), None),
        P(("dp", "dict"), None),
        P("dict", None),
        P("dict"),
        P("dict", None),
        P(),
    )
    return jax.shard_map(
        body,
        mesh=mesh,
        in_specs=placed,
        out_specs=(P(("dp", "dict"), None), P("dict", "dp"), P("dict", "dp")),
        check_vma=False,
    )
```
